256 devices in a mesh: dp: 8 (over z_lo, core), slab: 32 (over z_hi, x, y).
Axes of the slice: x: 4, y: 4, z: 8 (z_hi: 2, z_lo: 4; z = z_hi * 4 + z_lo), core: 2. Of those that a mesh axis runs over, the one named last changes fastest.
Arguments:
- inputs: float32 [8, 16, 128, 128, 128], P('dp', None, 'slab'), may hold values from -6 to 6
- cotangent: float32 [8, 16, 128, 128, 128], P('dp', None, 'slab'), may hold values from -6 to 6
- spectral_weights: float32 [16, 16, 2, 12288], P(None, None, None, 'slab'), may hold values from -6 to 6
- pointwise_weights: float32 [16, 16], replicated, may hold values from -1.5 to 1.5
Outputs:
- grad_inputs: float32 [8, 16, 128, 128, 128], P('dp', None, 'slab')
- grad_spectral: float32 [16, 16, 2, 12288], P('dp', None, None, 'slab')
- grad_pointwise: float32 [16, 16], replicated
The draws below stay inside these ranges and needn't reach their ends.
All inputs are finite; a program needn't handle non-finite values.
Results may differ from the reference program's by a relative error of at most 0.00011.
Values sent between devices are 32-bit elements; how exact they have to be, the bound alone decides.
A program may use at most 128 MiB of HBM per device.

```python
import math
import jax
import jax.numpy as jnp
from jax import lax

CH = 16
NY = 128
NZ = 128
KX = 32
KY = 32
KZ = 12
NX = 128
MODES = 12288
SAMPLES = 8


def shard_levels(rng, shape, cuts, smallest, top_value):
    level, own = 1.0, jax.random.fold_in(rng, 6)
    for axis_at, shards_of in cuts:
        draws = jnp.exp(jax.random.uniform(jax.random.fold_in(own, axis_at), (shards_of,), jnp.float32, smallest / len(cuts), top_value / len(cuts)))
        level = level * jnp.repeat(draws, shape[axis_at] // shards_of).reshape([-1 if axis == axis_at else 1 for axis in range(len(shape))])
    return level


def centred(key, shape, deviation, reach, pieces=(), held_as=jnp.bfloat16):
    loudness = shard_levels(key, shape, pieces, -0.22, 0.18) if pieces else 1.0
    drawn = jax.random.normal(key, shape, jnp.float32) * deviation * loudness
    return jnp.minimum(jnp.maximum(drawn, -reach), reach).astype(held_as)


def setup_inputs(seed: int = 0) -> dict:
    arg_keys = jax.random.split(jax.random.key(seed), 5)
    inputs = centred(arg_keys[0], (SAMPLES, CH, NX, NY, NZ), 1.0, 6.0, ((0, 8), (2, 32)), jnp.float32)
    cotangent = centred(arg_keys[1], (SAMPLES, CH, NX, NY, NZ), 1.0, 6.0, ((0, 8), (2, 32)), jnp.float32)
    spectral_weights = centred(arg_keys[2], (CH, CH, 2, MODES), 1.0, 6.0, ((3, 32),), jnp.float32)
    pointwise_weights = centred(arg_keys[3], (CH, CH), CH ** -0.5, 1.5, (), jnp.float32)
    return dict(inputs=inputs, cotangent=cotangent, spectral_weights=spectral_weights, pointwise_weights=pointwise_weights)


def contract(pattern, left_operand, right_operand):
    return jnp.einsum(pattern, left_operand, right_operand, precision=lax.Precision.HIGHEST)

def twiddle(length, number, centered):
    places = lax.iota(jnp.int32, length)[:, None]
    orders = lax.iota(jnp.int32, number)[None, :]
    if centered:
        orders = jnp.where(orders < number // 2, orders, orders - number)
    angles = jnp.mod(places * orders, length).astype(jnp.float32) * (2.0 * math.pi / length)
    return (jnp.cos(angles), jnp.sin(angles))

def depth_weights():
    orders = lax.iota(jnp.int32, KZ)
    return jnp.where(orders == 0, 1.0, 2.0).astype(jnp.float32)

def spectrum(values):
    third_cosine, third_sine = twiddle(NZ, KZ, False)
    second_cosine, second_sine = twiddle(NY, KY, True)
    first_cosine, first_sine = twiddle(NX, KX, True)
    partial_real = contract('cxyz,zk->cxyk', values, third_cosine)
    partial_imag = -contract('cxyz,zk->cxyk', values, third_sine)
    middle_real = contract('cxyk,yj->cxjk', partial_real, second_cosine) + contract('cxyk,yj->cxjk', partial_imag, second_sine)
    middle_imag = contract('cxyk,yj->cxjk', partial_imag, second_cosine) - contract('cxyk,yj->cxjk', partial_real, second_sine)
    final_real = contract('cxjk,xi->cjki', middle_real, first_cosine) + contract('cxjk,xi->cjki', middle_imag, first_sine)
    final_imag = contract('cxjk,xi->cjki', middle_imag, first_cosine) - contract('cxjk,xi->cjki', middle_real, first_sine)
    norm_scale = 1.0 / math.sqrt(NX * NY * NZ)
    return (final_real.reshape(CH, MODES) * norm_scale, final_imag.reshape(CH, MODES) * norm_scale)

def synthesis(real_part, imag_part, weights):
    third_cosine, third_sine = twiddle(NZ, KZ, False)
    second_cosine, second_sine = twiddle(NY, KY, True)
    first_cosine, first_sine = twiddle(NX, KX, True)
    spectra_real = real_part.reshape(CH, KY, KZ, KX)
    spectra_imag = imag_part.reshape(CH, KY, KZ, KX)
    upper_real = contract('cjki,xi->cjkx', spectra_real, first_cosine) - contract('cjki,xi->cjkx', spectra_imag, first_sine)
    upper_imag = contract('cjki,xi->cjkx', spectra_real, first_sine) + contract('cjki,xi->cjkx', spectra_imag, first_cosine)
    lower_real = contract('cjkx,yj->cxyk', upper_real, second_cosine) - contract('cjkx,yj->cxyk', upper_imag, second_sine)
    lower_imag = contract('cjkx,yj->cxyk', upper_real, second_sine) + contract('cjkx,yj->cxyk', upper_imag, second_cosine)
    result = contract('cxyk,zk->cxyz', lower_real, third_cosine * weights[None, :]) - contract('cxyk,zk->cxyz', lower_imag, third_sine * weights[None, :])
    return result * (1.0 / math.sqrt(NX * NY * NZ))

def layer(values, spectral_weights, pointwise_weights):
    value_real, value_imag = spectrum(values)
    weight_real = spectral_weights[:, :, 0]
    weight_imag = spectral_weights[:, :, 1]
    mixed_real = contract('com,cm->om', weight_real, value_real) - contract('com,cm->om', weight_imag, value_imag)
    mixed_imag = contract('com,cm->om', weight_real, value_imag) + contract('com,cm->om', weight_imag, value_real)
    carried = synthesis(mixed_real, mixed_imag, depth_weights())
    before = contract('co,cxyz->oxyz', pointwise_weights, values) + carried
    return jax.nn.gelu(before, approximate=False)

def reference(inputs, cotangent, spectral_weights, pointwise_weights):

    def per_sample(totals, sample_pair):
        values, upstream = sample_pair
        outputs, pullback = jax.vjp(layer, values, spectral_weights, pointwise_weights)
        grad_values, grad_modes, grad_mixing = pullback(upstream)
        return ((totals[0] + grad_modes, totals[1] + grad_mixing), grad_values)
    initial = (jnp.zeros_like(spectral_weights), jnp.zeros_like(pointwise_weights))
    (spectral_total, pointwise_total), grad_inputs = lax.scan(per_sample, initial, (inputs, cotangent))
    pointwise_total = pointwise_total / math.sqrt(SAMPLES * NX * NY * NZ)
    return (grad_inputs, spectral_total, pointwise_total)
```

```python
import functools
import math

import jax
import jax.numpy as jnp
import ml_dtypes
import numpy as np
from jax import lax
from jax.experimental import pallas as pl
from jax.experimental.pallas import tpu as pltpu
from jax.sharding import PartitionSpec as P

CH = 16
XP = 4
NX = 128
NY = 128
NZ = 128
KX = 32
KY = 32
KZ = 12
SLAB = 32
DP = 8
ROWS = 16
F32 = jnp.float32
BF16 = jnp.bfloat16
MESH = pl.DeviceIdType.MESH
NORM = 1.0 / math.sqrt(NX * NY * NZ)


def halves(table):
    table = np.asarray(table, np.float64)
    high = table.astype(ml_dtypes.bfloat16)
    low = (table - high.astype(np.float64)).astype(ml_dtypes.bfloat16)
    return high, low


def angles(length, orders):
    places = np.arange(length)[:, None]
    return ((places * orders[None, :]) % length) * (2.0 * math.pi / length)


@functools.cache
def tables():
    centred = np.arange(KY)
    centred = np.where(centred < KY // 2, centred, centred - KY)
    second = angles(NY, centred)
    third = angles(NZ, np.arange(KZ))
    first = angles(NX, centred)
    ty = np.concatenate([np.cos(second).T, -np.sin(second).T], axis=0)
    ty_high, ty_low = halves(ty)
    ty_stack = np.concatenate(
        [np.concatenate([ty_high, ty_high], axis=1), np.concatenate([ty_low, np.zeros_like(ty_low)], axis=1)], axis=0
    )
    ty_inverse = np.concatenate([ty_high.T, ty_high.T, ty_low.T], axis=1)
    depth = {}
    for name, weights in (("plain", np.ones(KZ)), ("weighted", np.where(np.arange(KZ) == 0, 1.0, 2.0))):
        cosine = (np.cos(third) * weights[None, :]).T
        sine = (np.sin(third) * weights[None, :]).T
        real_row = np.concatenate([cosine, sine], axis=1)
        imag_row = np.concatenate([-sine, cosine], axis=1)
        analysis = np.zeros((2 * ROWS, 2 * NZ))
        analysis[:KZ] = real_row
        analysis[ROWS : ROWS + KZ] = imag_row
        synthesis = np.zeros((2, 15 * ROWS, 2 * NZ))
        synthesis[0, 7 * ROWS : 7 * ROWS + KZ] = real_row
        synthesis[1, 7 * ROWS : 7 * ROWS + KZ] = imag_row
        depth[name] = (np.concatenate(halves(analysis), axis=0),) + halves(synthesis)
    place = first.reshape(SLAB, XP, KX)
    cosine = np.cos(place).transpose(1, 0, 2) * NORM
    sine = np.sin(place).transpose(1, 0, 2) * NORM
    rows = np.zeros((2, XP, 4, SLAB, 2, 4, KX))
    for group in range(4):
        rows[0, :, group, :, 0, group] = cosine
        rows[1, :, group, :, 0, group] = sine
        rows[0, :, group, :, 1, group] = -sine
        rows[1, :, group, :, 1, group] = cosine
    rows_high, rows_low = halves(rows.reshape(2 * XP * 4 * SLAB, 2 * 4 * KX))
    return (ty_stack, ty_inverse) + depth["plain"] + depth["weighted"] + (rows_high, rows_low)


def split(value):
    high = value.astype(BF16)
    low = (value - high.astype(F32)).astype(BF16)
    return high, low


def dot(left, right):
    return jnp.dot(left, right, preferred_element_type=F32)


def dot_t(left, right):
    return lax.dot_general(left, right, (((1,), (1,)), ((), ())), preferred_element_type=F32)


def cat(pieces, axis):
    return jnp.concatenate(pieces, axis=axis)


def analyse_y(pair, ty_stack, store, group):
    high, low = split(pair)
    out = dot(ty_stack[...], cat([high, low], 0))
    out = out[:64] + out[64:]
    store[pl.ds(pl.multiple_of(group * 64, 64), 64), :] = out[:, :NZ]
    store[pl.ds(pl.multiple_of(group * 64 + 64, 64), 64), :] = out[:, NZ:]


def analyse_z(store, tz_stack, sbuf):
    lanes = lax.broadcasted_iota(jnp.int32, (ROWS, 128), 1) < 64

    def step(group, carry):
        pieces = []
        for each in range(4):
            j = group * 4 + each
            pieces.append(cat([store[pl.ds(j, 64, stride=64), :], store[pl.ds(KY + j, 64, stride=64), :]], 1))
        high, low = split(cat(pieces, 0))
        out = dot_t(tz_stack[...], high)
        out = out[:32] + out[32:] + dot_t(tz_stack[:32, :], low)
        for each in range(2):
            tile = out[:, 128 * each : 128 * each + 128]
            real, imag = tile[:ROWS], tile[ROWS:]
            first = jnp.where(lanes, real, pltpu.roll(imag, 64, axis=1))
            second = jnp.where(lanes, pltpu.roll(real, 64, axis=1), imag)
            base = pl.multiple_of((group * 4 + 2 * each) * ROWS, ROWS)
            sbuf[pl.ds(base, ROWS), :] = first
            sbuf[pl.ds(base + ROWS, ROWS), :] = second
        return carry

    lax.fori_loop(0, KY // 4, step, 0)


def analyse_x(rbuf, rows_high, rows_low):
    parts = []
    for t in range(3):
        block = cat([rbuf[pl.ds(4 * t + k, SLAB, stride=ROWS), :] for k in range(4)], 0).T
        parts.append(cat([block[16 * q : 16 * q + 16] for q in range(8)], 1))
    high, low = split(cat(parts, 0))
    out = dot(cat([high, low], 0), rows_high[...])
    return out[:48] + out[48:] + dot(high, rows_low[...])


def synthesise_x(modes, rows_high, rows_low, sbuf):
    high, low = split(modes)
    out = dot_t(cat([high, low], 0), rows_high[...])
    out = out[:48] + out[48:] + dot_t(high, rows_low[...])
    for t in range(3):
        part = out[16 * t : 16 * t + 16]
        block = cat([part[:, 128 * q : 128 * q + 128] for q in range(8)], 0).T
        for k in range(4):
            sbuf[pl.ds(4 * t + k, SLAB, stride=ROWS), :] = block[SLAB * k : SLAB * k + SLAB]


def synthesise_z(rbuf, zi_high, zi_low, held, store):
    for g in range(4):
        block = rbuf[pl.ds(128 * g, 128), :].T
        high, low = split(cat([block[:64], block[64:]], 1))
        held[pl.ds(64 * g, 64), :] = high
        held[pl.ds(256 + 64 * g, 64), :] = low

    def step(jj, carry):
        at = pl.multiple_of(7 * ROWS - ROWS * jj, ROWS)
        table_high = cat([zi_high[0, pl.ds(at, 128), :], zi_high[1, pl.ds(at, 128), :]], 0)
        table_low = cat([zi_low[0, pl.ds(at, 128), :], zi_low[1, pl.ds(at, 128), :]], 0)
        out = dot(held[...], table_high)
        out = out[:256] + out[256:] + dot(held[:256, :], table_low)
        for g in range(4):
            store[pl.ds(8 * g + jj, 64, stride=64), :] = out[64 * g : 64 * g + 64, :NZ]
            store[pl.ds(KY + 8 * g + jj, 64, stride=64), :] = out[64 * g : 64 * g + 64, NZ:]
        return carry

    lax.fori_loop(0, 8, step, 0)


def synthesise_y(store, ty_inverse, group):
    pair = cat(
        [
            store[pl.ds(pl.multiple_of(group * 64, 64), 64), :],
            store[pl.ds(pl.multiple_of(group * 64 + 64, 64), 64), :],
        ],
        1,
    )
    high, low = split(pair)
    return dot(ty_inverse[...], cat([high, low, high], 0))


def rows_of(source, x, y0):
    left = cat([source[c, x, pl.ds(y0, 8), :] for c in range(CH)], 0)
    right = cat([source[c, x, pl.ds(y0 + 8, 8), :] for c in range(CH)], 0)
    return cat([left, right], 1)


def mix_channels(kron, halves_stack, target, x, y0):
    out = dot(kron[...], halves_stack)
    out = out[:128] + out[128:]
    for c in range(CH):
        target[c, x, pl.ds(y0, 8), :] = out[8 * c : 8 * c + 8, :NZ]
        target[c, x, pl.ds(y0 + 8, 8), :] = out[8 * c : 8 * c + 8, NZ:]


def kernel(
    x_hbm, cot_hbm, w_hbm, pw_ref, ty_stack, ty_inverse, tz_plain, zp_high, zp_low, tz_weighted, zw_high, zw_low,
    rows_high, rows_low,
    gi_hbm, gs_ref, gp_ref,
    xv, cv, bv, wv, store, store2, held, sbuf, rbuf, vv, gv, kron1, kron2, pacc,
    vsend, vrecv, gsend, grecv, psend, precv,
    xsem, csem, wsem, osem, ssem, rsem, vssem, vrsem, gssem, grsem, pssem, prsem,
):
    me = lax.axis_index("slab")
    mine = lax.axis_index("dp")

    barrier = pltpu.get_barrier_semaphore()

    def greet_slab(d, carry):
        pl.semaphore_signal(barrier, inc=1, device_id={"slab": lax.rem(me + d, SLAB)}, device_id_type=MESH)
        return carry

    def greet_dp(d, carry):
        pl.semaphore_signal(barrier, inc=1, device_id={"dp": lax.rem(mine + d, DP)}, device_id_type=MESH)
        return carry

    def x_copy(c):
        return pltpu.make_async_copy(x_hbm.at[pl.ds(2 * c, 2)], xv.at[pl.ds(2 * c, 2)], xsem.at[c])

    for c in range(CH // 2):
        x_copy(c).start()
    w_copy = pltpu.make_async_copy(w_hbm, wv, wsem)
    w_copy.start()
    c_copy = pltpu.make_async_copy(cot_hbm, cv, csem)
    c_copy.start()
    lax.fori_loop(1, SLAB, greet_slab, 0)
    lax.fori_loop(1, DP, greet_dp, 0)

    def slab_copy(phase, p, slot):
        return pltpu.make_async_remote_copy(
            src_ref=sbuf.at[phase, pl.ds(pl.multiple_of(ROWS * p, ROWS), ROWS)],
            dst_ref=rbuf.at[phase, pl.ds(pl.multiple_of(ROWS * slot, ROWS), ROWS)],
            send_sem=ssem.at[phase, p],
            recv_sem=rsem.at[phase, slot],
            device_id={"slab": p},
            device_id_type=MESH,
        )

    def send_all(phase):
        def step(d, carry):
            slab_copy(phase, lax.rem(me + d, SLAB), me).start()
            return carry

        lax.fori_loop(1, SLAB, step, 0)
        own = pl.ds(pl.multiple_of(ROWS * me, ROWS), ROWS)
        rbuf[phase, own, :] = sbuf[phase, own, :]

    def receive_all(phase):
        def step(d, carry):
            peer = lax.rem(me + d, SLAB)
            slab_copy(phase, peer, peer).wait_recv()
            return carry

        lax.fori_loop(1, SLAB, step, 0)

    def sent_all(phase):
        def step(d, carry):
            slab_copy(phase, lax.rem(me + d, SLAB), me).wait_send()
            return carry

        lax.fori_loop(1, SLAB, step, 0)

    spread = (
        lax.broadcasted_iota(jnp.int32, (128, CH), 0) // 8 == lax.broadcasted_iota(jnp.int32, (128, CH), 1)
    ).astype(F32)
    same_row = (
        lax.broadcasted_iota(jnp.int32, (128, 128), 0) % 8 == lax.broadcasted_iota(jnp.int32, (128, 128), 1) % 8
    )
    wide = jnp.dot(spread, pw_ref[...], precision=lax.Precision.HIGHEST, preferred_element_type=F32)
    wide = lax.dot_general(
        wide, spread, (((1,), (1,)), ((), ())), precision=lax.Precision.HIGHEST, preferred_element_type=F32
    )
    wide = jnp.where(same_row, wide, 0.0)
    for kron, value in ((kron1, wide.T), (kron2, wide)):
        high, low = split(value)
        kron[...] = cat([cat([high, high], 1), cat([low, jnp.zeros_like(low)], 1)], 0)
    for phase in (1, 3):
        for k in range(KZ, ROWS):
            sbuf[phase, pl.ds(k, SLAB, stride=ROWS), :] = jnp.zeros((SLAB, 128), F32)

    def forward_step(c, carry):
        x_copy(c).wait()
        for x in range(XP):
            analyse_y(cat([xv[2 * c, x], xv[2 * c + 1, x]], 1), ty_stack, store, x * CH + 2 * c)
        return carry

    lax.fori_loop(0, CH // 2, forward_step, 0)
    analyse_z(store, tz_plain, sbuf.at[0])
    pl.semaphore_wait(barrier, SLAB - 1 + DP - 1)
    send_all(0)

    def mix_step(yg, carry):
        y0 = pl.multiple_of(yg * 16, 16)
        for x in range(XP):
            high, low = split(rows_of(xv, x, y0))
            mix_channels(kron1, cat([high, low], 0), bv, x, y0)
        return carry

    lax.fori_loop(0, NY // 16, mix_step, 0)
    w_copy.wait()
    receive_all(0)
    modes = analyse_x(rbuf.at[0], rows_high, rows_low)
    vv[:48, :] = modes[:, :128]
    vv[48:, :] = modes[:, 128:]

    def mode_step(c, carry):
        out = []
        for t in range(3):
            wr = wv[c, :, 0, 128 * t : 128 * t + 128]
            wi = wv[c, :, 1, 128 * t : 128 * t + 128]
            vr = vv[pl.ds(16 * t + c, 1), :]
            vi = vv[pl.ds(48 + 16 * t + c, 1), :]
            out.append(carry[2 * t] + (wr * vr - wi * vi))
            out.append(carry[2 * t + 1] + (wr * vi + wi * vr))
        return tuple(out)

    mixed = lax.fori_loop(0, CH, mode_step, tuple(jnp.zeros((CH, 128), F32) for _ in range(6)))
    mixed = cat([cat([mixed[2 * t], mixed[2 * t + 1]], 1) for t in range(3)], 0)
    synthesise_x(mixed, rows_high, rows_low, sbuf.at[1])
    send_all(1)

    def v_copy(d, slot):
        return pltpu.make_async_remote_copy(
            src_ref=vsend.at[pl.ds(pl.multiple_of(16 * d, 16), 16)],
            dst_ref=vrecv.at[pl.ds(pl.multiple_of(16 * slot, 16), 16)],
            send_sem=vssem.at[d],
            recv_sem=vrsem.at[slot],
            device_id={"dp": d},
            device_id_type=MESH,
        )

    vsend[...] = jnp.zeros_like(vsend)
    for d in range(DP):
        for c in range(2):
            for t in range(3):
                row = 16 * t + 2 * d + c
                at = 16 * d + 6 * c + t
                vsend[at : at + 1, :] = vv[row : row + 1, :]
                vsend[at + 3 : at + 4, :] = vv[row + 48 : row + 49, :]

    def v_send(d, carry):
        v_copy(lax.rem(mine + d, DP), mine).start()
        return carry

    lax.fori_loop(1, DP, v_send, 0)
    own_v = pl.ds(pl.multiple_of(16 * mine, 16), 16)
    vrecv[own_v, :] = vsend[own_v, :]

    c_copy.wait()
    receive_all(1)

    synthesise_z(rbuf.at[1], zw_high, zw_low, held, store)

    def middle_step(o, carry):
        for x in range(XP):
            carried = synthesise_y(store, ty_inverse, x * CH + 2 * o)
            grads = []
            for each in range(2):
                before = carried[:, NZ * each : NZ * each + NZ] + bv[2 * o + each, x]
                slope = 0.5 * (1.0 + lax.erf(before * (1.0 / math.sqrt(2.0)))) + before * jnp.exp(
                    -0.5 * before * before
                ) * (1.0 / math.sqrt(2.0 * math.pi))
                grad = cv[2 * o + each, x] * slope
                cv[2 * o + each, x] = grad
                grads.append(grad)
            analyse_y(cat(grads, 1), ty_stack, store2, x * CH + 2 * o)
        return carry

    lax.fori_loop(0, CH // 2, middle_step, 0)
    analyse_z(store2, tz_weighted, sbuf.at[2])
    send_all(2)

    pacc[...] = jnp.zeros_like(pacc)

    def back_step(yg, carry):
        y0 = pl.multiple_of(yg * 16, 16)
        for x in range(XP):
            high, low = split(rows_of(cv, x, y0))
            stack = cat([high, low], 0)
            mix_channels(kron2, stack, bv, x, y0)
            xhigh, xlow = split(rows_of(xv, x, y0))
            pacc[...] += dot_t(cat([xhigh, xlow], 0), stack)
        return carry

    lax.fori_loop(0, NY // 16, back_step, 0)
    part = pacc[:128, :128] + pacc[:128, 128:] + pacc[128:, :128] + pacc[128:, 128:]
    part = jnp.where(same_row, part, 0.0)
    part = jnp.dot(part, spread, precision=lax.Precision.HIGHEST, preferred_element_type=F32)
    part = lax.dot_general(
        spread, part, (((0,), (0,)), ((), ())), precision=lax.Precision.HIGHEST, preferred_element_type=F32
    )
    gsend[96:112, :] = cat([part, jnp.zeros((CH, 128 - CH), F32)], 1)

    receive_all(2)
    modes = analyse_x(rbuf.at[2], rows_high, rows_low)
    gv[:48, :] = modes[:, :128]
    gv[48:, :] = modes[:, 128:]

    def back_mode_step(c, carry):
        for t in range(3):
            wr = wv[c, :, 0, 128 * t : 128 * t + 128]
            wi = wv[c, :, 1, 128 * t : 128 * t + 128]
            gr = gv[16 * t : 16 * t + 16, :]
            gi = gv[48 + 16 * t : 64 + 16 * t, :]
            vv[pl.ds(16 * t + c, 1), :] = jnp.sum(wr * gr + wi * gi, axis=0, keepdims=True)
            vv[pl.ds(48 + 16 * t + c, 1), :] = jnp.sum(wr * gi - wi * gr, axis=0, keepdims=True)
        return carry

    lax.fori_loop(0, CH, back_mode_step, 0)
    synthesise_x(cat([vv[:48, :], vv[48:, :]], 1), rows_high, rows_low, sbuf.at[3])
    send_all(3)

    def g_copy(d, slot):
        return pltpu.make_async_remote_copy(
            src_ref=gsend,
            dst_ref=grecv.at[pl.ds(pl.multiple_of(112 * slot, 16), 112)],
            send_sem=gssem.at[d],
            recv_sem=grsem.at[slot],
            device_id={"dp": d},
            device_id_type=MESH,
        )

    gsend[:96, :] = gv[...]

    def g_send(d, carry):
        g_copy(lax.rem(mine + d, DP), mine).start()
        return carry

    lax.fori_loop(1, DP, g_send, 0)
    grecv[pl.ds(pl.multiple_of(112 * mine, 16), 112), :] = gsend[...]

    def dp_receive(d, carry):
        peer = lax.rem(mine + d, DP)
        g_copy(peer, peer).wait_recv()
        v_copy(peer, peer).wait_recv()
        return carry

    lax.fori_loop(1, DP, dp_receive, 0)

    for c in range(2):
        def sample_step(d, carry):
            out = []
            base = pl.multiple_of(112 * d, 16)
            for t in range(3):
                vr = vrecv[pl.ds(16 * d + 6 * c + t, 1), :]
                vi = vrecv[pl.ds(16 * d + 6 * c + 3 + t, 1), :]
                gr = grecv[pl.ds(base + 16 * t, 16), :]
                gi = grecv[pl.ds(base + 48 + 16 * t, 16), :]
                out.append(carry[2 * t] + (gr * vr + gi * vi))
                out.append(carry[2 * t + 1] + (gi * vr - gr * vi))
            return tuple(out)

        total = lax.fori_loop(0, DP, sample_step, tuple(jnp.zeros((CH, 128), F32) for _ in range(6)))
        for t in range(3):
            gs_ref[c, :, 0, 128 * t : 128 * t + 128] = total[2 * t]
            gs_ref[c, :, 1, 128 * t : 128 * t + 128] = total[2 * t + 1]

    def p_copy(p, slot):
        return pltpu.make_async_remote_copy(
            src_ref=psend,
            dst_ref=precv.at[pl.ds(pl.multiple_of(16 * slot, 16), 16)],
            send_sem=pssem.at[p],
            recv_sem=prsem.at[slot],
            device_id={"slab": p},
            device_id_type=MESH,
        )

    psum = grecv[96:112, :]
    for d in range(1, DP):
        psum = psum + grecv[112 * d + 96 : 112 * d + 112, :]
    psend[...] = psum

    def p_send(d, carry):
        p_copy(lax.rem(me + d, SLAB), me).start()
        return carry

    lax.fori_loop(1, SLAB, p_send, 0)
    precv[pl.ds(pl.multiple_of(16 * me, 16), 16), :] = psum

    receive_all(3)

    synthesise_z(rbuf.at[3], zp_high, zp_low, held, store)

    def o_copy(c):
        return pltpu.make_async_copy(bv.at[pl.ds(2 * c, 2)], gi_hbm.at[pl.ds(2 * c, 2)], osem.at[c])

    def last_step(c, carry):
        for x in range(XP):
            out = synthesise_y(store, ty_inverse, x * CH + 2 * c)
            bv[2 * c, x] = bv[2 * c, x] + out[:, :NZ]
            bv[2 * c + 1, x] = bv[2 * c + 1, x] + out[:, NZ:]
        o_copy(c).start()
        return carry

    lax.fori_loop(0, CH // 2, last_step, 0)

    def p_receive(d, carry):
        peer = lax.rem(me + d, SLAB)
        p_copy(peer, peer).wait_recv()
        return carry

    lax.fori_loop(1, SLAB, p_receive, 0)
    total = precv[0:16, :]
    for s in range(1, SLAB):
        total = total + precv[16 * s : 16 * s + 16, :]
    gp_ref[...] = total[:, :CH] * (1.0 / math.sqrt(DP * NX * NY * NZ))

    for phase in range(4):
        sent_all(phase)

    def dp_sent(d, carry):
        peer = lax.rem(mine + d, DP)
        v_copy(peer, mine).wait_send()
        g_copy(peer, mine).wait_send()
        return carry

    lax.fori_loop(1, DP, dp_sent, 0)

    def p_sent(d, carry):
        p_copy(lax.rem(me + d, SLAB), me).wait_send()
        return carry

    lax.fori_loop(1, SLAB, p_sent, 0)
    for c in range(CH // 2):
        o_copy(c).wait()


def body(inputs, cotangent, spectral_weights, pointwise_weights):
    constants = [jnp.asarray(table) for table in tables()]
    anywhere = pl.BlockSpec(memory_space=pl.ANY)
    vmem = pl.BlockSpec(memory_space=pltpu.VMEM)
    block = (CH, XP, NY, NZ)
    dma = pltpu.SemaphoreType.DMA
    grad_inputs, grad_spectral, grad_pointwise = pl.pallas_call(
        kernel,
        out_shape=[
            jax.ShapeDtypeStruct(block, F32),
            jax.ShapeDtypeStruct((2, CH, 2, KX * KZ), F32),
            jax.ShapeDtypeStruct((CH, CH), F32),
        ],
        in_specs=[anywhere] * 3 + [vmem] * (1 + len(constants)),
        out_specs=[anywhere, vmem, vmem],
        scratch_shapes=[
            pltpu.VMEM(block, F32),
            pltpu.VMEM(block, F32),
            pltpu.VMEM(block, F32),
            pltpu.VMEM((CH, CH, 2, KX * KZ), F32),
            pltpu.VMEM((CH * XP * 64, NZ), F32),
            pltpu.VMEM((CH * XP * 64, NZ), F32),
            pltpu.VMEM((512, 256), BF16),
            pltpu.VMEM((4, SLAB * ROWS, 128), F32),
            pltpu.VMEM((4, SLAB * ROWS, 128), F32),
            pltpu.VMEM((96, 128), F32),
            pltpu.VMEM((96, 128), F32),
            pltpu.VMEM((256, 256), BF16),
            pltpu.VMEM((256, 256), BF16),
            pltpu.VMEM((256, 256), F32),
            pltpu.VMEM((16 * DP, 128), F32),
            pltpu.VMEM((16 * DP, 128), F32),
            pltpu.VMEM((112, 128), F32),
            pltpu.VMEM((112 * DP, 128), F32),
            pltpu.VMEM((16, 128), F32),
            pltpu.VMEM((16 * SLAB, 128), F32),
            dma((CH // 2,)),
            dma,
            dma,
            dma((CH // 2,)),
            dma((4, SLAB)),
            dma((4, SLAB)),
            dma((DP,)),
            dma((DP,)),
            dma((DP,)),
            dma((DP,)),
            dma((SLAB,)),
            dma((SLAB,)),
        ],
        compiler_params=pltpu.CompilerParams(
            collective_id=0, has_side_effects=True, vmem_limit_bytes=48 * 1024 * 1024
        ),
        name="layer_backward",
    )(inputs.reshape(block), cotangent.reshape(block), spectral_weights, pointwise_weights, *constants)
    return (grad_inputs[None], grad_spectral, grad_pointwise)


def solution(mesh):
    placed = (
        P("dp", None, "slab", None, None),
        P("dp", None, "slab", None, None),
        P(None, None, None, "slab"),
        P(),
    )
    return jax.shard_map(
        body,
        mesh=mesh,
        in_specs=placed,
        out_specs=(P("dp", None, "slab", None, None), P("dp", None, None, "slab"), P()),
        check_vma=False,
    )
```

```python
import functools
import math

import jax
import jax.numpy as jnp
import ml_dtypes
import numpy as np
from jax import lax
from jax.experimental import pallas as pl
from jax.experimental.pallas import tpu as pltpu
from jax.sharding import PartitionSpec as P

CH = 16
XP = 4
NX = 128
NY = 128
NZ = 128
KX = 32
KY = 32
KZ = 12
SLAB = 32
DP = 8
ROWS = 16
PITCH = 72
F32 = jnp.float32
BF16 = jnp.bfloat16
MESH = pl.DeviceIdType.MESH
NORM = 1.0 / math.sqrt(NX * NY * NZ)


def halves(table):
    table = np.asarray(table, np.float64)
    high = table.astype(ml_dtypes.bfloat16)
    low = (table - high.astype(np.float64)).astype(ml_dtypes.bfloat16)
    return high, low


def angles(length, orders):
    places = np.arange(length)[:, None]
    return ((places * orders[None, :]) % length) * (2.0 * math.pi / length)


@functools.cache
def tables():
    centred = np.arange(KY)
    centred = np.where(centred < KY // 2, centred, centred - KY)
    second = angles(NY, centred)
    third = angles(NZ, np.arange(KZ))
    first = angles(NX, centred)
    ty = np.concatenate([np.cos(second).T, -np.sin(second).T], axis=0)
    ty_high, ty_low = halves(ty)
    ty_stack = np.concatenate(
        [np.concatenate([ty_high, ty_high], axis=1), np.concatenate([ty_low, np.zeros_like(ty_low)], axis=1)], axis=0
    )
    ty_inverse = np.concatenate([ty_high.T, ty_high.T, ty_low.T], axis=1)
    depth = {}
    for name, weights in (("plain", np.ones(KZ)), ("weighted", np.where(np.arange(KZ) == 0, 1.0, 2.0))):
        cosine = (np.cos(third) * weights[None, :]).T
        sine = (np.sin(third) * weights[None, :]).T
        real_row = np.concatenate([cosine, sine], axis=1)
        imag_row = np.concatenate([-sine, cosine], axis=1)
        analysis = np.zeros((2 * ROWS, 2 * NZ))
        analysis[:KZ] = real_row
        analysis[ROWS : ROWS + KZ] = imag_row
        synthesis = np.zeros((2, 15 * ROWS, 2 * NZ))
        synthesis[0, 7 * ROWS : 7 * ROWS + KZ] = real_row
        synthesis[1, 7 * ROWS : 7 * ROWS + KZ] = imag_row
        depth[name] = (np.concatenate(halves(analysis), axis=0),) + halves(synthesis)
    place = first.reshape(SLAB, XP, KX)
    cosine = np.cos(place).transpose(1, 0, 2) * NORM
    sine = np.sin(place).transpose(1, 0, 2) * NORM
    rows = np.zeros((2, XP, 4, SLAB, 2, 4, KX))
    for group in range(4):
        rows[0, :, group, :, 0, group] = cosine
        rows[1, :, group, :, 0, group] = sine
        rows[0, :, group, :, 1, group] = -sine
        rows[1, :, group, :, 1, group] = cosine
    rows = rows.reshape(2 * XP * 4 * SLAB, 2 * 4 * KX)
    ty_inverse = np.concatenate([ty_inverse, np.zeros_like(ty_inverse[:, :64])], axis=1)
    flat = {}
    for name, (analysis, high, low) in depth.items():
        flat[name] = (analysis, high.reshape(-1, 2 * NZ), low.reshape(-1, 2 * NZ))
    columns = rows.T.reshape(256, 4, 256).transpose(1, 0, 2).reshape(1024, 256)
    first_part = (ty_stack, flat["plain"][0]) + halves(rows) + halves(columns) + (ty_inverse,) + flat["weighted"]
    return np.concatenate(first_part, axis=0), np.concatenate((ty_inverse,) + flat["plain"][1:], axis=0)


TY = 0
TZP = 128
XH = 192
XL = XH + 1024
IH = XL + 1024
IL = IH + 1024
TYI = IL + 1024
TZW = TYI + 128
ZWH = TZW + 64
ZWL = ZWH + 480
TABLE = ZWL + 480
LAST_TABLE = 128 + 960


def split(value):
    high = value.astype(BF16)
    low = (value - high.astype(F32)).astype(BF16)
    return high, low


def dot(left, right):
    return jnp.dot(left, right, preferred_element_type=F32)


def dot_t(left, right):
    return lax.dot_general(left, right, (((1,), (1,)), ((), ())), preferred_element_type=F32)


def cat(pieces, axis):
    return jnp.concatenate(pieces, axis=axis)


def analyse_y(pair, ty_stack, store, group):
    high, low = split(pair)
    out = dot(ty_stack[...], cat([high, low], 0))
    out = out[:64] + out[64:]
    store[pl.ds(pl.multiple_of(group * PITCH, 8), 64), :] = out[:, :NZ]
    store[pl.ds(pl.multiple_of((group + 1) * PITCH, 8), 64), :] = out[:, NZ:]


def analyse_z(store, tz_stack, sbuf, first_group, send):
    lanes = lax.broadcasted_iota(jnp.int32, (ROWS, 128), 1) < 64

    def step(turn, carry):
        group = lax.rem(first_group + turn, KY // 4)
        pieces = []
        for each in range(4):
            j = group * 4 + each
            pieces.append(cat([store[pl.ds(j, 64, stride=PITCH), :], store[pl.ds(KY + j, 64, stride=PITCH), :]], 1))
        high, low = split(cat(pieces, 0))
        out = dot_t(tz_stack[...], high)
        out = out[:32] + out[32:] + dot_t(tz_stack[:32, :], low)
        for each in range(2):
            tile = out[:, 128 * each : 128 * each + 128]
            real, imag = tile[:ROWS], tile[ROWS:]
            first = jnp.where(lanes, real, pltpu.roll(imag, 64, axis=1))
            second = jnp.where(lanes, pltpu.roll(real, 64, axis=1), imag)
            base = pl.multiple_of((group * 4 + 2 * each) * ROWS, ROWS)
            sbuf[pl.ds(base, ROWS), :] = first
            sbuf[pl.ds(base + ROWS, ROWS), :] = second
        for each in range(4):
            send(group * 4 + each)
        return carry

    lax.fori_loop(0, KY // 4, step, 0)


def analyse_x(rbuf, rows_high, rows_low):
    parts = []
    for t in range(3):
        block = cat([rbuf[pl.ds(4 * t + k, SLAB, stride=ROWS), :] for k in range(4)], 0).T
        parts.append(cat([block[16 * q : 16 * q + 16] for q in range(8)], 1))
    high, low = split(cat(parts, 0))
    out = dot(cat([high, low], 0), rows_high[...])
    return out[:48] + out[48:] + dot(high, rows_low[...])


def synthesise_x(modes, columns_high, columns_low, sbuf):
    high, low = split(modes)
    both = cat([high, low], 0)
    tiles = []
    for n in range(4):
        out = dot(both, columns_high[pl.ds(256 * n, 256), :])
        tiles.append(out[:48] + out[48:] + dot(high, columns_low[pl.ds(256 * n, 256), :]))
    out = cat(tiles, 1)
    for t in range(3):
        part = out[16 * t : 16 * t + 16]
        block = cat([part[:, 128 * q : 128 * q + 128] for q in range(8)], 0).T
        for k in range(4):
            sbuf[pl.ds(4 * t + k, SLAB, stride=ROWS), :] = block[SLAB * k : SLAB * k + SLAB]


def synthesise_z(rbuf, zi_high, zi_low, held, store):
    for g in range(4):
        block = rbuf[pl.ds(128 * g, 128), :].T
        high, low = split(cat([block[:64], block[64:]], 1))
        held[pl.ds(64 * g, 64), :] = high
        held[pl.ds(256 + 64 * g, 64), :] = low

    def step(jj, carry):
        at = pl.multiple_of(7 * ROWS - ROWS * jj, ROWS)
        table_high = cat([zi_high[pl.ds(at, 128), :], zi_high[pl.ds(at + 240, 128), :]], 0)
        table_low = cat([zi_low[pl.ds(at, 128), :], zi_low[pl.ds(at + 240, 128), :]], 0)
        out = dot(held[...], table_high)
        out = out[:256] + out[256:] + dot(held[:256, :], table_low)
        for g in range(4):
            store[pl.ds(8 * g + jj, 64, stride=PITCH), :] = out[64 * g : 64 * g + 64, :NZ]
            store[pl.ds(KY + 8 * g + jj, 64, stride=PITCH), :] = out[64 * g : 64 * g + 64, NZ:]
        return carry

    lax.fori_loop(0, 8, step, 0)


def synthesise_y(store, ty_inverse, group):
    pair = cat(
        [
            store[pl.ds(pl.multiple_of(group * PITCH, 8), 64), :],
            store[pl.ds(pl.multiple_of((group + 1) * PITCH, 8), 64), :],
        ],
        1,
    )
    high, low = split(pair)
    return dot(ty_inverse[:, :192], cat([high, low, high], 0))


def rows_of(source, x, y0):
    left = cat([source[c, x, pl.ds(y0, 8), :] for c in range(CH)], 0)
    right = cat([source[c, x, pl.ds(y0 + 8, 8), :] for c in range(CH)], 0)
    return cat([left, right], 1)


def mix_channels(kron, halves_stack, target, x, y0):
    out = dot(kron[...], halves_stack)
    out = out[:128] + out[128:]
    for c in range(CH):
        target[c, x, pl.ds(y0, 8), :] = out[8 * c : 8 * c + 8, :NZ]
        target[c, x, pl.ds(y0 + 8, 8), :] = out[8 * c : 8 * c + 8, NZ:]


def kernel(
    x_hbm, cot_hbm, w_hbm, pw_hbm, table_hbm,
    last_ref, mixed_hbm, gs_ref,
    xv, cv, bv, wv, pw, table, store, store2, held, sbuf, rbuf, vv, gv, kron1, kron2, pacc,
    vsend, vrecv, gsend, grecv, psend, precv,
    xsem, csem, wsem, pwsem, tsem, osem, ssem, rsem, vssem, vrsem, gssem, grsem, pssem, prsem,
):
    me = lax.axis_index("slab")
    mine = lax.axis_index("dp")

    def x_copy(c):
        return pltpu.make_async_copy(x_hbm.at[pl.ds(2 * c, 2)], xv.at[pl.ds(2 * c, 2)], xsem.at[c])

    def table_copy(index, start, size):
        return pltpu.make_async_copy(
            table_hbm.at[pl.ds(start, size)], table.at[pl.ds(start, size)], tsem.at[index]
        )

    first_table = table_copy(0, 0, XH)
    first_table.start()
    for c in range(CH // 2):
        x_copy(c).start()
    pw_copy = pltpu.make_async_copy(pw_hbm, pw, pwsem)
    pw_copy.start()
    second_table = table_copy(1, XH, TABLE - XH)
    second_table.start()
    w_copy = pltpu.make_async_copy(w_hbm, wv, wsem)
    w_copy.start()
    c_copy = pltpu.make_async_copy(cot_hbm, cv, csem)
    c_copy.start()

    barrier = pltpu.get_barrier_semaphore()

    def greet_slab(d, carry):
        pl.semaphore_signal(barrier, inc=1, device_id={"slab": lax.rem(me + d, SLAB)}, device_id_type=MESH)
        return carry

    def greet_dp(d, carry):
        pl.semaphore_signal(barrier, inc=1, device_id={"dp": lax.rem(mine + d, DP)}, device_id_type=MESH)
        return carry

    lax.fori_loop(1, SLAB, greet_slab, 0)
    lax.fori_loop(1, DP, greet_dp, 0)

    ty_stack = table.at[pl.ds(TY, 128)]
    tz_plain = table.at[pl.ds(TZP, 64)]
    rows_high = table.at[pl.ds(XH, 1024)]
    rows_low = table.at[pl.ds(XL, 1024)]
    columns_high = table.at[pl.ds(IH, 1024)]
    columns_low = table.at[pl.ds(IL, 1024)]
    ty_inverse = table.at[pl.ds(TYI, 128)]
    tz_weighted = table.at[pl.ds(TZW, 64)]
    zw_high = table.at[pl.ds(ZWH, 480)]
    zw_low = table.at[pl.ds(ZWL, 480)]

    def slab_copy(phase, p):
        return pltpu.make_async_remote_copy(
            src_ref=sbuf.at[phase, pl.ds(pl.multiple_of(ROWS * p, ROWS), ROWS)],
            dst_ref=rbuf.at[phase, pl.ds(pl.multiple_of(ROWS * me, ROWS), ROWS)],
            send_sem=ssem.at[phase],
            recv_sem=rsem.at[phase],
            device_id={"slab": p},
            device_id_type=MESH,
        )

    def slab_all(phase):
        every = pl.ds(0, ROWS * (SLAB - 1))
        return pltpu.make_async_remote_copy(
            src_ref=sbuf.at[phase, every],
            dst_ref=rbuf.at[phase, every],
            send_sem=ssem.at[phase],
            recv_sem=rsem.at[phase],
            device_id={"slab": lax.rem(me + 1, SLAB)},
            device_id_type=MESH,
        )

    def keep_own(phase):
        own = pl.ds(pl.multiple_of(ROWS * me, ROWS), ROWS)
        rbuf[phase, own, :] = sbuf[phase, own, :]

    def send_one(phase):
        def send(p):
            @pl.when(p != me)
            def _():
                slab_copy(phase, p).start()

            @pl.when(p == me)
            def _():
                keep_own(phase)

        return send

    def send_all(phase):
        def step(turn, carry):
            for each in range(4):
                slab_copy(phase, lax.rem(me + 16 + 4 * turn + each, SLAB)).start()
            return carry

        lax.fori_loop(0, 4, step, 0)

        def near_step(turn, carry):
            for each in range(3):
                slab_copy(phase, lax.rem(me + 1 + 3 * turn + each, SLAB)).start()
            return carry

        lax.fori_loop(0, 5, near_step, 0)
        keep_own(phase)

    first_group = me // 4 + 4

    spread = (
        lax.broadcasted_iota(jnp.int32, (128, CH), 0) // 8 == lax.broadcasted_iota(jnp.int32, (128, CH), 1)
    ).astype(F32)
    same_row = (
        lax.broadcasted_iota(jnp.int32, (128, 128), 0) % 8 == lax.broadcasted_iota(jnp.int32, (128, 128), 1) % 8
    )

    first_table.wait()

    def forward_step(c, carry):
        x_copy(c).wait()
        for x in range(XP):
            analyse_y(cat([xv[2 * c, x], xv[2 * c + 1, x]], 1), ty_stack, store, x * CH + 2 * c)
        return carry

    lax.fori_loop(0, CH // 2, forward_step, 0)
    pl.semaphore_wait(barrier, SLAB - 1 + DP - 1)
    analyse_z(store, tz_plain, sbuf.at[0], first_group, send_one(0))

    pw_copy.wait()
    wide = jnp.dot(spread, pw[...], precision=lax.Precision.HIGHEST, preferred_element_type=F32)
    wide = lax.dot_general(
        wide, spread, (((1,), (1,)), ((), ())), precision=lax.Precision.HIGHEST, preferred_element_type=F32
    )
    wide = jnp.where(same_row, wide, 0.0)
    for kron, value in ((kron1, wide.T), (kron2, wide)):
        high, low = split(value)
        kron[...] = cat([cat([high, high], 1), cat([low, jnp.zeros_like(low)], 1)], 0)
    for phase in (1, 3):
        for k in range(KZ, ROWS):
            sbuf[phase, pl.ds(k, SLAB, stride=ROWS), :] = jnp.zeros((SLAB, 128), F32)

    def mix_step(yg, carry):
        y0 = pl.multiple_of(yg * 16, 16)
        for x in range(XP):
            high, low = split(rows_of(xv, x, y0))
            mix_channels(kron1, cat([high, low], 0), bv, x, y0)
        return carry

    lax.fori_loop(0, NY // 16, mix_step, 0)
    w_copy.wait()
    second_table.wait()
    slab_all(0).wait_recv()
    modes = analyse_x(rbuf.at[0], rows_high, rows_low)
    vv[:48, :] = modes[:, :128]
    vv[48:, :] = modes[:, 128:]

    def mode_step(c, carry):
        out = []
        for t in range(3):
            wr = wv[c, :, 0, 128 * t : 128 * t + 128]
            wi = wv[c, :, 1, 128 * t : 128 * t + 128]
            vr = vv[pl.ds(16 * t + c, 1), :]
            vi = vv[pl.ds(48 + 16 * t + c, 1), :]
            out.append(carry[2 * t] + (wr * vr - wi * vi))
            out.append(carry[2 * t + 1] + (wr * vi + wi * vr))
        return tuple(out)

    mixed = lax.fori_loop(0, CH, mode_step, tuple(jnp.zeros((CH, 128), F32) for _ in range(6)))
    mixed = cat([cat([mixed[2 * t], mixed[2 * t + 1]], 1) for t in range(3)], 0)
    synthesise_x(mixed, columns_high, columns_low, sbuf.at[1])
    send_all(1)

    def v_copy(d):
        return pltpu.make_async_remote_copy(
            src_ref=vsend.at[pl.ds(pl.multiple_of(16 * d, 16), 16)],
            dst_ref=vrecv.at[pl.ds(pl.multiple_of(16 * mine, 16), 16)],
            send_sem=vssem,
            recv_sem=vrsem,
            device_id={"dp": d},
            device_id_type=MESH,
        )

    vsend[...] = jnp.zeros_like(vsend)
    for d in range(DP):
        for c in range(2):
            for t in range(3):
                row = 16 * t + 2 * d + c
                at = 16 * d + 6 * c + t
                vsend[at : at + 1, :] = vv[row : row + 1, :]
                vsend[at + 3 : at + 4, :] = vv[row + 48 : row + 49, :]

    def v_send(d, carry):
        v_copy(lax.rem(mine + d, DP)).start()
        return carry

    lax.fori_loop(1, DP, v_send, 0)
    own_v = pl.ds(pl.multiple_of(16 * mine, 16), 16)
    vrecv[own_v, :] = vsend[own_v, :]

    c_copy.wait()
    slab_all(1).wait_recv()

    synthesise_z(rbuf.at[1], zw_high, zw_low, held, store)

    def middle_step(o, carry):
        for x in range(XP):
            carried = synthesise_y(store, ty_inverse, x * CH + 2 * o)
            grads = []
            for each in range(2):
                before = carried[:, NZ * each : NZ * each + NZ] + bv[2 * o + each, x]
                slope = 0.5 * (1.0 + lax.erf(before * (1.0 / math.sqrt(2.0)))) + before * jnp.exp(
                    -0.5 * before * before
                ) * (1.0 / math.sqrt(2.0 * math.pi))
                grad = cv[2 * o + each, x] * slope
                cv[2 * o + each, x] = grad
                grads.append(grad)
            analyse_y(cat(grads, 1), ty_stack, store2, x * CH + 2 * o)
        return carry

    lax.fori_loop(0, CH // 2, middle_step, 0)
    analyse_z(store2, tz_weighted, sbuf.at[2], first_group, send_one(2))

    pacc[...] = jnp.zeros_like(pacc)

    def back_step(yg, carry):
        y0 = pl.multiple_of(yg * 16, 16)
        for x in range(XP):
            high, low = split(rows_of(cv, x, y0))
            stack = cat([high, low], 0)
            mix_channels(kron2, stack, bv, x, y0)
            xhigh, xlow = split(rows_of(xv, x, y0))
            pacc[...] += dot_t(cat([xhigh, xlow], 0), stack)
        return carry

    lax.fori_loop(0, NY // 16, back_step, 0)
    o_copy = pltpu.make_async_copy(bv, mixed_hbm, osem)
    o_copy.start()
    part = pacc[:128, :128] + pacc[:128, 128:] + pacc[128:, :128] + pacc[128:, 128:]
    part = jnp.where(same_row, part, 0.0)
    part = jnp.dot(part, spread, precision=lax.Precision.HIGHEST, preferred_element_type=F32)
    part = lax.dot_general(
        spread, part, (((0,), (0,)), ((), ())), precision=lax.Precision.HIGHEST, preferred_element_type=F32
    )
    part = cat([part, jnp.zeros((CH, 128 - CH), F32)], 1)

    def p_copy(d):
        return pltpu.make_async_remote_copy(
            src_ref=psend,
            dst_ref=precv.at[pl.ds(pl.multiple_of(16 * mine, 16), 16)],
            send_sem=pssem,
            recv_sem=prsem,
            device_id={"dp": d},
            device_id_type=MESH,
        )

    psend[...] = part

    def p_send(d, carry):
        p_copy(lax.rem(mine + d, DP)).start()
        return carry

    lax.fori_loop(1, DP, p_send, 0)
    precv[pl.ds(pl.multiple_of(16 * mine, 16), 16), :] = part

    slab_all(2).wait_recv()
    modes = analyse_x(rbuf.at[2], rows_high, rows_low)
    gv[:48, :] = modes[:, :128]
    gv[48:, :] = modes[:, 128:]

    def back_mode_step(c, carry):
        for t in range(3):
            wr = wv[c, :, 0, 128 * t : 128 * t + 128]
            wi = wv[c, :, 1, 128 * t : 128 * t + 128]
            gr = gv[16 * t : 16 * t + 16, :]
            gi = gv[48 + 16 * t : 64 + 16 * t, :]
            vv[pl.ds(16 * t + c, 1), :] = jnp.sum(wr * gr + wi * gi, axis=0, keepdims=True)
            vv[pl.ds(48 + 16 * t + c, 1), :] = jnp.sum(wr * gi - wi * gr, axis=0, keepdims=True)
        return carry

    lax.fori_loop(0, CH, back_mode_step, 0)

    def dp_all(source, target, size, send_sem, recv_sem):
        return pltpu.make_async_remote_copy(
            src_ref=source.at[pl.ds(0, size)],
            dst_ref=target.at[pl.ds(0, size)],
            send_sem=send_sem,
            recv_sem=recv_sem,
            device_id={"dp": lax.rem(mine + 1, DP)},
            device_id_type=MESH,
        )

    p_all = dp_all(precv, precv, 16 * (DP - 1), pssem, prsem)
    v_all = dp_all(vrecv, vrecv, 16 * (DP - 1), vssem, vrsem)
    g_all = dp_all(grecv, grecv, 96 * (DP - 1), gssem, grsem)
    p_all.wait_recv()
    total = precv[0:16, :]
    for d in range(1, DP):
        total = total + precv[16 * d : 16 * d + 16, :]
    for r in range(2):
        flat = cat([total[8 * r + i : 8 * r + i + 1, :CH] for i in range(8)], 1)
        sbuf[3, pl.ds(KZ + r, SLAB, stride=ROWS), :] = jnp.broadcast_to(flat, (SLAB, 128))
    synthesise_x(cat([vv[:48, :], vv[48:, :]], 1), columns_high, columns_low, sbuf.at[3])
    send_all(3)

    def g_copy(d):
        return pltpu.make_async_remote_copy(
            src_ref=gsend,
            dst_ref=grecv.at[pl.ds(pl.multiple_of(96 * mine, 16), 96)],
            send_sem=gssem,
            recv_sem=grsem,
            device_id={"dp": d},
            device_id_type=MESH,
        )

    gsend[...] = gv[...]

    def g_send(d, carry):
        g_copy(lax.rem(mine + d, DP)).start()
        return carry

    lax.fori_loop(1, DP, g_send, 0)
    grecv[pl.ds(pl.multiple_of(96 * mine, 16), 96), :] = gv[...]
    v_all.wait_recv()
    g_all.wait_recv()

    for c in range(2):
        def sample_step(d, carry):
            out = []
            base = pl.multiple_of(96 * d, 16)
            for t in range(3):
                vr = vrecv[pl.ds(16 * d + 6 * c + t, 1), :]
                vi = vrecv[pl.ds(16 * d + 6 * c + 3 + t, 1), :]
                gr = grecv[pl.ds(base + 16 * t, 16), :]
                gi = grecv[pl.ds(base + 48 + 16 * t, 16), :]
                out.append(carry[2 * t] + (gr * vr + gi * vi))
                out.append(carry[2 * t + 1] + (gi * vr - gr * vi))
            return tuple(out)

        total = lax.fori_loop(0, DP, sample_step, tuple(jnp.zeros((CH, 128), F32) for _ in range(6)))
        for t in range(3):
            gs_ref[c, :, 0, 128 * t : 128 * t + 128] = total[2 * t]
            gs_ref[c, :, 1, 128 * t : 128 * t + 128] = total[2 * t + 1]

    slab_all(3).wait_recv()
    last_ref[...] = rbuf[3]

    for phase in range(4):
        slab_all(phase).wait_send()
    p_out = pltpu.make_async_remote_copy(
        src_ref=precv.at[pl.ds(0, 16 * (DP - 1))],
        dst_ref=precv.at[pl.ds(0, 16 * (DP - 1))],
        send_sem=pssem,
        recv_sem=prsem,
        device_id={"dp": lax.rem(mine + 1, DP)},
        device_id_type=MESH,
    )
    p_out.wait_send()
    v_all.wait_send()
    g_all.wait_send()
    o_copy.wait()


def last_kernel(
    rows_hbm, mixed_hbm, gs_in, table_hbm, gi_hbm, gs_hbm, gp_hbm,
    rows_ref, gs_ref, bv, table, held, store, gp, insem, tsem, osem, gssem, gpsem, rsem,
):
    rows_copy = pltpu.make_async_copy(rows_hbm, rows_ref, rsem)
    rows_copy.start()
    table_copy = pltpu.make_async_copy(table_hbm, table, tsem)
    table_copy.start()

    def in_copy(c):
        return pltpu.make_async_copy(mixed_hbm.at[pl.ds(2 * c, 2)], bv.at[pl.ds(2 * c, 2)], insem.at[c])

    def out_copy(c):
        return pltpu.make_async_copy(bv.at[pl.ds(2 * c, 2)], gi_hbm.at[pl.ds(2 * c, 2)], osem.at[c])

    for c in range(CH // 2):
        in_copy(c).start()
    gs_load = pltpu.make_async_copy(gs_in, gs_ref, gssem)
    gs_load.start()
    rows_copy.wait()
    for r in range(2):
        flat = jnp.sum(rows_ref[pl.ds(KZ + r, SLAB, stride=ROWS), :], axis=0, keepdims=True)
        for i in range(8):
            gp[8 * r + i : 8 * r + i + 1, :] = flat[:, CH * i : CH * i + CH] * (1.0 / math.sqrt(DP * NX * NY * NZ))
    gp_copy = pltpu.make_async_copy(gp, gp_hbm, gpsem)
    gp_copy.start()
    table_copy.wait()
    ty_inverse = table.at[pl.ds(0, 128)]
    synthesise_z(rows_ref, table.at[pl.ds(128, 480)], table.at[pl.ds(608, 480)], held, store)

    def last_step(c, carry):
        in_copy(c).wait()
        for x in range(XP):
            out = synthesise_y(store, ty_inverse, x * CH + 2 * c)
            bv[2 * c, x] = bv[2 * c, x] + out[:, :NZ]
            bv[2 * c + 1, x] = bv[2 * c + 1, x] + out[:, NZ:]
        out_copy(c).start()
        return carry

    gs_load.wait()
    gs_copy = pltpu.make_async_copy(gs_ref, gs_hbm, gssem)
    gs_copy.start()
    lax.fori_loop(0, CH // 2, last_step, 0)
    gs_copy.wait()
    gp_copy.wait()
    for c in range(CH // 2):
        out_copy(c).wait()


def body(inputs, cotangent, spectral_weights, pointwise_weights):
    main_table, last_table = (jnp.asarray(table) for table in tables())
    hbm = pl.BlockSpec(memory_space=pltpu.HBM)
    vmem = pl.BlockSpec(memory_space=pltpu.VMEM)
    block = (CH, XP, NY, NZ)
    dma = pltpu.SemaphoreType.DMA
    block_shape = jax.ShapeDtypeStruct(block, F32)
    weight_shape = jax.ShapeDtypeStruct((2, CH, 2, KX * KZ), F32)
    store_shape = pltpu.VMEM((CH * XP * PITCH, NZ), F32)
    rows, mixed, weight_part = pl.pallas_call(
        kernel,
        out_shape=[jax.ShapeDtypeStruct((SLAB * ROWS, 128), F32), block_shape, weight_shape],
        in_specs=[hbm] * 5,
        out_specs=[vmem, hbm, vmem],
        scratch_shapes=[
            pltpu.VMEM(block, F32),
            pltpu.VMEM(block, F32),
            pltpu.VMEM(block, F32),
            pltpu.VMEM((CH, CH, 2, KX * KZ), F32),
            pltpu.VMEM((CH, CH), F32),
            pltpu.VMEM((TABLE, 256), BF16),
            store_shape,
            store_shape,
            pltpu.VMEM((512, 256), BF16),
            pltpu.VMEM((4, SLAB * ROWS, 128), F32),
            pltpu.VMEM((4, SLAB * ROWS, 128), F32),
            pltpu.VMEM((96, 128), F32),
            pltpu.VMEM((96, 128), F32),
            pltpu.VMEM((256, 256), BF16),
            pltpu.VMEM((256, 256), BF16),
            pltpu.VMEM((256, 256), F32),
            pltpu.VMEM((16 * DP, 128), F32),
            pltpu.VMEM((16 * DP, 128), F32),
            pltpu.VMEM((96, 128), F32),
            pltpu.VMEM((96 * DP, 128), F32),
            pltpu.VMEM((16, 128), F32),
            pltpu.VMEM((16 * DP, 128), F32),
            dma((CH // 2,)),
            dma,
            dma,
            dma,
            dma((2,)),
            dma,
            dma((4,)),
            dma((4,)),
            dma,
            dma,
            dma,
            dma,
            dma,
            dma,
        ],
        compiler_params=pltpu.CompilerParams(
            collective_id=0, has_side_effects=True, vmem_limit_bytes=60 * 1024 * 1024
        ),
        name="layer_backward",
    )(inputs.reshape(block), cotangent.reshape(block), spectral_weights, pointwise_weights, main_table)
    grad_inputs, grad_spectral, grad_pointwise = pl.pallas_call(
        last_kernel,
        out_shape=[block_shape, weight_shape, jax.ShapeDtypeStruct((CH, CH), F32)],
        in_specs=[hbm] * 4,
        out_specs=[hbm, hbm, hbm],
        scratch_shapes=[
            pltpu.VMEM((SLAB * ROWS, 128), F32),
            pltpu.VMEM((2, CH, 2, KX * KZ), F32),
            pltpu.VMEM(block, F32),
            pltpu.VMEM((LAST_TABLE, 256), BF16),
            pltpu.VMEM((512, 256), BF16),
            store_shape,
            pltpu.VMEM((CH, CH), F32),
            dma((CH // 2,)),
            dma,
            dma((CH // 2,)),
            dma,
            dma,
            dma,
        ],
        compiler_params=pltpu.CompilerParams(vmem_limit_bytes=60 * 1024 * 1024),
        name="input_gradient",
    )(rows, mixed, weight_part, last_table)
    return (grad_inputs[None], grad_spectral, grad_pointwise)


def solution(mesh):
    placed = (
        P("dp", None, "slab", None, None),
        P("dp", None, "slab", None, None),
        P(None, None, None, "slab"),
        P(),
    )
    return jax.shard_map(
        body,
        mesh=mesh,
        in_specs=placed,
        out_specs=(P("dp", None, "slab", None, None), P("dp", None, None, "slab"), P()),
        check_vma=False,
    )
```

```python
import functools
import math

import jax
import jax.numpy as jnp
import ml_dtypes
import numpy as np
from jax import lax
from jax.experimental import pallas as pl
from jax.experimental.pallas import tpu as pltpu
from jax.sharding import PartitionSpec as P

CH = 16
XP = 4
NX = 128
NY = 128
NZ = 128
KX = 32
KY = 32
KZ = 12
SLAB = 32
DP = 8
ROWS = 16
PITCH = 72
F32 = jnp.float32
BF16 = jnp.bfloat16
MESH = pl.DeviceIdType.MESH
NORM = 1.0 / math.sqrt(NX * NY * NZ)


def halves(table):
    table = np.asarray(table, np.float64)
    high = table.astype(ml_dtypes.bfloat16)
    low = (table - high.astype(np.float64)).astype(ml_dtypes.bfloat16)
    return high, low


def angles(length, orders):
    places = np.arange(length)[:, None]
    return ((places * orders[None, :]) % length) * (2.0 * math.pi / length)


@functools.cache
def tables():
    centred = np.arange(KY)
    centred = np.where(centred < KY // 2, centred, centred - KY)
    second = angles(NY, centred)
    third = angles(NZ, np.arange(KZ))
    first = angles(NX, centred)
    ty = np.concatenate([np.cos(second).T, -np.sin(second).T], axis=0)
    ty_high, ty_low = halves(ty)
    ty_stack = np.concatenate(
        [np.concatenate([ty_high, ty_high], axis=1), np.concatenate([ty_low, np.zeros_like(ty_low)], axis=1)], axis=0
    )
    ty_inverse = np.concatenate([ty_high.T, ty_high.T, ty_low.T], axis=1)
    depth = {}
    for name, weights in (("plain", np.ones(KZ)), ("weighted", np.where(np.arange(KZ) == 0, 1.0, 2.0))):
        cosine = (np.cos(third) * weights[None, :]).T
        sine = (np.sin(third) * weights[None, :]).T
        real_row = np.concatenate([cosine, sine], axis=1)
        imag_row = np.concatenate([-sine, cosine], axis=1)
        analysis = np.zeros((2 * ROWS, 2 * NZ))
        analysis[:KZ] = real_row
        analysis[ROWS : ROWS + KZ] = imag_row
        synthesis = np.zeros((2, 15 * ROWS, 2 * NZ))
        synthesis[0, 7 * ROWS : 7 * ROWS + KZ] = real_row
        synthesis[1, 7 * ROWS : 7 * ROWS + KZ] = imag_row
        depth[name] = (np.concatenate(halves(analysis), axis=0),) + halves(synthesis)
    place = first.reshape(SLAB, XP, KX)
    cosine = np.cos(place).transpose(1, 0, 2) * NORM
    sine = np.sin(place).transpose(1, 0, 2) * NORM
    rows = np.zeros((2, XP, 4, SLAB, 2, 4, KX))
    for group in range(4):
        rows[0, :, group, :, 0, group] = cosine
        rows[1, :, group, :, 0, group] = sine
        rows[0, :, group, :, 1, group] = -sine
        rows[1, :, group, :, 1, group] = cosine
    rows = rows.reshape(2 * XP * 4 * SLAB, 2 * 4 * KX)
    ty_inverse = np.concatenate([ty_inverse, np.zeros_like(ty_inverse[:, :64])], axis=1)
    flat = {}
    for name, (analysis, high, low) in depth.items():
        flat[name] = (analysis, high.reshape(-1, 2 * NZ), low.reshape(-1, 2 * NZ))
    columns = rows.T.reshape(256, 4, 256).transpose(1, 0, 2).reshape(1024, 256)
    first_part = (ty_stack, flat["plain"][0]) + halves(rows) + halves(columns) + (ty_inverse,) + flat["weighted"]
    return np.concatenate(first_part, axis=0), np.concatenate((ty_inverse,) + flat["plain"][1:], axis=0)


TY = 0
TZP = 128
XH = 192
XL = XH + 1024
IH = XL + 1024
IL = IH + 1024
TYI = IL + 1024
TZW = TYI + 128
ZWH = TZW + 64
ZWL = ZWH + 480
TABLE = ZWL + 480
LAST_TABLE = 128 + 960


def split(value):
    high = value.astype(BF16)
    low = (value - high.astype(F32)).astype(BF16)
    return high, low


def dot(left, right):
    return jnp.dot(left, right, preferred_element_type=F32)


def dot_t(left, right):
    return lax.dot_general(left, right, (((1,), (1,)), ((), ())), preferred_element_type=F32)


def cat(pieces, axis):
    return jnp.concatenate(pieces, axis=axis)


def analyse_y(pair, ty_stack, store, group):
    high, low = split(pair)
    out = dot(ty_stack[...], cat([high, low], 0))
    out = out[:64] + out[64:]
    store[pl.ds(pl.multiple_of(group * PITCH, 8), 64), :] = out[:, :NZ]
    store[pl.ds(pl.multiple_of((group + 1) * PITCH, 8), 64), :] = out[:, NZ:]


def analyse_z(store, tz_stack, sbuf, phase, first_group, send):
    lanes = lax.broadcasted_iota(jnp.int32, (ROWS, 128), 1) < 64

    def step(turn, carry):
        group = lax.rem(first_group + turn, KY // 4)
        pieces = []
        for each in range(4):
            j = group * 4 + each
            pieces.append(cat([store[pl.ds(j, 64, stride=PITCH), :], store[pl.ds(KY + j, 64, stride=PITCH), :]], 1))
        high, low = split(cat(pieces, 0))
        out = dot_t(tz_stack[...], high)
        out = out[:32] + out[32:] + dot_t(tz_stack[:32, :], low)
        for each in range(2):
            tile = out[:, 128 * each : 128 * each + 128]
            real, imag = tile[:ROWS], tile[ROWS:]
            first = jnp.where(lanes, real, pltpu.roll(imag, 64, axis=1))
            second = jnp.where(lanes, pltpu.roll(real, 64, axis=1), imag)
            sbuf[phase, group * 4 + 2 * each] = first[:KZ]
            sbuf[phase, group * 4 + 2 * each + 1] = second[:KZ]
        for each in range(4):
            send(group * 4 + each)
        return carry

    lax.fori_loop(0, KY // 4, step, 0)


def analyse_x(rbuf, phase, rows_high, rows_low):
    parts = []
    for t in range(3):
        block = cat([rbuf[phase, :, 4 * t + k, :] for k in range(4)], 0).T
        parts.append(cat([block[16 * q : 16 * q + 16] for q in range(8)], 1))
    high, low = split(cat(parts, 0))
    out = dot(cat([high, low], 0), rows_high[...])
    return out[:48] + out[48:] + dot(high, rows_low[...])


def synthesise_x(modes, columns_high, columns_low, put):
    high, low = split(modes)
    both = cat([high, low], 0)
    tiles = []
    for n in range(4):
        out = dot(both, columns_high[pl.ds(256 * n, 256), :])
        tiles.append(out[:48] + out[48:] + dot(high, columns_low[pl.ds(256 * n, 256), :]))
    out = cat(tiles, 1)
    for t in range(3):
        part = out[16 * t : 16 * t + 16]
        block = cat([part[:, 128 * q : 128 * q + 128] for q in range(8)], 0).T
        for k in range(4):
            put(4 * t + k, block[SLAB * k : SLAB * k + SLAB])


def synthesise_z(block_of, zi_high, zi_low, held, store):
    for g in range(4):
        block = block_of(g).T
        high, low = split(cat([block[:64], block[64:]], 1))
        held[pl.ds(64 * g, 64), :] = high
        held[pl.ds(256 + 64 * g, 64), :] = low

    def step(jj, carry):
        at = pl.multiple_of(7 * ROWS - ROWS * jj, ROWS)
        table_high = cat([zi_high[pl.ds(at, 128), :], zi_high[pl.ds(at + 240, 128), :]], 0)
        table_low = cat([zi_low[pl.ds(at, 128), :], zi_low[pl.ds(at + 240, 128), :]], 0)
        out = dot(held[...], table_high)
        out = out[:256] + out[256:] + dot(held[:256, :], table_low)
        for g in range(4):
            store[pl.ds(8 * g + jj, 64, stride=PITCH), :] = out[64 * g : 64 * g + 64, :NZ]
            store[pl.ds(KY + 8 * g + jj, 64, stride=PITCH), :] = out[64 * g : 64 * g + 64, NZ:]
        return carry

    lax.fori_loop(0, 8, step, 0)


def synthesise_y(store, ty_inverse, group):
    pair = cat(
        [
            store[pl.ds(pl.multiple_of(group * PITCH, 8), 64), :],
            store[pl.ds(pl.multiple_of((group + 1) * PITCH, 8), 64), :],
        ],
        1,
    )
    high, low = split(pair)
    return dot(ty_inverse[:, :192], cat([high, low, high], 0))


def rows_of(source, x, y0):
    left = cat([source[c, x, pl.ds(y0, 8), :] for c in range(CH)], 0)
    right = cat([source[c, x, pl.ds(y0 + 8, 8), :] for c in range(CH)], 0)
    return cat([left, right], 1)


def mix_channels(kron, halves_stack, target, x, y0):
    out = dot(kron[...], halves_stack)
    out = out[:128] + out[128:]
    for c in range(CH):
        target[c, x, pl.ds(y0, 8), :] = out[8 * c : 8 * c + 8, :NZ]
        target[c, x, pl.ds(y0 + 8, 8), :] = out[8 * c : 8 * c + 8, NZ:]


def kernel(
    x_hbm, cot_hbm, w_hbm, pw_hbm, table_hbm,
    last_ref, mixed_hbm, gs_ref,
    xv, cv, bv, wv, wco, woc, pw, table, store, store2, held, sbuf, rbuf, sbuf3, rbuf3, vv, gv, kron1, kron2, pacc,
    vsend, vrecv, grecv, psend, precv,
    xsem, csem, wsem, pwsem, tsem, osem, ssem, rsem, vssem, vrsem, gssem, grsem, hssem, hrsem, pssem, prsem,
):
    me = lax.axis_index("slab")
    mine = lax.axis_index("dp")

    def x_copy(c):
        return pltpu.make_async_copy(x_hbm.at[pl.ds(2 * c, 2)], xv.at[pl.ds(2 * c, 2)], xsem.at[c])

    def table_copy(index, start, size):
        return pltpu.make_async_copy(
            table_hbm.at[pl.ds(start, size)], table.at[pl.ds(start, size)], tsem.at[index]
        )

    first_table = table_copy(0, 0, XH)
    first_table.start()
    for c in range(CH // 2):
        x_copy(c).start()
    pw_copy = pltpu.make_async_copy(pw_hbm, pw, pwsem)
    pw_copy.start()
    second_table = table_copy(1, XH, TABLE - XH)
    second_table.start()
    w_copy = pltpu.make_async_copy(w_hbm, wv, wsem)
    w_copy.start()
    c_copy = pltpu.make_async_copy(cot_hbm, cv, csem)
    c_copy.start()

    barrier = pltpu.get_barrier_semaphore()

    def greet_slab(d, carry):
        pl.semaphore_signal(barrier, inc=1, device_id={"slab": lax.rem(me + d, SLAB)}, device_id_type=MESH)
        return carry

    def greet_dp(d, carry):
        pl.semaphore_signal(barrier, inc=1, device_id={"dp": lax.rem(mine + d, DP)}, device_id_type=MESH)
        return carry

    lax.fori_loop(1, SLAB, greet_slab, 0)
    lax.fori_loop(1, DP, greet_dp, 0)

    ty_stack = table.at[pl.ds(TY, 128)]
    tz_plain = table.at[pl.ds(TZP, 64)]
    rows_high = table.at[pl.ds(XH, 1024)]
    rows_low = table.at[pl.ds(XL, 1024)]
    columns_high = table.at[pl.ds(IH, 1024)]
    columns_low = table.at[pl.ds(IL, 1024)]
    ty_inverse = table.at[pl.ds(TYI, 128)]
    tz_weighted = table.at[pl.ds(TZW, 64)]
    zw_high = table.at[pl.ds(ZWH, 480)]
    zw_low = table.at[pl.ds(ZWL, 480)]

    def source(phase, p):
        if phase == 3:
            return sbuf3.at[pl.ds(pl.multiple_of(ROWS * p, ROWS), ROWS)]
        return sbuf.at[phase, p]

    def target(phase, p):
        if phase == 3:
            return rbuf3.at[pl.ds(pl.multiple_of(ROWS * p, ROWS), ROWS)]
        return rbuf.at[phase, p]

    def slab_copy(phase, p):
        return pltpu.make_async_remote_copy(
            src_ref=source(phase, p),
            dst_ref=target(phase, me),
            send_sem=ssem.at[phase],
            recv_sem=rsem.at[phase],
            device_id={"slab": p},
            device_id_type=MESH,
        )

    def slab_all(phase):
        if phase == 3:
            every = pl.ds(0, ROWS * (SLAB - 1))
            src, dst = sbuf3.at[every], rbuf3.at[every]
        else:
            every = pl.ds(0, SLAB - 1)
            src, dst = sbuf.at[phase, every], rbuf.at[phase, every]
        return pltpu.make_async_remote_copy(
            src_ref=src,
            dst_ref=dst,
            send_sem=ssem.at[phase],
            recv_sem=rsem.at[phase],
            device_id={"slab": lax.rem(me + 1, SLAB)},
            device_id_type=MESH,
        )

    def keep_own(phase):
        if phase == 3:
            own = pl.ds(pl.multiple_of(ROWS * me, ROWS), ROWS)
            rbuf3[own, :] = sbuf3[own, :]
        else:
            rbuf[phase, me] = sbuf[phase, me]

    def send_one(phase):
        def send(p):
            @pl.when(p != me)
            def _():
                slab_copy(phase, p).start()

            @pl.when(p == me)
            def _():
                keep_own(phase)

        return send

    def send_all(phase):
        def step(turn, carry):
            for each in range(4):
                slab_copy(phase, lax.rem(me + 16 + 4 * turn + each, SLAB)).start()
            return carry

        lax.fori_loop(0, 4, step, 0)

        def near_step(turn, carry):
            for each in range(3):
                slab_copy(phase, lax.rem(me + 1 + 3 * turn + each, SLAB)).start()
            return carry

        lax.fori_loop(0, 5, near_step, 0)
        keep_own(phase)

    first_group = me // 4 + 4
    core = lax.rem(mine, 2)
    place = core * 4 + mine // 2

    spread = (
        lax.broadcasted_iota(jnp.int32, (128, CH), 0) // 8 == lax.broadcasted_iota(jnp.int32, (128, CH), 1)
    ).astype(F32)
    same_row = (
        lax.broadcasted_iota(jnp.int32, (128, 128), 0) % 8 == lax.broadcasted_iota(jnp.int32, (128, 128), 1) % 8
    )

    first_table.wait()

    def forward_step(c, carry):
        x_copy(c).wait()
        for x in range(XP):
            analyse_y(cat([xv[2 * c, x], xv[2 * c + 1, x]], 1), ty_stack, store, x * CH + 2 * c)
        return carry

    lax.fori_loop(0, CH // 2, forward_step, 0)
    pl.semaphore_wait(barrier, SLAB - 1 + DP - 1)
    analyse_z(store, tz_plain, sbuf, 0, first_group, send_one(0))

    pw_copy.wait()
    wide = jnp.dot(spread, pw[...], precision=lax.Precision.HIGHEST, preferred_element_type=F32)
    wide = lax.dot_general(
        wide, spread, (((1,), (1,)), ((), ())), precision=lax.Precision.HIGHEST, preferred_element_type=F32
    )
    wide = jnp.where(same_row, wide, 0.0)
    for kron, value in ((kron1, wide.T), (kron2, wide)):
        high, low = split(value)
        kron[...] = cat([cat([high, high], 1), cat([low, jnp.zeros_like(low)], 1)], 0)
    for k in range(KZ + 2, ROWS):
        sbuf3[pl.ds(k, SLAB, stride=ROWS), :] = jnp.zeros((SLAB, 128), F32)

    def mix_step(yg, carry):
        y0 = pl.multiple_of(yg * 16, 16)
        for x in range(XP):
            high, low = split(rows_of(xv, x, y0))
            mix_channels(kron1, cat([high, low], 0), bv, x, y0)
        return carry

    lax.fori_loop(0, NY // 16, mix_step, 0)
    w_copy.wait()

    def regroup_step(c, carry):
        base = pl.multiple_of(c * 96, 16)
        for ri in range(2):
            for t in range(3):
                wco[pl.ds(base + 48 * ri + 16 * t, 16), :] = wv[c, :, ri, 128 * t : 128 * t + 128]
        return carry

    lax.fori_loop(0, CH, regroup_step, 0)
    second_table.wait()
    slab_all(0).wait_recv()
    modes = analyse_x(rbuf, 0, rows_high, rows_low)
    vv[:48, :] = modes[:, :128]
    vv[48:, :] = modes[:, 128:]

    def spread_row(modes, c):
        return cat([jnp.broadcast_to(modes[pl.ds(16 * t + c, 1), :], (16, 128)) for t in range(3)], 0), cat(
            [jnp.broadcast_to(modes[pl.ds(48 + 16 * t + c, 1), :], (16, 128)) for t in range(3)], 0
        )

    def mode_step(c, carry):
        base = pl.multiple_of(c * 96, 16)
        wr, wi = wco[pl.ds(base, 48), :], wco[pl.ds(base + 48, 48), :]
        vr, vi = spread_row(vv, c)
        return carry[0] + (wr * vr - wi * vi), carry[1] + (wr * vi + wi * vr)

    no_modes = (jnp.zeros((48, 128), F32), jnp.zeros((48, 128), F32))
    mixed = cat(lax.fori_loop(0, CH, mode_step, no_modes), 1)

    def put_mixed(k, value):
        sbuf[1, :, k, :] = value

    synthesise_x(mixed, columns_high, columns_low, put_mixed)
    send_all(1)

    def v_copy(d):
        return pltpu.make_async_remote_copy(
            src_ref=vsend.at[pl.ds(pl.multiple_of(16 * d, 16), 16)],
            dst_ref=vrecv.at[pl.ds(pl.multiple_of(16 * place, 16), 16)],
            send_sem=vssem,
            recv_sem=vrsem,
            device_id={"dp": d},
            device_id_type=MESH,
        )

    vsend[...] = jnp.zeros_like(vsend)
    for d in range(DP):
        for c in range(2):
            for t in range(3):
                row = 16 * t + 2 * d + c
                at = 16 * d + 6 * c + t
                vsend[at : at + 1, :] = vv[row : row + 1, :]
                vsend[at + 3 : at + 4, :] = vv[row + 48 : row + 49, :]

    def v_send(d, carry):
        v_copy(lax.rem(mine + d, DP)).start()
        return carry

    lax.fori_loop(1, DP, v_send, 0)
    vrecv[pl.ds(pl.multiple_of(16 * place, 16), 16), :] = vsend[pl.ds(pl.multiple_of(16 * mine, 16), 16), :]

    def turn_step(o, carry):
        base = pl.multiple_of(o * 96, 16)
        for part in range(6):
            woc[pl.ds(base + 16 * part, 16), :] = wco[pl.ds(16 * part + o, 16, stride=96), :]
        return carry

    lax.fori_loop(0, CH, turn_step, 0)

    c_copy.wait()
    slab_all(1).wait_recv()

    def block_of(g):
        spare = jnp.zeros((ROWS - KZ, 128), F32)
        pieces = []
        for each in range(8):
            pieces += [rbuf[1, 8 * g + each], spare]
        return cat(pieces, 0)

    synthesise_z(block_of, zw_high, zw_low, held, store)

    def middle_step(o, carry):
        for x in range(XP):
            carried = synthesise_y(store, ty_inverse, x * CH + 2 * o)
            grads = []
            for each in range(2):
                before = carried[:, NZ * each : NZ * each + NZ] + bv[2 * o + each, x]
                slope = 0.5 * (1.0 + lax.erf(before * (1.0 / math.sqrt(2.0)))) + before * jnp.exp(
                    -0.5 * before * before
                ) * (1.0 / math.sqrt(2.0 * math.pi))
                grad = cv[2 * o + each, x] * slope
                cv[2 * o + each, x] = grad
                grads.append(grad)
            analyse_y(cat(grads, 1), ty_stack, store2, x * CH + 2 * o)
        return carry

    lax.fori_loop(0, CH // 2, middle_step, 0)
    analyse_z(store2, tz_weighted, sbuf, 2, first_group, send_one(2))

    pacc[...] = jnp.zeros_like(pacc)

    def back_step(yg, carry):
        y0 = pl.multiple_of(yg * 16, 16)
        for x in range(XP):
            high, low = split(rows_of(cv, x, y0))
            stack = cat([high, low], 0)
            mix_channels(kron2, stack, bv, x, y0)
            xhigh, xlow = split(rows_of(xv, x, y0))
            pacc[...] += dot_t(cat([xhigh, xlow], 0), stack)
        return carry

    lax.fori_loop(0, NY // 16, back_step, 0)
    o_copy = pltpu.make_async_copy(bv, mixed_hbm, osem)
    o_copy.start()
    part = pacc[:128, :128] + pacc[:128, 128:] + pacc[128:, :128] + pacc[128:, 128:]
    part = jnp.where(same_row, part, 0.0)
    part = jnp.dot(part, spread, precision=lax.Precision.HIGHEST, preferred_element_type=F32)
    part = lax.dot_general(
        spread, part, (((0,), (0,)), ((), ())), precision=lax.Precision.HIGHEST, preferred_element_type=F32
    )
    flat = [cat([part[8 * r + i : 8 * r + i + 1, :] for i in range(8)], 1) for r in range(2)]
    part = cat(flat + [jnp.zeros((6, 128), F32)], 0)

    def p_copy(d):
        return pltpu.make_async_remote_copy(
            src_ref=psend,
            dst_ref=precv.at[pl.ds(pl.multiple_of(8 * mine, 8), 8)],
            send_sem=pssem,
            recv_sem=prsem,
            device_id={"dp": d},
            device_id_type=MESH,
        )

    psend[...] = part

    def p_send(d, carry):
        p_copy(lax.rem(mine + d, DP)).start()
        return carry

    lax.fori_loop(1, DP, p_send, 0)
    precv[pl.ds(pl.multiple_of(8 * mine, 8), 8), :] = part

    slab_all(2).wait_recv()
    modes = analyse_x(rbuf, 2, rows_high, rows_low)
    gv[:48, :] = modes[:, :128]
    gv[48:, :] = modes[:, 128:]

    def back_mode_step(o, carry):
        base = pl.multiple_of(o * 96, 16)
        wr, wi = woc[pl.ds(base, 48), :], woc[pl.ds(base + 48, 48), :]
        gr, gi = spread_row(gv, o)
        return carry[0] + (wr * gr + wi * gi), carry[1] + (wr * gi - wi * gr)

    back = cat(lax.fori_loop(0, CH, back_mode_step, no_modes), 1)

    def put_back(k, value):
        sbuf3[pl.ds(k, SLAB, stride=ROWS), :] = value

    def dp_all(source, target, size, send_sem, recv_sem):
        return pltpu.make_async_remote_copy(
            src_ref=source.at[pl.ds(0, size)],
            dst_ref=target.at[pl.ds(0, size)],
            send_sem=send_sem,
            recv_sem=recv_sem,
            device_id={"dp": lax.rem(mine + 1, DP)},
            device_id_type=MESH,
        )

    p_all = dp_all(precv, precv, 8 * (DP - 1), pssem, prsem)
    v_all = dp_all(vrecv, vrecv, 16 * (DP - 1), vssem, vrsem)
    g_all = dp_all(grecv, grecv, 96 * 3, gssem, grsem)
    p_all.wait_recv()
    total = precv[0:8, :]
    for d in range(1, DP):
        total = total + precv[8 * d : 8 * d + 8, :]
    for r in range(2):
        sbuf3[pl.ds(KZ + r, SLAB, stride=ROWS), :] = jnp.broadcast_to(total[r : r + 1, :], (SLAB, 128))
    synthesise_x(back, columns_high, columns_low, put_back)
    send_all(3)

    def g_copy(d):
        return pltpu.make_async_remote_copy(
            src_ref=gv,
            dst_ref=grecv.at[pl.ds(pl.multiple_of(96 * place, 16), 96)],
            send_sem=gssem,
            recv_sem=grsem,
            device_id={"dp": lax.rem(mine + 2 * d, DP)},
            device_id_type=MESH,
        )

    for d in range(1, 4):
        g_copy(d).start()
    grecv[pl.ds(pl.multiple_of(96 * place, 16), 96), :] = gv[...]
    v_all.wait_recv()
    g_all.wait_recv()
    half = pl.ds(pl.multiple_of(core * 384, 16), 384)
    h_copy = pltpu.make_async_remote_copy(
        src_ref=grecv.at[half],
        dst_ref=grecv.at[half],
        send_sem=hssem,
        recv_sem=hrsem,
        device_id={"dp": mine + 1 - 2 * core},
        device_id_type=MESH,
    )
    h_copy.start()
    slab_all(3).wait_recv()
    last_ref[...] = rbuf3[...]
    h_copy.wait()

    for c in range(2):
        def sample_step(d, carry):
            out = []
            base = pl.multiple_of(96 * d, 16)
            for t in range(3):
                vr = vrecv[pl.ds(16 * d + 6 * c + t, 1), :]
                vi = vrecv[pl.ds(16 * d + 6 * c + 3 + t, 1), :]
                gr = grecv[pl.ds(base + 16 * t, 16), :]
                gi = grecv[pl.ds(base + 48 + 16 * t, 16), :]
                out.append(carry[2 * t] + (gr * vr + gi * vi))
                out.append(carry[2 * t + 1] + (gi * vr - gr * vi))
            return tuple(out)

        total = lax.fori_loop(0, DP, sample_step, tuple(jnp.zeros((CH, 128), F32) for _ in range(6)))
        for t in range(3):
            gs_ref[c, :, 0, 128 * t : 128 * t + 128] = total[2 * t]
            gs_ref[c, :, 1, 128 * t : 128 * t + 128] = total[2 * t + 1]

    for phase in range(4):
        slab_all(phase).wait_send()
    p_all.wait_send()
    v_all.wait_send()
    g_all.wait_send()
    o_copy.wait()


def last_kernel(
    rows_hbm, mixed_hbm, gs_in, table_hbm, gi_hbm, gs_hbm, gp_hbm,
    rows_ref, gs_ref, bv, table, held, store, gp, insem, tsem, osem, gssem, gpsem, rsem,
):
    rows_copy = pltpu.make_async_copy(rows_hbm, rows_ref, rsem)
    rows_copy.start()
    table_copy = pltpu.make_async_copy(table_hbm, table, tsem)
    table_copy.start()

    def in_copy(c):
        return pltpu.make_async_copy(mixed_hbm.at[pl.ds(2 * c, 2)], bv.at[pl.ds(2 * c, 2)], insem.at[c])

    def out_copy(c):
        return pltpu.make_async_copy(bv.at[pl.ds(2 * c, 2)], gi_hbm.at[pl.ds(2 * c, 2)], osem.at[c])

    for c in range(CH // 2):
        in_copy(c).start()
    gs_load = pltpu.make_async_copy(gs_in, gs_ref, gssem)
    gs_load.start()
    rows_copy.wait()
    for r in range(2):
        flat = jnp.sum(rows_ref[pl.ds(KZ + r, SLAB, stride=ROWS), :], axis=0, keepdims=True)
        for i in range(8):
            gp[8 * r + i : 8 * r + i + 1, :] = flat[:, CH * i : CH * i + CH] * (1.0 / math.sqrt(DP * NX * NY * NZ))
    gp_copy = pltpu.make_async_copy(gp, gp_hbm, gpsem)
    gp_copy.start()
    table_copy.wait()
    ty_inverse = table.at[pl.ds(0, 128)]
    synthesise_z(lambda g: rows_ref[pl.ds(128 * g, 128), :], table.at[pl.ds(128, 480)], table.at[pl.ds(608, 480)], held, store)

    def last_step(c, carry):
        in_copy(c).wait()
        for x in range(XP):
            out = synthesise_y(store, ty_inverse, x * CH + 2 * c)
            bv[2 * c, x] = bv[2 * c, x] + out[:, :NZ]
            bv[2 * c + 1, x] = bv[2 * c + 1, x] + out[:, NZ:]
        out_copy(c).start()
        return carry

    gs_load.wait()
    gs_copy = pltpu.make_async_copy(gs_ref, gs_hbm, gssem)
    gs_copy.start()
    lax.fori_loop(0, CH // 2, last_step, 0)
    gs_copy.wait()
    gp_copy.wait()
    for c in range(CH // 2):
        out_copy(c).wait()


def body(inputs, cotangent, spectral_weights, pointwise_weights):
    main_table, last_table = (jnp.asarray(table) for table in tables())
    hbm = pl.BlockSpec(memory_space=pltpu.HBM)
    vmem = pl.BlockSpec(memory_space=pltpu.VMEM)
    block = (CH, XP, NY, NZ)
    dma = pltpu.SemaphoreType.DMA
    block_shape = jax.ShapeDtypeStruct(block, F32)
    weight_shape = jax.ShapeDtypeStruct((2, CH, 2, KX * KZ), F32)
    store_shape = pltpu.VMEM((CH * XP * PITCH, NZ), F32)
    rows, mixed, weight_part = pl.pallas_call(
        kernel,
        out_shape=[jax.ShapeDtypeStruct((SLAB * ROWS, 128), F32), block_shape, weight_shape],
        in_specs=[hbm] * 5,
        out_specs=[vmem, hbm, vmem],
        scratch_shapes=[
            pltpu.VMEM(block, F32),
            pltpu.VMEM(block, F32),
            pltpu.VMEM(block, F32),
            pltpu.VMEM((CH, CH, 2, KX * KZ), F32),
            pltpu.VMEM((CH * 96, 128), F32),
            pltpu.VMEM((CH * 96, 128), F32),
            pltpu.VMEM((CH, CH), F32),
            pltpu.VMEM((TABLE, 256), BF16),
            store_shape,
            store_shape,
            pltpu.VMEM((512, 256), BF16),
            pltpu.VMEM((3, SLAB, KZ, 128), F32),
            pltpu.VMEM((3, SLAB, KZ, 128), F32),
            pltpu.VMEM((SLAB * ROWS, 128), F32),
            pltpu.VMEM((SLAB * ROWS, 128), F32),
            pltpu.VMEM((96, 128), F32),
            pltpu.VMEM((96, 128), F32),
            pltpu.VMEM((256, 256), BF16),
            pltpu.VMEM((256, 256), BF16),
            pltpu.VMEM((256, 256), F32),
            pltpu.VMEM((16 * DP, 128), F32),
            pltpu.VMEM((16 * DP, 128), F32),
            pltpu.VMEM((96 * DP, 128), F32),
            pltpu.VMEM((8, 128), F32),
            pltpu.VMEM((8 * DP, 128), F32),
            dma((CH // 2,)),
            dma,
            dma,
            dma,
            dma((2,)),
            dma,
            dma((4,)),
            dma((4,)),
            dma,
            dma,
            dma,
            dma,
            dma,
            dma,
            dma,
            dma,
        ],
        compiler_params=pltpu.CompilerParams(
            collective_id=0, has_side_effects=True, vmem_limit_bytes=60 * 1024 * 1024
        ),
        name="layer_backward",
    )(inputs.reshape(block), cotangent.reshape(block), spectral_weights, pointwise_weights, main_table)
    grad_inputs, grad_spectral, grad_pointwise = pl.pallas_call(
        last_kernel,
        out_shape=[block_shape, weight_shape, jax.ShapeDtypeStruct((CH, CH), F32)],
        in_specs=[hbm] * 4,
        out_specs=[hbm, hbm, hbm],
        scratch_shapes=[
            pltpu.VMEM((SLAB * ROWS, 128), F32),
            pltpu.VMEM((2, CH, 2, KX * KZ), F32),
            pltpu.VMEM(block, F32),
            pltpu.VMEM((LAST_TABLE, 256), BF16),
            pltpu.VMEM((512, 256), BF16),
            store_shape,
            pltpu.VMEM((CH, CH), F32),
            dma((CH // 2,)),
            dma,
            dma((CH // 2,)),
            dma,
            dma,
            dma,
        ],
        compiler_params=pltpu.CompilerParams(vmem_limit_bytes=60 * 1024 * 1024),
        name="input_gradient",
    )(rows, mixed, weight_part, last_table)
    return (grad_inputs[None], grad_spectral, grad_pointwise)


def solution(mesh):
    placed = (
        P("dp", None, "slab", None, None),
        P("dp", None, "slab", None, None),
        P(None, None, None, "slab"),
        P(),
    )
    return jax.shard_map(
        body,
        mesh=mesh,
        in_specs=placed,
        out_specs=(P("dp", None, "slab", None, None), P("dp", None, None, "slab"), P()),
        check_vma=False,
    )
```

```python
import functools
import math

import jax
import jax.numpy as jnp
import ml_dtypes
import numpy as np
from jax import lax
from jax.experimental import pallas as pl
from jax.experimental.pallas import tpu as pltpu
from jax.sharding import PartitionSpec as P

CH = 16
XP = 4
NX = 128
NY = 128
NZ = 128
KX = 32
KY = 32
KZ = 12
SLAB = 32
DP = 8
ROWS = 16
PITCH = 72
F32 = jnp.float32
BF16 = jnp.bfloat16
MESH = pl.DeviceIdType.MESH
NORM = 1.0 / math.sqrt(NX * NY * NZ)


def halves(table):
    table = np.asarray(table, np.float64)
    high = table.astype(ml_dtypes.bfloat16)
    low = (table - high.astype(np.float64)).astype(ml_dtypes.bfloat16)
    return high, low


def angles(length, orders):
    places = np.arange(length)[:, None]
    return ((places * orders[None, :]) % length) * (2.0 * math.pi / length)


@functools.cache
def tables():
    centred = np.arange(KY)
    centred = np.where(centred < KY // 2, centred, centred - KY)
    second = angles(NY, centred)
    third = angles(NZ, np.arange(KZ))
    first = angles(NX, centred)
    ty = np.concatenate([np.cos(second).T, -np.sin(second).T], axis=0)
    ty_high, ty_low = halves(ty)
    ty_stack = np.concatenate(
        [np.concatenate([ty_high, ty_high], axis=1), np.concatenate([ty_low, np.zeros_like(ty_low)], axis=1)], axis=0
    )
    ty_inverse = np.concatenate([ty_high.T, ty_high.T, ty_low.T], axis=1)
    depth = {}
    for name, weights in (("plain", np.ones(KZ)), ("weighted", np.where(np.arange(KZ) == 0, 1.0, 2.0))):
        cosine = (np.cos(third) * weights[None, :]).T
        sine = (np.sin(third) * weights[None, :]).T
        real_row = np.concatenate([cosine, sine], axis=1)
        imag_row = np.concatenate([-sine, cosine], axis=1)
        analysis = np.zeros((2 * ROWS, 2 * NZ))
        analysis[:KZ] = real_row
        analysis[ROWS : ROWS + KZ] = imag_row
        synthesis = np.zeros((2, 15 * ROWS, 2 * NZ))
        synthesis[0, 7 * ROWS : 7 * ROWS + KZ] = real_row
        synthesis[1, 7 * ROWS : 7 * ROWS + KZ] = imag_row
        depth[name] = (np.concatenate(halves(analysis), axis=0),) + halves(synthesis)
    place = first.reshape(SLAB, XP, KX)
    cosine = np.cos(place).transpose(1, 0, 2) * NORM
    sine = np.sin(place).transpose(1, 0, 2) * NORM
    rows = np.zeros((2, XP, 4, SLAB, 2, 4, KX))
    for group in range(4):
        rows[0, :, group, :, 0, group] = cosine
        rows[1, :, group, :, 0, group] = sine
        rows[0, :, group, :, 1, group] = -sine
        rows[1, :, group, :, 1, group] = cosine
    rows = rows.reshape(2 * XP * 4 * SLAB, 2 * 4 * KX)
    ty_inverse = np.concatenate([ty_inverse, np.zeros_like(ty_inverse[:, :64])], axis=1)
    flat = {}
    for name, (analysis, high, low) in depth.items():
        flat[name] = (analysis, high.reshape(-1, 2 * NZ), low.reshape(-1, 2 * NZ))
    columns = rows.T.reshape(256, 4, 256).transpose(1, 0, 2).reshape(1024, 256)
    first_part = (ty_stack, flat["plain"][0]) + halves(rows) + halves(columns) + (ty_inverse,) + flat["weighted"]
    return np.concatenate(first_part, axis=0), np.concatenate((ty_inverse,) + flat["plain"][1:], axis=0)


TY = 0
TZP = 128
XH = 192
XL = XH + 1024
IH = XL + 1024
IL = IH + 1024
TYI = IL + 1024
TZW = TYI + 128
ZWH = TZW + 64
ZWL = ZWH + 480
TABLE = ZWL + 480
LAST_TABLE = 128 + 960


def split(value):
    high = value.astype(BF16)
    low = (value - high.astype(F32)).astype(BF16)
    return high, low


def dot(left, right):
    return jnp.dot(left, right, preferred_element_type=F32)


def dot_t(left, right):
    return lax.dot_general(left, right, (((1,), (1,)), ((), ())), preferred_element_type=F32)


def cat(pieces, axis):
    return jnp.concatenate(pieces, axis=axis)


def analyse_y(pair, ty_stack, store, group):
    high, low = split(pair)
    out = dot(ty_stack[...], cat([high, low], 0))
    out = out[:64] + out[64:]
    store[pl.ds(pl.multiple_of(group * PITCH, 8), 64), :] = out[:, :NZ]
    store[pl.ds(pl.multiple_of((group + 1) * PITCH, 8), 64), :] = out[:, NZ:]


def analyse_z(store, tz_stack, sbuf, phase, first_group, send):
    lanes = lax.broadcasted_iota(jnp.int32, (ROWS, 128), 1) < 64

    def step(turn, carry):
        group = lax.rem(first_group + turn, KY // 4)
        pieces = []
        for each in range(4):
            j = group * 4 + each
            pieces.append(cat([store[pl.ds(j, 64, stride=PITCH), :], store[pl.ds(KY + j, 64, stride=PITCH), :]], 1))
        high, low = split(cat(pieces, 0))
        out = dot_t(tz_stack[...], high)
        out = out[:32] + out[32:] + dot_t(tz_stack[:32, :], low)
        for each in range(2):
            tile = out[:, 128 * each : 128 * each + 128]
            real, imag = tile[:ROWS], tile[ROWS:]
            first = jnp.where(lanes, real, pltpu.roll(imag, 64, axis=1))
            second = jnp.where(lanes, pltpu.roll(real, 64, axis=1), imag)
            sbuf[phase, group * 4 + 2 * each] = first[:KZ]
            sbuf[phase, group * 4 + 2 * each + 1] = second[:KZ]
        for each in range(4):
            send(group * 4 + each)
        return carry

    lax.fori_loop(0, KY // 4, step, 0)


def analyse_x(rbuf, phase, rows_high, rows_low):
    parts = []
    for t in range(3):
        block = cat([rbuf[phase, :, 4 * t + k, :] for k in range(4)], 0).T
        parts.append(cat([block[16 * q : 16 * q + 16] for q in range(8)], 1))
    high, low = split(cat(parts, 0))
    out = dot(cat([high, low], 0), rows_high[...])
    return out[:48] + out[48:] + dot(high, rows_low[...])


def synthesise_x(modes, columns_high, columns_low, put):
    high, low = split(modes)
    both = cat([high, low], 0)
    tiles = []
    for n in range(4):
        out = dot(both, columns_high[pl.ds(256 * n, 256), :])
        tiles.append(out[:48] + out[48:] + dot(high, columns_low[pl.ds(256 * n, 256), :]))
    out = cat(tiles, 1)
    for t in range(3):
        part = out[16 * t : 16 * t + 16]
        block = cat([part[:, 128 * q : 128 * q + 128] for q in range(8)], 0).T
        for k in range(4):
            put(4 * t + k, block[SLAB * k : SLAB * k + SLAB])


def synthesise_z(rbuf, zi_high, zi_low, held, store):
    spare = jnp.zeros((ROWS - KZ, 128), F32)
    for g in range(4):
        pieces = []
        for each in range(8):
            pieces += [rbuf[8 * g + each], spare]
        block = cat(pieces, 0).T
        high, low = split(cat([block[:64], block[64:]], 1))
        held[pl.ds(64 * g, 64), :] = high
        held[pl.ds(256 + 64 * g, 64), :] = low

    def step(jj, carry):
        at = pl.multiple_of(7 * ROWS - ROWS * jj, ROWS)
        table_high = cat([zi_high[pl.ds(at, 128), :], zi_high[pl.ds(at + 240, 128), :]], 0)
        table_low = cat([zi_low[pl.ds(at, 128), :], zi_low[pl.ds(at + 240, 128), :]], 0)
        out = dot(held[...], table_high)
        out = out[:256] + out[256:] + dot(held[:256, :], table_low)
        for g in range(4):
            store[pl.ds(8 * g + jj, 64, stride=PITCH), :] = out[64 * g : 64 * g + 64, :NZ]
            store[pl.ds(KY + 8 * g + jj, 64, stride=PITCH), :] = out[64 * g : 64 * g + 64, NZ:]
        return carry

    lax.fori_loop(0, 8, step, 0, unroll=2)


def synthesise_y(store, ty_inverse, group):
    pair = cat(
        [
            store[pl.ds(pl.multiple_of(group * PITCH, 8), 64), :],
            store[pl.ds(pl.multiple_of((group + 1) * PITCH, 8), 64), :],
        ],
        1,
    )
    high, low = split(pair)
    return dot(ty_inverse[:, :192], cat([high, low, high], 0))


def rows_of(source, x, y0):
    left = cat([source[c, x, pl.ds(y0, 8), :] for c in range(CH)], 0)
    right = cat([source[c, x, pl.ds(y0 + 8, 8), :] for c in range(CH)], 0)
    return cat([left, right], 1)


def mix_channels(kron, halves_stack, target, x, y0):
    out = dot(kron[...], halves_stack)
    out = out[:128] + out[128:]
    for c in range(CH):
        target[c, x, pl.ds(y0, 8), :] = out[8 * c : 8 * c + 8, :NZ]
        target[c, x, pl.ds(y0 + 8, 8), :] = out[8 * c : 8 * c + 8, NZ:]


def kernel(
    x_hbm, cot_hbm, w_hbm, pw_hbm, table_hbm,
    last_ref, mixed_hbm, gs_ref, gp_ref,
    xv, cv, bv, wv, wco, woc, pw, table, store, store2, held, sbuf, rbuf, vv, gv, kron1, kron2, pacc,
    vsend, vrecv, grecv, psend, precv, qsend, qrecv,
    xsem, csem, wsem, pwsem, tsem, osem, ssem, rsem, vssem, vrsem, gssem, grsem, hssem, hrsem, pssem, prsem, qssem, qrsem,
):
    me = lax.axis_index("slab")
    mine = lax.axis_index("dp")

    def x_copy(c):
        return pltpu.make_async_copy(x_hbm.at[pl.ds(2 * c, 2)], xv.at[pl.ds(2 * c, 2)], xsem.at[c])

    def table_copy(index, start, size):
        return pltpu.make_async_copy(
            table_hbm.at[pl.ds(start, size)], table.at[pl.ds(start, size)], tsem.at[index]
        )

    first_table = table_copy(0, 0, XH)
    first_table.start()
    for c in range(CH // 2):
        x_copy(c).start()
    pw_copy = pltpu.make_async_copy(pw_hbm, pw, pwsem)
    pw_copy.start()
    second_table = table_copy(1, XH, TABLE - XH)
    second_table.start()
    w_copy = pltpu.make_async_copy(w_hbm, wv, wsem)
    w_copy.start()
    c_copy = pltpu.make_async_copy(cot_hbm, cv, csem)
    c_copy.start()

    barrier = pltpu.get_barrier_semaphore()

    def greet_slab(d, carry):
        pl.semaphore_signal(barrier, inc=1, device_id={"slab": lax.rem(me + d, SLAB)}, device_id_type=MESH)
        return carry

    def greet_dp(d, carry):
        pl.semaphore_signal(barrier, inc=1, device_id={"dp": lax.rem(mine + d, DP)}, device_id_type=MESH)
        return carry

    lax.fori_loop(1, SLAB, greet_slab, 0)
    lax.fori_loop(1, DP, greet_dp, 0)

    ty_stack = table.at[pl.ds(TY, 128)]
    tz_plain = table.at[pl.ds(TZP, 64)]
    rows_high = table.at[pl.ds(XH, 1024)]
    rows_low = table.at[pl.ds(XL, 1024)]
    columns_high = table.at[pl.ds(IH, 1024)]
    columns_low = table.at[pl.ds(IL, 1024)]
    ty_inverse = table.at[pl.ds(TYI, 128)]
    tz_weighted = table.at[pl.ds(TZW, 64)]
    zw_high = table.at[pl.ds(ZWH, 480)]
    zw_low = table.at[pl.ds(ZWL, 480)]

    def slab_copy(phase, p):
        return pltpu.make_async_remote_copy(
            src_ref=sbuf.at[phase, p],
            dst_ref=rbuf.at[phase, me],
            send_sem=ssem.at[phase],
            recv_sem=rsem.at[phase],
            device_id={"slab": p},
            device_id_type=MESH,
        )

    def slab_all(phase):
        every = pl.ds(0, SLAB - 1)
        return pltpu.make_async_remote_copy(
            src_ref=sbuf.at[phase, every],
            dst_ref=rbuf.at[phase, every],
            send_sem=ssem.at[phase],
            recv_sem=rsem.at[phase],
            device_id={"slab": lax.rem(me + 1, SLAB)},
            device_id_type=MESH,
        )

    def keep_own(phase):
        rbuf[phase, me] = sbuf[phase, me]

    def send_one(phase):
        def send(p):
            @pl.when(p != me)
            def _():
                slab_copy(phase, p).start()

            @pl.when(p == me)
            def _():
                keep_own(phase)

        return send

    def send_all(phase):
        def step(turn, carry):
            for each in range(4):
                slab_copy(phase, lax.rem(me + 16 + 4 * turn + each, SLAB)).start()
            return carry

        lax.fori_loop(0, 4, step, 0)

        def near_step(turn, carry):
            for each in range(3):
                slab_copy(phase, lax.rem(me + 1 + 3 * turn + each, SLAB)).start()
            return carry

        lax.fori_loop(0, 5, near_step, 0)
        keep_own(phase)

    first_group = me // 4 + 4
    core = lax.rem(mine, 2)
    place = core * 4 + mine // 2

    spread = (
        lax.broadcasted_iota(jnp.int32, (128, CH), 0) // 8 == lax.broadcasted_iota(jnp.int32, (128, CH), 1)
    ).astype(F32)
    same_row = (
        lax.broadcasted_iota(jnp.int32, (128, 128), 0) % 8 == lax.broadcasted_iota(jnp.int32, (128, 128), 1) % 8
    )

    first_table.wait()

    def forward_step(c, carry):
        x_copy(c).wait()
        for x in range(XP):
            analyse_y(cat([xv[2 * c, x], xv[2 * c + 1, x]], 1), ty_stack, store, x * CH + 2 * c)
        return carry

    lax.fori_loop(0, CH // 2, forward_step, 0)
    pl.semaphore_wait(barrier, SLAB - 1 + DP - 1)
    analyse_z(store, tz_plain, sbuf, 0, first_group, send_one(0))

    pw_copy.wait()
    wide = jnp.dot(spread, pw[...], precision=lax.Precision.HIGHEST, preferred_element_type=F32)
    wide = lax.dot_general(
        wide, spread, (((1,), (1,)), ((), ())), precision=lax.Precision.HIGHEST, preferred_element_type=F32
    )
    wide = jnp.where(same_row, wide, 0.0)
    for kron, value in ((kron1, wide.T), (kron2, wide)):
        high, low = split(value)
        kron[...] = cat([cat([high, high], 1), cat([low, jnp.zeros_like(low)], 1)], 0)

    w_copy.wait()

    def regroup_step(c, carry):
        base = pl.multiple_of(c * 96, 16)
        for ri in range(2):
            for t in range(3):
                wco[pl.ds(base + 48 * ri + 16 * t, 16), :] = wv[c, :, ri, 128 * t : 128 * t + 128]
        return carry

    lax.fori_loop(0, CH, regroup_step, 0)
    second_table.wait()
    slab_all(0).wait_recv()
    modes = analyse_x(rbuf, 0, rows_high, rows_low)
    vv[:48, :] = modes[:, :128]
    vv[48:, :] = modes[:, 128:]

    def spread_row(modes, c):
        return cat([jnp.broadcast_to(modes[pl.ds(16 * t + c, 1), :], (16, 128)) for t in range(3)], 0), cat(
            [jnp.broadcast_to(modes[pl.ds(48 + 16 * t + c, 1), :], (16, 128)) for t in range(3)], 0
        )

    def mode_step(c, carry):
        base = pl.multiple_of(c * 96, 16)
        wr, wi = wco[pl.ds(base, 48), :], wco[pl.ds(base + 48, 48), :]
        vr, vi = spread_row(vv, c)
        return carry[0] + (wr * vr - wi * vi), carry[1] + (wr * vi + wi * vr)

    no_modes = (jnp.zeros((48, 128), F32), jnp.zeros((48, 128), F32))
    mixed = cat(lax.fori_loop(0, CH, mode_step, no_modes), 1)

    def put_mixed(k, value):
        sbuf[1, :, k, :] = value

    synthesise_x(mixed, columns_high, columns_low, put_mixed)
    send_all(1)

    def v_copy(d):
        return pltpu.make_async_remote_copy(
            src_ref=vsend.at[pl.ds(pl.multiple_of(16 * d, 16), 16)],
            dst_ref=vrecv.at[pl.ds(pl.multiple_of(16 * place, 16), 16)],
            send_sem=vssem,
            recv_sem=vrsem,
            device_id={"dp": d},
            device_id_type=MESH,
        )

    vsend[...] = jnp.zeros_like(vsend)
    for d in range(DP):
        for c in range(2):
            for t in range(3):
                row = 16 * t + 2 * d + c
                at = 16 * d + 6 * c + t
                vsend[at : at + 1, :] = vv[row : row + 1, :]
                vsend[at + 3 : at + 4, :] = vv[row + 48 : row + 49, :]

    def v_send(d, carry):
        v_copy(lax.rem(mine + d, DP)).start()
        return carry

    lax.fori_loop(1, DP, v_send, 0)
    vrecv[pl.ds(pl.multiple_of(16 * place, 16), 16), :] = vsend[pl.ds(pl.multiple_of(16 * mine, 16), 16), :]

    def turn_step(o, carry):
        base = pl.multiple_of(o * 96, 16)
        for part in range(6):
            woc[pl.ds(base + 16 * part, 16), :] = wco[pl.ds(16 * part + o, 16, stride=96), :]
        return carry

    lax.fori_loop(0, CH, turn_step, 0)

    def mix_step(yg, carry):
        y0 = pl.multiple_of(yg * 16, 16)
        for x in range(XP):
            high, low = split(rows_of(xv, x, y0))
            mix_channels(kron1, cat([high, low], 0), bv, x, y0)
        return carry

    lax.fori_loop(0, NY // 16, mix_step, 0)
    c_copy.wait()
    slab_all(1).wait_recv()

    synthesise_z(rbuf.at[1], zw_high, zw_low, held, store)

    def middle_step(o, carry):
        for x in range(XP):
            carried = synthesise_y(store, ty_inverse, x * CH + 2 * o)
            grads = []
            for each in range(2):
                before = carried[:, NZ * each : NZ * each + NZ] + bv[2 * o + each, x]
                slope = 0.5 * (1.0 + lax.erf(before * (1.0 / math.sqrt(2.0)))) + before * jnp.exp(
                    -0.5 * before * before
                ) * (1.0 / math.sqrt(2.0 * math.pi))
                grad = cv[2 * o + each, x] * slope
                cv[2 * o + each, x] = grad
                grads.append(grad)
            analyse_y(cat(grads, 1), ty_stack, store2, x * CH + 2 * o)
        return carry

    lax.fori_loop(0, CH // 2, middle_step, 0, unroll=2)
    analyse_z(store2, tz_weighted, sbuf, 2, first_group, send_one(2))

    pacc[...] = jnp.zeros_like(pacc)

    def pointwise_step(yg, carry):
        y0 = pl.multiple_of(yg * 16, 16)
        for x in range(XP):
            high, low = split(rows_of(cv, x, y0))
            xhigh, xlow = split(rows_of(xv, x, y0))
            pacc[...] += dot_t(cat([xhigh, xlow], 0), cat([high, low], 0))
        return carry

    lax.fori_loop(0, NY // 16, pointwise_step, 0)
    part = pacc[:128, :128] + pacc[:128, 128:] + pacc[128:, :128] + pacc[128:, 128:]
    part = jnp.where(same_row, part, 0.0)
    part = jnp.dot(part, spread, precision=lax.Precision.HIGHEST, preferred_element_type=F32)
    part = lax.dot_general(
        spread, part, (((0,), (0,)), ((), ())), precision=lax.Precision.HIGHEST, preferred_element_type=F32
    )
    flat = [cat([part[8 * r + i : 8 * r + i + 1, :] for i in range(8)], 1) for r in range(2)]
    part = cat(flat + [jnp.zeros((6, 128), F32)], 0)

    def p_copy(p):
        return pltpu.make_async_remote_copy(
            src_ref=psend,
            dst_ref=precv.at[pl.ds(pl.multiple_of(8 * me, 8), 8)],
            send_sem=pssem,
            recv_sem=prsem,
            device_id={"slab": p},
            device_id_type=MESH,
        )

    psend[...] = part

    def p_send(d, carry):
        p_copy(lax.rem(me + d, SLAB)).start()
        return carry

    lax.fori_loop(1, SLAB, p_send, 0)
    precv[pl.ds(pl.multiple_of(8 * me, 8), 8), :] = part

    slab_all(2).wait_recv()
    modes = analyse_x(rbuf, 2, rows_high, rows_low)
    gv[:48, :] = modes[:, :128]
    gv[48:, :] = modes[:, 128:]

    def g_copy(d):
        return pltpu.make_async_remote_copy(
            src_ref=gv,
            dst_ref=grecv.at[pl.ds(pl.multiple_of(96 * place, 16), 96)],
            send_sem=gssem,
            recv_sem=grsem,
            device_id={"dp": lax.rem(mine + 2 * d, DP)},
            device_id_type=MESH,
        )

    for d in range(1, 4):
        g_copy(d).start()
    grecv[pl.ds(pl.multiple_of(96 * place, 16), 96), :] = gv[...]

    def back_mode_step(o, carry):
        base = pl.multiple_of(o * 96, 16)
        wr, wi = woc[pl.ds(base, 48), :], woc[pl.ds(base + 48, 48), :]
        gr, gi = spread_row(gv, o)
        return carry[0] + (wr * gr + wi * gi), carry[1] + (wr * gi - wi * gr)

    back = cat(lax.fori_loop(0, CH, back_mode_step, no_modes), 1)

    def put_back(k, value):
        sbuf[3, :, k, :] = value

    def dp_all(source, target, size, send_sem, recv_sem):
        return pltpu.make_async_remote_copy(
            src_ref=source.at[pl.ds(0, size)],
            dst_ref=target.at[pl.ds(0, size)],
            send_sem=send_sem,
            recv_sem=recv_sem,
            device_id={"dp": lax.rem(mine + 1, DP)},
            device_id_type=MESH,
        )

    v_all = dp_all(vrecv, vrecv, 16 * (DP - 1), vssem, vrsem)
    g_all = dp_all(grecv, grecv, 96 * 3, gssem, grsem)
    synthesise_x(back, columns_high, columns_low, put_back)
    send_all(3)

    p_all = pltpu.make_async_remote_copy(
        src_ref=precv.at[pl.ds(0, 8 * (SLAB - 1))],
        dst_ref=precv.at[pl.ds(0, 8 * (SLAB - 1))],
        send_sem=pssem,
        recv_sem=prsem,
        device_id={"slab": lax.rem(me + 1, SLAB)},
        device_id_type=MESH,
    )
    p_all.wait_recv()
    total = precv[0:8, :]
    for p in range(1, SLAB):
        total = total + precv[8 * p : 8 * p + 8, :]
    qsend[...] = total

    def q_copy(d):
        return pltpu.make_async_remote_copy(
            src_ref=qsend,
            dst_ref=qrecv.at[pl.ds(pl.multiple_of(8 * mine, 8), 8)],
            send_sem=qssem,
            recv_sem=qrsem,
            device_id={"dp": d},
            device_id_type=MESH,
        )

    def q_send(d, carry):
        q_copy(lax.rem(mine + d, DP)).start()
        return carry

    lax.fori_loop(1, DP, q_send, 0)
    qrecv[pl.ds(pl.multiple_of(8 * mine, 8), 8), :] = total
    q_all = dp_all(qrecv, qrecv, 8 * (DP - 1), qssem, qrsem)
    v_all.wait_recv()
    g_all.wait_recv()
    half = pl.ds(pl.multiple_of(core * 384, 16), 384)
    h_copy = pltpu.make_async_remote_copy(
        src_ref=grecv.at[half],
        dst_ref=grecv.at[half],
        send_sem=hssem,
        recv_sem=hrsem,
        device_id={"dp": mine + 1 - 2 * core},
        device_id_type=MESH,
    )
    h_copy.start()

    def back_step(yg, carry):
        y0 = pl.multiple_of(yg * 16, 16)
        for x in range(XP):
            high, low = split(rows_of(cv, x, y0))
            mix_channels(kron2, cat([high, low], 0), bv, x, y0)
        return carry

    lax.fori_loop(0, NY // 16, back_step, 0)
    o_copy = pltpu.make_async_copy(bv, mixed_hbm, osem)
    o_copy.start()
    slab_all(3).wait_recv()
    last_ref[...] = rbuf[3]
    h_copy.wait()

    for c in range(2):
        def sample_step(d, carry):
            out = []
            base = pl.multiple_of(96 * d, 16)
            for t in range(3):
                vr = vrecv[pl.ds(16 * d + 6 * c + t, 1), :]
                vi = vrecv[pl.ds(16 * d + 6 * c + 3 + t, 1), :]
                gr = grecv[pl.ds(base + 16 * t, 16), :]
                gi = grecv[pl.ds(base + 48 + 16 * t, 16), :]
                out.append(carry[2 * t] + (gr * vr + gi * vi))
                out.append(carry[2 * t + 1] + (gi * vr - gr * vi))
            return tuple(out)

        total = lax.fori_loop(0, DP, sample_step, tuple(jnp.zeros((CH, 128), F32) for _ in range(6)))
        for t in range(3):
            gs_ref[c, :, 0, 128 * t : 128 * t + 128] = total[2 * t]
            gs_ref[c, :, 1, 128 * t : 128 * t + 128] = total[2 * t + 1]

    for phase in range(4):
        slab_all(phase).wait_send()
    p_all.wait_send()
    q_all.wait_recv()
    total = qrecv[0:8, :]
    for d in range(1, DP):
        total = total + qrecv[8 * d : 8 * d + 8, :]
    gp_ref[...] = total
    q_all.wait_send()
    v_all.wait_send()
    g_all.wait_send()
    o_copy.wait()


def last_kernel(
    rows_hbm, mixed_hbm, gs_in, gp_in, table_hbm, gi_hbm, gs_hbm, gp_hbm,
    rows_ref, gs_ref, bv, table, held, store, gp, insem, tsem, osem, gssem, gpsem, rsem,
):
    rows_copy = pltpu.make_async_copy(rows_hbm, rows_ref, rsem)
    rows_copy.start()
    table_copy = pltpu.make_async_copy(table_hbm, table, tsem)
    table_copy.start()

    def in_copy(c):
        return pltpu.make_async_copy(mixed_hbm.at[pl.ds(2 * c, 2)], bv.at[pl.ds(2 * c, 2)], insem.at[c])

    def out_copy(c):
        return pltpu.make_async_copy(bv.at[pl.ds(2 * c, 2)], gi_hbm.at[pl.ds(2 * c, 2)], osem.at[c])

    for c in range(CH // 2):
        in_copy(c).start()
    gs_load = pltpu.make_async_copy(gs_in, gs_ref, gssem)
    gs_load.start()
    rows_copy.wait()
    for r in range(2):
        flat = gp_in[r : r + 1, :]
        for i in range(8):
            gp[8 * r + i : 8 * r + i + 1, :] = flat[:, CH * i : CH * i + CH] * (1.0 / math.sqrt(DP * NX * NY * NZ))
    gp_copy = pltpu.make_async_copy(gp, gp_hbm, gpsem)
    gp_copy.start()
    table_copy.wait()
    ty_inverse = table.at[pl.ds(0, 128)]
    synthesise_z(rows_ref, table.at[pl.ds(128, 480)], table.at[pl.ds(608, 480)], held, store)

    def last_step(c, carry):
        in_copy(c).wait()
        for x in range(XP):
            out = synthesise_y(store, ty_inverse, x * CH + 2 * c)
            bv[2 * c, x] = bv[2 * c, x] + out[:, :NZ]
            bv[2 * c + 1, x] = bv[2 * c + 1, x] + out[:, NZ:]
        out_copy(c).start()
        return carry

    gs_load.wait()
    gs_copy = pltpu.make_async_copy(gs_ref, gs_hbm, gssem)
    gs_copy.start()
    lax.fori_loop(0, CH // 2, last_step, 0)
    gs_copy.wait()
    gp_copy.wait()
    for c in range(CH // 2):
        out_copy(c).wait()


def body(inputs, cotangent, spectral_weights, pointwise_weights):
    main_table, last_table = (jnp.asarray(table) for table in tables())
    hbm = pl.BlockSpec(memory_space=pltpu.HBM)
    vmem = pl.BlockSpec(memory_space=pltpu.VMEM)
    block = (CH, XP, NY, NZ)
    dma = pltpu.SemaphoreType.DMA
    block_shape = jax.ShapeDtypeStruct(block, F32)
    weight_shape = jax.ShapeDtypeStruct((2, CH, 2, KX * KZ), F32)
    store_shape = pltpu.VMEM((CH * XP * PITCH, NZ), F32)
    rows, mixed, weight_part, point_part = pl.pallas_call(
        kernel,
        out_shape=[
            jax.ShapeDtypeStruct((SLAB, KZ, 128), F32),
            block_shape,
            weight_shape,
            jax.ShapeDtypeStruct((8, 128), F32),
        ],
        in_specs=[hbm] * 5,
        out_specs=[vmem, hbm, vmem, vmem],
        scratch_shapes=[
            pltpu.VMEM(block, F32),
            pltpu.VMEM(block, F32),
            pltpu.VMEM(block, F32),
            pltpu.VMEM((CH, CH, 2, KX * KZ), F32),
            pltpu.VMEM((CH * 96, 128), F32),
            pltpu.VMEM((CH * 96, 128), F32),
            pltpu.VMEM((CH, CH), F32),
            pltpu.VMEM((TABLE, 256), BF16),
            store_shape,
            store_shape,
            pltpu.VMEM((512, 256), BF16),
            pltpu.VMEM((4, SLAB, KZ, 128), F32),
            pltpu.VMEM((4, SLAB, KZ, 128), F32),
            pltpu.VMEM((96, 128), F32),
            pltpu.VMEM((96, 128), F32),
            pltpu.VMEM((256, 256), BF16),
            pltpu.VMEM((256, 256), BF16),
            pltpu.VMEM((256, 256), F32),
            pltpu.VMEM((16 * DP, 128), F32),
            pltpu.VMEM((16 * DP, 128), F32),
            pltpu.VMEM((96 * DP, 128), F32),
            pltpu.VMEM((8, 128), F32),
            pltpu.VMEM((8 * SLAB, 128), F32),
            pltpu.VMEM((8, 128), F32),
            pltpu.VMEM((8 * DP, 128), F32),
            dma((CH // 2,)),
            dma,
            dma,
            dma,
            dma((2,)),
            dma,
            dma((4,)),
            dma((4,)),
            dma,
            dma,
            dma,
            dma,
            dma,
            dma,
            dma,
            dma,
            dma,
            dma,
        ],
        compiler_params=pltpu.CompilerParams(
            collective_id=0, has_side_effects=True, vmem_limit_bytes=60 * 1024 * 1024
        ),
        name="layer_backward",
    )(inputs.reshape(block), cotangent.reshape(block), spectral_weights, pointwise_weights, main_table)
    grad_inputs, grad_spectral, grad_pointwise = pl.pallas_call(
        last_kernel,
        out_shape=[block_shape, weight_shape, jax.ShapeDtypeStruct((CH, CH), F32)],
        in_specs=[hbm, hbm, hbm, vmem, hbm],
        out_specs=[hbm, hbm, hbm],
        scratch_shapes=[
            pltpu.VMEM((SLAB, KZ, 128), F32),
            pltpu.VMEM((2, CH, 2, KX * KZ), F32),
            pltpu.VMEM(block, F32),
            pltpu.VMEM((LAST_TABLE, 256), BF16),
            pltpu.VMEM((512, 256), BF16),
            store_shape,
            pltpu.VMEM((CH, CH), F32),
            dma((CH // 2,)),
            dma,
            dma((CH // 2,)),
            dma,
            dma,
            dma,
        ],
        compiler_params=pltpu.CompilerParams(vmem_limit_bytes=60 * 1024 * 1024),
        name="input_gradient",
    )(rows, mixed, weight_part, point_part, last_table)
    return (grad_inputs[None], grad_spectral, grad_pointwise)


def solution(mesh):
    placed = (
        P("dp", None, "slab", None, None),
        P("dp", None, "slab", None, None),
        P(None, None, None, "slab"),
        P(),
    )
    return jax.shard_map(
        body,
        mesh=mesh,
        in_specs=placed,
        out_specs=(P("dp", None, "slab", None, None), P("dp", None, None, "slab"), P()),
        check_vma=False,
    )
```

```python
import functools
import math

import jax
import jax.numpy as jnp
import ml_dtypes
import numpy as np
from jax import lax
from jax.experimental import pallas as pl
from jax.experimental.pallas import tpu as pltpu
from jax.sharding import PartitionSpec as P

CH = 16
XP = 4
NX = 128
NY = 128
NZ = 128
KX = 32
KY = 32
KZ = 12
SLAB = 32
DP = 8
ROWS = 16
PITCH = 72
F32 = jnp.float32
BF16 = jnp.bfloat16
MESH = pl.DeviceIdType.MESH
NORM = 1.0 / math.sqrt(NX * NY * NZ)


def halves(table):
    table = np.asarray(table, np.float64)
    high = table.astype(ml_dtypes.bfloat16)
    low = (table - high.astype(np.float64)).astype(ml_dtypes.bfloat16)
    return high, low


def angles(length, orders):
    places = np.arange(length)[:, None]
    return ((places * orders[None, :]) % length) * (2.0 * math.pi / length)


@functools.cache
def tables():
    centred = np.arange(KY)
    centred = np.where(centred < KY // 2, centred, centred - KY)
    second = angles(NY, centred)
    third = angles(NZ, np.arange(KZ))
    first = angles(NX, centred)
    ty = np.concatenate([np.cos(second).T, -np.sin(second).T], axis=0)
    ty_high, ty_low = halves(ty)
    ty_stack = np.concatenate(
        [np.concatenate([ty_high, ty_high], axis=1), np.concatenate([ty_low, np.zeros_like(ty_low)], axis=1)], axis=0
    )
    ty_inverse = np.concatenate([ty_high.T, ty_high.T, ty_low.T], axis=1)
    depth = {}
    for name, weights in (("plain", np.ones(KZ)), ("weighted", np.where(np.arange(KZ) == 0, 1.0, 2.0))):
        cosine = (np.cos(third) * weights[None, :]).T
        sine = (np.sin(third) * weights[None, :]).T
        real_row = np.concatenate([cosine, sine], axis=1)
        imag_row = np.concatenate([-sine, cosine], axis=1)
        analysis = np.zeros((2 * ROWS, 2 * NZ))
        analysis[:KZ] = real_row
        analysis[ROWS : ROWS + KZ] = imag_row
        synthesis = np.zeros((2, 15 * ROWS, 2 * NZ))
        synthesis[0, 7 * ROWS : 7 * ROWS + KZ] = real_row
        synthesis[1, 7 * ROWS : 7 * ROWS + KZ] = imag_row
        depth[name] = (np.concatenate(halves(analysis), axis=0),) + halves(synthesis)
    place = first.reshape(SLAB, XP, KX)
    cosine = np.cos(place).transpose(1, 0, 2) * NORM
    sine = np.sin(place).transpose(1, 0, 2) * NORM
    rows = np.zeros((2, XP, 4, SLAB, 2, 4, KX))
    for group in range(4):
        rows[0, :, group, :, 0, group] = cosine
        rows[1, :, group, :, 0, group] = sine
        rows[0, :, group, :, 1, group] = -sine
        rows[1, :, group, :, 1, group] = cosine
    rows = rows.reshape(2 * XP * 4 * SLAB, 2 * 4 * KX)
    ty_inverse = np.concatenate([ty_inverse, np.zeros_like(ty_inverse[:, :64])], axis=1)
    flat = {}
    for name, (analysis, high, low) in depth.items():
        flat[name] = (analysis, high.reshape(-1, 2 * NZ), low.reshape(-1, 2 * NZ))
    columns = rows.T.reshape(256, 4, 256).transpose(1, 0, 2).reshape(1024, 256)
    first_part = (ty_stack, flat["plain"][0]) + halves(rows) + halves(columns) + (ty_inverse,) + flat["weighted"]
    return np.concatenate(first_part, axis=0), np.concatenate((ty_inverse,) + flat["plain"][1:], axis=0)


TY = 0
TZP = 128
XH = 192
XL = XH + 1024
IH = XL + 1024
IL = IH + 1024
TYI = IL + 1024
TZW = TYI + 128
ZWH = TZW + 64
ZWL = ZWH + 480
TABLE = ZWL + 480
LAST_TABLE = 128 + 960


def each_channel(step, carry):
    for c in range(CH):
        carry = step(c, carry)
    return carry


def split(value):
    high = value.astype(BF16)
    low = (value - high.astype(F32)).astype(BF16)
    return high, low


def dot(left, right):
    return jnp.dot(left, right, preferred_element_type=F32)


def dot_t(left, right):
    return lax.dot_general(left, right, (((1,), (1,)), ((), ())), preferred_element_type=F32)


def cat(pieces, axis):
    return jnp.concatenate(pieces, axis=axis)


def analyse_y(pair, ty_stack, store, group):
    high, low = split(pair)
    out = dot(ty_stack[...], cat([high, low], 0))
    out = out[:64] + out[64:]
    store[pl.ds(pl.multiple_of(group * PITCH, 8), 64), :] = out[:, :NZ]
    store[pl.ds(pl.multiple_of((group + 1) * PITCH, 8), 64), :] = out[:, NZ:]


def analyse_z(store, tz_stack, sbuf, phase, first_group, send, send_own):
    lanes = lax.broadcasted_iota(jnp.int32, (ROWS, 128), 1) < 64

    def analyse(group):
        pieces = []
        for each in range(4):
            j = group * 4 + each
            pieces.append(cat([store[pl.ds(j, 64, stride=PITCH), :], store[pl.ds(KY + j, 64, stride=PITCH), :]], 1))
        high, low = split(cat(pieces, 0))
        out = dot_t(tz_stack[...], high)
        out = out[:32] + out[32:] + dot_t(tz_stack[:32, :], low)
        for each in range(2):
            tile = out[:, 128 * each : 128 * each + 128]
            real, imag = tile[:ROWS], tile[ROWS:]
            first = jnp.where(lanes, real, pltpu.roll(imag, 64, axis=1))
            second = jnp.where(lanes, pltpu.roll(real, 64, axis=1), imag)
            sbuf[phase, group * 4 + 2 * each] = first[:KZ]
            sbuf[phase, group * 4 + 2 * each + 1] = second[:KZ]

    def step(turn, carry):
        group = lax.rem(first_group + turn, KY // 4)
        analyse(group)
        for each in range(4):
            send(group * 4 + each)
        return carry

    lax.fori_loop(0, 4, step, 0, unroll=4)
    analyse(lax.rem(first_group + 4, KY // 4))
    send_own()
    lax.fori_loop(5, KY // 4, step, 0, unroll=3)


def analyse_x(rbuf, phase, rows_high, rows_low):
    parts = []
    for t in range(3):
        block = cat([rbuf[phase, :, 4 * t + k, :] for k in range(4)], 0).T
        parts.append(cat([block[16 * q : 16 * q + 16] for q in range(8)], 1))
    high, low = split(cat(parts, 0))
    out = dot(cat([high, low], 0), rows_high[...])
    return out[:48] + out[48:] + dot(high, rows_low[...])


def synthesise_x(modes, columns_high, columns_low, put):
    high, low = split(modes)
    both = cat([high, low], 0)
    tiles = []
    for n in range(4):
        out = dot(both, columns_high[pl.ds(256 * n, 256), :])
        tiles.append(out[:48] + out[48:] + dot(high, columns_low[pl.ds(256 * n, 256), :]))
    out = cat(tiles, 1)
    for t in range(3):
        part = out[16 * t : 16 * t + 16]
        block = cat([part[:, 128 * q : 128 * q + 128] for q in range(8)], 0).T
        for k in range(4):
            put(4 * t + k, block[SLAB * k : SLAB * k + SLAB])


def synthesise_z(rbuf, zi_high, zi_low, held, store):
    spare = jnp.zeros((ROWS - KZ, 128), F32)
    for g in range(4):
        pieces = []
        for each in range(8):
            pieces += [rbuf[8 * g + each], spare]
        block = cat(pieces, 0).T
        high, low = split(cat([block[:64], block[64:]], 1))
        held[pl.ds(64 * g, 64), :] = high
        held[pl.ds(256 + 64 * g, 64), :] = low

    def step(jj, carry):
        at = pl.multiple_of(7 * ROWS - ROWS * jj, ROWS)
        table_high = cat([zi_high[pl.ds(at, 128), :], zi_high[pl.ds(at + 240, 128), :]], 0)
        table_low = cat([zi_low[pl.ds(at, 128), :], zi_low[pl.ds(at + 240, 128), :]], 0)
        out = dot(held[...], table_high)
        out = out[:256] + out[256:] + dot(held[:256, :], table_low)
        for g in range(4):
            store[pl.ds(8 * g + jj, 64, stride=PITCH), :] = out[64 * g : 64 * g + 64, :NZ]
            store[pl.ds(KY + 8 * g + jj, 64, stride=PITCH), :] = out[64 * g : 64 * g + 64, NZ:]
        return carry

    lax.fori_loop(0, 8, step, 0, unroll=8)


def synthesise_y(store, ty_inverse, group):
    pair = cat(
        [
            store[pl.ds(pl.multiple_of(group * PITCH, 8), 64), :],
            store[pl.ds(pl.multiple_of((group + 1) * PITCH, 8), 64), :],
        ],
        1,
    )
    high, low = split(pair)
    return dot(ty_inverse[:, :192], cat([high, low, high], 0))


def rows_of(source, x, y0):
    left = cat([source[c, x, pl.ds(y0, 8), :] for c in range(CH)], 0)
    right = cat([source[c, x, pl.ds(y0 + 8, 8), :] for c in range(CH)], 0)
    return cat([left, right], 1)


def mix_channels(kron, halves_stack, target, x, y0):
    out = dot(kron[...], halves_stack)
    out = out[:128] + out[128:]
    for c in range(CH):
        target[c, x, pl.ds(y0, 8), :] = out[8 * c : 8 * c + 8, :NZ]
        target[c, x, pl.ds(y0 + 8, 8), :] = out[8 * c : 8 * c + 8, NZ:]


def kernel(
    x_hbm, cot_hbm, w_hbm, pw_hbm, table_hbm,
    last_ref, mixed_hbm, gs_ref, gp_ref,
    xv, cv, bv, wv, wco, woc, pw, table, store, store2, held, sbuf, rbuf, vv, gv, kron1, kron2, pacc,
    vsend, vrecv, grecv, psend, precv, qsend, qrecv,
    xsem, csem, wsem, pwsem, tsem, osem, ssem, rsem, vssem, vrsem, gssem, grsem, hssem, hrsem, pssem, prsem, qssem, qrsem,
):
    me = lax.axis_index("slab")
    mine = lax.axis_index("dp")

    def x_copy(c):
        return pltpu.make_async_copy(x_hbm.at[pl.ds(2 * c, 2)], xv.at[pl.ds(2 * c, 2)], xsem.at[c])

    def table_copy(index, start, size):
        return pltpu.make_async_copy(
            table_hbm.at[pl.ds(start, size)], table.at[pl.ds(start, size)], tsem.at[index]
        )

    first_table = table_copy(0, 0, XH)
    first_table.start()
    for c in range(CH // 2):
        x_copy(c).start()
    pw_copy = pltpu.make_async_copy(pw_hbm, pw, pwsem)
    pw_copy.start()
    second_table = table_copy(1, XH, TABLE - XH)
    second_table.start()
    w_copy = pltpu.make_async_copy(w_hbm, wv, wsem)
    w_copy.start()
    c_copy = pltpu.make_async_copy(cot_hbm, cv, csem)
    c_copy.start()

    barrier = pltpu.get_barrier_semaphore()

    def greet_slab(d, carry):
        pl.semaphore_signal(barrier, inc=1, device_id={"slab": lax.rem(me + d, SLAB)}, device_id_type=MESH)
        return carry

    def greet_dp(d, carry):
        pl.semaphore_signal(barrier, inc=1, device_id={"dp": lax.rem(mine + d, DP)}, device_id_type=MESH)
        return carry

    lax.fori_loop(1, SLAB, greet_slab, 0)
    lax.fori_loop(1, DP, greet_dp, 0)

    ty_stack = table.at[pl.ds(TY, 128)]
    tz_plain = table.at[pl.ds(TZP, 64)]
    rows_high = table.at[pl.ds(XH, 1024)]
    rows_low = table.at[pl.ds(XL, 1024)]
    columns_high = table.at[pl.ds(IH, 1024)]
    columns_low = table.at[pl.ds(IL, 1024)]
    ty_inverse = table.at[pl.ds(TYI, 128)]
    tz_weighted = table.at[pl.ds(TZW, 64)]
    zw_high = table.at[pl.ds(ZWH, 480)]
    zw_low = table.at[pl.ds(ZWL, 480)]

    def slab_copy(phase, p):
        return pltpu.make_async_remote_copy(
            src_ref=sbuf.at[phase, p],
            dst_ref=rbuf.at[phase, me],
            send_sem=ssem.at[phase],
            recv_sem=rsem.at[phase],
            device_id={"slab": p},
            device_id_type=MESH,
        )

    def slab_all(phase):
        every = pl.ds(0, SLAB - 1)
        return pltpu.make_async_remote_copy(
            src_ref=sbuf.at[phase, every],
            dst_ref=rbuf.at[phase, every],
            send_sem=ssem.at[phase],
            recv_sem=rsem.at[phase],
            device_id={"slab": lax.rem(me + 1, SLAB)},
            device_id_type=MESH,
        )

    def keep_own(phase):
        rbuf[phase, me] = sbuf[phase, me]

    def send_one(phase):
        def send(p):
            slab_copy(phase, p).start()

        return send

    def send_group(phase):
        def send():
            for d in range(1, 4):
                slab_copy(phase, me // 4 * 4 + lax.rem(me + d, 4)).start()
            keep_own(phase)

        return send

    def send_all(phase):
        def step(turn, carry):
            for each in range(4):
                slab_copy(phase, lax.rem(me + 16 + 4 * turn + each, SLAB)).start()
            return carry

        lax.fori_loop(0, 4, step, 0)

        def near_step(turn, carry):
            for each in range(3):
                slab_copy(phase, lax.rem(me + 1 + 3 * turn + each, SLAB)).start()
            return carry

        lax.fori_loop(0, 5, near_step, 0)
        keep_own(phase)

    first_group = me // 4 + 4
    core = lax.rem(mine, 2)
    place = core * 4 + mine // 2

    spread = (
        lax.broadcasted_iota(jnp.int32, (128, CH), 0) // 8 == lax.broadcasted_iota(jnp.int32, (128, CH), 1)
    ).astype(F32)
    same_row = (
        lax.broadcasted_iota(jnp.int32, (128, 128), 0) % 8 == lax.broadcasted_iota(jnp.int32, (128, 128), 1) % 8
    )

    first_table.wait()

    def forward_step(c, carry):
        x_copy(c).wait()
        for x in range(XP):
            analyse_y(cat([xv[2 * c, x], xv[2 * c + 1, x]], 1), ty_stack, store, x * CH + 2 * c)
        return carry

    lax.fori_loop(0, CH // 2, forward_step, 0)
    pl.semaphore_wait(barrier, SLAB - 1 + DP - 1)
    analyse_z(store, tz_plain, sbuf, 0, first_group, send_one(0), send_group(0))

    pw_copy.wait()
    wide = jnp.dot(spread, pw[...], precision=lax.Precision.HIGHEST, preferred_element_type=F32)
    wide = lax.dot_general(
        wide, spread, (((1,), (1,)), ((), ())), precision=lax.Precision.HIGHEST, preferred_element_type=F32
    )
    wide = jnp.where(same_row, wide, 0.0)
    for kron, value in ((kron1, wide.T), (kron2, wide)):
        high, low = split(value)
        kron[...] = cat([cat([high, high], 1), cat([low, jnp.zeros_like(low)], 1)], 0)

    w_copy.wait()

    def regroup_step(c, carry):
        base = pl.multiple_of(c * 96, 16)
        for ri in range(2):
            for t in range(3):
                wco[pl.ds(base + 48 * ri + 16 * t, 16), :] = wv[c, :, ri, 128 * t : 128 * t + 128]
        return carry

    lax.fori_loop(0, CH, regroup_step, 0)
    second_table.wait()
    slab_all(0).wait_recv()
    modes = analyse_x(rbuf, 0, rows_high, rows_low)
    vv[:48, :] = modes[:, :128]
    vv[48:, :] = modes[:, 128:]

    def spread_row(modes, c):
        return cat([jnp.broadcast_to(modes[pl.ds(16 * t + c, 1), :], (16, 128)) for t in range(3)], 0), cat(
            [jnp.broadcast_to(modes[pl.ds(48 + 16 * t + c, 1), :], (16, 128)) for t in range(3)], 0
        )

    def mode_step(c, carry):
        base = c * 96
        wr, wi = wco[pl.ds(base, 48), :], wco[pl.ds(base + 48, 48), :]
        vr, vi = spread_row(vv, c)
        return carry[0] + (wr * vr - wi * vi), carry[1] + (wr * vi + wi * vr)

    no_modes = (jnp.zeros((48, 128), F32), jnp.zeros((48, 128), F32))
    mixed = cat(each_channel(mode_step, no_modes), 1)

    def put_mixed(k, value):
        sbuf[1, :, k, :] = value

    synthesise_x(mixed, columns_high, columns_low, put_mixed)
    send_all(1)

    def v_copy(d):
        return pltpu.make_async_remote_copy(
            src_ref=vsend.at[pl.ds(pl.multiple_of(16 * d, 16), 16)],
            dst_ref=vrecv.at[pl.ds(pl.multiple_of(16 * place, 16), 16)],
            send_sem=vssem,
            recv_sem=vrsem,
            device_id={"dp": d},
            device_id_type=MESH,
        )

    vsend[...] = jnp.zeros_like(vsend)
    for d in range(DP):
        for c in range(2):
            for t in range(3):
                row = 16 * t + 2 * d + c
                at = 16 * d + 6 * c + t
                vsend[at : at + 1, :] = vv[row : row + 1, :]
                vsend[at + 3 : at + 4, :] = vv[row + 48 : row + 49, :]

    def v_send(d, carry):
        v_copy(lax.rem(mine + d, DP)).start()
        return carry

    lax.fori_loop(1, DP, v_send, 0)
    vrecv[pl.ds(pl.multiple_of(16 * place, 16), 16), :] = vsend[pl.ds(pl.multiple_of(16 * mine, 16), 16), :]

    def turn_step(o, carry):
        base = pl.multiple_of(o * 96, 16)
        for part in range(6):
            woc[pl.ds(base + 16 * part, 16), :] = wco[pl.ds(16 * part + o, 16, stride=96), :]
        return carry

    lax.fori_loop(0, CH, turn_step, 0)

    def mix_step(yg, carry):
        y0 = pl.multiple_of(yg * 16, 16)
        for x in range(XP):
            high, low = split(rows_of(xv, x, y0))
            mix_channels(kron1, cat([high, low], 0), bv, x, y0)
        return carry

    lax.fori_loop(0, NY // 16, mix_step, 0)
    c_copy.wait()
    slab_all(1).wait_recv()

    synthesise_z(rbuf.at[1], zw_high, zw_low, held, store)

    def middle_step(o, carry):
        for x in range(XP):
            carried = synthesise_y(store, ty_inverse, x * CH + 2 * o)
            grads = []
            for each in range(2):
                before = carried[:, NZ * each : NZ * each + NZ] + bv[2 * o + each, x]
                slope = 0.5 * (1.0 + lax.erf(before * (1.0 / math.sqrt(2.0)))) + before * jnp.exp(
                    -0.5 * before * before
                ) * (1.0 / math.sqrt(2.0 * math.pi))
                grad = cv[2 * o + each, x] * slope
                cv[2 * o + each, x] = grad
                grads.append(grad)
            analyse_y(cat(grads, 1), ty_stack, store2, x * CH + 2 * o)
        return carry

    lax.fori_loop(0, CH // 2, middle_step, 0, unroll=4)
    analyse_z(store2, tz_weighted, sbuf, 2, first_group, send_one(2), send_group(2))

    pacc[...] = jnp.zeros_like(pacc)

    def pointwise_step(yg, carry):
        y0 = pl.multiple_of(yg * 16, 16)
        for x in range(XP):
            high, low = split(rows_of(cv, x, y0))
            xhigh, xlow = split(rows_of(xv, x, y0))
            pacc[...] += dot_t(cat([xhigh, xlow], 0), cat([high, low], 0))
        return carry

    lax.fori_loop(0, NY // 16, pointwise_step, 0)
    part = pacc[:128, :128] + pacc[:128, 128:] + pacc[128:, :128] + pacc[128:, 128:]
    part = jnp.where(same_row, part, 0.0)
    part = jnp.dot(part, spread, precision=lax.Precision.HIGHEST, preferred_element_type=F32)
    part = lax.dot_general(
        spread, part, (((0,), (0,)), ((), ())), precision=lax.Precision.HIGHEST, preferred_element_type=F32
    )
    flat = [cat([part[8 * r + i : 8 * r + i + 1, :] for i in range(8)], 1) for r in range(2)]
    part = cat(flat + [jnp.zeros((6, 128), F32)], 0)

    def p_copy(p):
        return pltpu.make_async_remote_copy(
            src_ref=psend,
            dst_ref=precv.at[pl.ds(pl.multiple_of(8 * me, 8), 8)],
            send_sem=pssem,
            recv_sem=prsem,
            device_id={"slab": p},
            device_id_type=MESH,
        )

    psend[...] = part

    def p_send(d, carry):
        p_copy(lax.rem(me + d, SLAB)).start()
        return carry

    lax.fori_loop(1, SLAB, p_send, 0)
    precv[pl.ds(pl.multiple_of(8 * me, 8), 8), :] = part

    slab_all(2).wait_recv()
    modes = analyse_x(rbuf, 2, rows_high, rows_low)
    gv[:48, :] = modes[:, :128]
    gv[48:, :] = modes[:, 128:]

    def g_copy(d):
        return pltpu.make_async_remote_copy(
            src_ref=gv,
            dst_ref=grecv.at[pl.ds(pl.multiple_of(96 * place, 16), 96)],
            send_sem=gssem,
            recv_sem=grsem,
            device_id={"dp": lax.rem(mine + 2 * d, DP)},
            device_id_type=MESH,
        )

    for d in range(1, 4):
        g_copy(d).start()
    grecv[pl.ds(pl.multiple_of(96 * place, 16), 96), :] = gv[...]

    def back_mode_step(o, carry):
        base = o * 96
        wr, wi = woc[pl.ds(base, 48), :], woc[pl.ds(base + 48, 48), :]
        gr, gi = spread_row(gv, o)
        return carry[0] + (wr * gr + wi * gi), carry[1] + (wr * gi - wi * gr)

    back = cat(each_channel(back_mode_step, no_modes), 1)

    def put_back(k, value):
        sbuf[3, :, k, :] = value

    def dp_all(source, target, size, send_sem, recv_sem):
        return pltpu.make_async_remote_copy(
            src_ref=source.at[pl.ds(0, size)],
            dst_ref=target.at[pl.ds(0, size)],
            send_sem=send_sem,
            recv_sem=recv_sem,
            device_id={"dp": lax.rem(mine + 1, DP)},
            device_id_type=MESH,
        )

    v_all = dp_all(vrecv, vrecv, 16 * (DP - 1), vssem, vrsem)
    g_all = dp_all(grecv, grecv, 96 * 3, gssem, grsem)
    synthesise_x(back, columns_high, columns_low, put_back)
    send_all(3)

    p_all = pltpu.make_async_remote_copy(
        src_ref=precv.at[pl.ds(0, 8 * (SLAB - 1))],
        dst_ref=precv.at[pl.ds(0, 8 * (SLAB - 1))],
        send_sem=pssem,
        recv_sem=prsem,
        device_id={"slab": lax.rem(me + 1, SLAB)},
        device_id_type=MESH,
    )
    p_all.wait_recv()
    total = precv[0:8, :]
    for p in range(1, SLAB):
        total = total + precv[8 * p : 8 * p + 8, :]
    qsend[...] = total

    def q_copy(d):
        return pltpu.make_async_remote_copy(
            src_ref=qsend,
            dst_ref=qrecv.at[pl.ds(pl.multiple_of(8 * mine, 8), 8)],
            send_sem=qssem,
            recv_sem=qrsem,
            device_id={"dp": d},
            device_id_type=MESH,
        )

    def q_send(d, carry):
        q_copy(lax.rem(mine + d, DP)).start()
        return carry

    lax.fori_loop(1, DP, q_send, 0)
    qrecv[pl.ds(pl.multiple_of(8 * mine, 8), 8), :] = total
    q_all = dp_all(qrecv, qrecv, 8 * (DP - 1), qssem, qrsem)
    v_all.wait_recv()
    g_all.wait_recv()
    half = pl.ds(pl.multiple_of(core * 384, 16), 384)
    h_copy = pltpu.make_async_remote_copy(
        src_ref=grecv.at[half],
        dst_ref=grecv.at[half],
        send_sem=hssem,
        recv_sem=hrsem,
        device_id={"dp": mine + 1 - 2 * core},
        device_id_type=MESH,
    )
    h_copy.start()

    def back_step(yg, carry):
        y0 = pl.multiple_of(yg * 16, 16)
        for x in range(XP):
            high, low = split(rows_of(cv, x, y0))
            mix_channels(kron2, cat([high, low], 0), bv, x, y0)
        return carry

    lax.fori_loop(0, NY // 16, back_step, 0)
    o_copy = pltpu.make_async_copy(bv, mixed_hbm, osem)
    o_copy.start()
    slab_all(3).wait_recv()
    last_ref[...] = rbuf[3]
    h_copy.wait()

    for c in range(2):
        def sample_step(d, carry):
            out = []
            base = pl.multiple_of(96 * d, 16)
            for t in range(3):
                vr = vrecv[pl.ds(16 * d + 6 * c + t, 1), :]
                vi = vrecv[pl.ds(16 * d + 6 * c + 3 + t, 1), :]
                gr = grecv[pl.ds(base + 16 * t, 16), :]
                gi = grecv[pl.ds(base + 48 + 16 * t, 16), :]
                out.append(carry[2 * t] + (gr * vr + gi * vi))
                out.append(carry[2 * t + 1] + (gi * vr - gr * vi))
            return tuple(out)

        total = lax.fori_loop(0, DP, sample_step, tuple(jnp.zeros((CH, 128), F32) for _ in range(6)))
        for t in range(3):
            gs_ref[c, :, 0, 128 * t : 128 * t + 128] = total[2 * t]
            gs_ref[c, :, 1, 128 * t : 128 * t + 128] = total[2 * t + 1]

    for phase in range(4):
        slab_all(phase).wait_send()
    p_all.wait_send()
    q_all.wait_recv()
    total = qrecv[0:8, :]
    for d in range(1, DP):
        total = total + qrecv[8 * d : 8 * d + 8, :]
    gp_ref[...] = total
    q_all.wait_send()
    v_all.wait_send()
    g_all.wait_send()
    o_copy.wait()


def last_kernel(
    rows_hbm, mixed_hbm, gs_in, gp_in, table_hbm, gi_hbm, gs_hbm, gp_hbm,
    rows_ref, gs_ref, bv, table, held, store, gp, insem, tsem, osem, gssem, gpsem, rsem,
):
    rows_copy = pltpu.make_async_copy(rows_hbm, rows_ref, rsem)
    rows_copy.start()
    table_copy = pltpu.make_async_copy(table_hbm, table, tsem)
    table_copy.start()

    def in_copy(c):
        return pltpu.make_async_copy(mixed_hbm.at[pl.ds(2 * c, 2)], bv.at[pl.ds(2 * c, 2)], insem.at[c])

    def out_copy(c):
        return pltpu.make_async_copy(bv.at[pl.ds(2 * c, 2)], gi_hbm.at[pl.ds(2 * c, 2)], osem.at[c])

    for c in range(CH // 2):
        in_copy(c).start()
    gs_load = pltpu.make_async_copy(gs_in, gs_ref, gssem)
    gs_load.start()
    rows_copy.wait()
    for r in range(2):
        flat = gp_in[r : r + 1, :]
        for i in range(8):
            gp[8 * r + i : 8 * r + i + 1, :] = flat[:, CH * i : CH * i + CH] * (1.0 / math.sqrt(DP * NX * NY * NZ))
    gp_copy = pltpu.make_async_copy(gp, gp_hbm, gpsem)
    gp_copy.start()
    table_copy.wait()
    ty_inverse = table.at[pl.ds(0, 128)]
    synthesise_z(rows_ref, table.at[pl.ds(128, 480)], table.at[pl.ds(608, 480)], held, store)

    def last_step(c, carry):
        in_copy(c).wait()
        for x in range(XP):
            out = synthesise_y(store, ty_inverse, x * CH + 2 * c)
            bv[2 * c, x] = bv[2 * c, x] + out[:, :NZ]
            bv[2 * c + 1, x] = bv[2 * c + 1, x] + out[:, NZ:]
        out_copy(c).start()
        return carry

    gs_load.wait()
    gs_copy = pltpu.make_async_copy(gs_ref, gs_hbm, gssem)
    gs_copy.start()
    lax.fori_loop(0, CH // 2, last_step, 0)
    gs_copy.wait()
    gp_copy.wait()
    for c in range(CH // 2):
        out_copy(c).wait()


def body(inputs, cotangent, spectral_weights, pointwise_weights):
    main_table, last_table = (jnp.asarray(table) for table in tables())
    hbm = pl.BlockSpec(memory_space=pltpu.HBM)
    vmem = pl.BlockSpec(memory_space=pltpu.VMEM)
    block = (CH, XP, NY, NZ)
    dma = pltpu.SemaphoreType.DMA
    block_shape = jax.ShapeDtypeStruct(block, F32)
    weight_shape = jax.ShapeDtypeStruct((2, CH, 2, KX * KZ), F32)
    store_shape = pltpu.VMEM((CH * XP * PITCH, NZ), F32)
    rows, mixed, weight_part, point_part = pl.pallas_call(
        kernel,
        out_shape=[
            jax.ShapeDtypeStruct((SLAB, KZ, 128), F32),
            block_shape,
            weight_shape,
            jax.ShapeDtypeStruct((8, 128), F32),
        ],
        in_specs=[hbm] * 5,
        out_specs=[vmem, hbm, vmem, vmem],
        scratch_shapes=[
            pltpu.VMEM(block, F32),
            pltpu.VMEM(block, F32),
            pltpu.VMEM(block, F32),
            pltpu.VMEM((CH, CH, 2, KX * KZ), F32),
            pltpu.VMEM((CH * 96, 128), F32),
            pltpu.VMEM((CH * 96, 128), F32),
            pltpu.VMEM((CH, CH), F32),
            pltpu.VMEM((TABLE, 256), BF16),
            store_shape,
            store_shape,
            pltpu.VMEM((512, 256), BF16),
            pltpu.VMEM((4, SLAB, KZ, 128), F32),
            pltpu.VMEM((4, SLAB, KZ, 128), F32),
            pltpu.VMEM((96, 128), F32),
            pltpu.VMEM((96, 128), F32),
            pltpu.VMEM((256, 256), BF16),
            pltpu.VMEM((256, 256), BF16),
            pltpu.VMEM((256, 256), F32),
            pltpu.VMEM((16 * DP, 128), F32),
            pltpu.VMEM((16 * DP, 128), F32),
            pltpu.VMEM((96 * DP, 128), F32),
            pltpu.VMEM((8, 128), F32),
            pltpu.VMEM((8 * SLAB, 128), F32),
            pltpu.VMEM((8, 128), F32),
            pltpu.VMEM((8 * DP, 128), F32),
            dma((CH // 2,)),
            dma,
            dma,
            dma,
            dma((2,)),
            dma,
            dma((4,)),
            dma((4,)),
            dma,
            dma,
            dma,
            dma,
            dma,
            dma,
            dma,
            dma,
            dma,
            dma,
        ],
        compiler_params=pltpu.CompilerParams(
            collective_id=0, has_side_effects=True, vmem_limit_bytes=60 * 1024 * 1024
        ),
        name="layer_backward",
    )(inputs.reshape(block), cotangent.reshape(block), spectral_weights, pointwise_weights, main_table)
    grad_inputs, grad_spectral, grad_pointwise = pl.pallas_call(
        last_kernel,
        out_shape=[block_shape, weight_shape, jax.ShapeDtypeStruct((CH, CH), F32)],
        in_specs=[hbm, hbm, hbm, vmem, hbm],
        out_specs=[hbm, hbm, hbm],
        scratch_shapes=[
            pltpu.VMEM((SLAB, KZ, 128), F32),
            pltpu.VMEM((2, CH, 2, KX * KZ), F32),
            pltpu.VMEM(block, F32),
            pltpu.VMEM((LAST_TABLE, 256), BF16),
            pltpu.VMEM((512, 256), BF16),
            store_shape,
            pltpu.VMEM((CH, CH), F32),
            dma((CH // 2,)),
            dma,
            dma((CH // 2,)),
            dma,
            dma,
            dma,
        ],
        compiler_params=pltpu.CompilerParams(vmem_limit_bytes=60 * 1024 * 1024),
        name="input_gradient",
    )(rows, mixed, weight_part, point_part, last_table)
    return (grad_inputs[None], grad_spectral, grad_pointwise)


def solution(mesh):
    placed = (
        P("dp", None, "slab", None, None),
        P("dp", None, "slab", None, None),
        P(None, None, None, "slab"),
        P(),
    )
    return jax.shard_map(
        body,
        mesh=mesh,
        in_specs=placed,
        out_specs=(P("dp", None, "slab", None, None), P("dp", None, None, "slab"), P()),
        check_vma=False,
    )
```

```python
import functools
import math

import jax
import jax.numpy as jnp
import ml_dtypes
import numpy as np
from jax import lax
from jax.experimental import pallas as pl
from jax.experimental.pallas import tpu as pltpu
from jax.sharding import PartitionSpec as P

CH = 16
XP = 4
NX = 128
NY = 128
NZ = 128
KX = 32
KY = 32
KZ = 12
SLAB = 32
DP = 8
ROWS = 16
PITCH = 72
F32 = jnp.float32
BF16 = jnp.bfloat16
MESH = pl.DeviceIdType.MESH
NORM = 1.0 / math.sqrt(NX * NY * NZ)


def halves(table):
    table = np.asarray(table, np.float64)
    high = table.astype(ml_dtypes.bfloat16)
    low = (table - high.astype(np.float64)).astype(ml_dtypes.bfloat16)
    return high, low


def angles(length, orders):
    places = np.arange(length)[:, None]
    return ((places * orders[None, :]) % length) * (2.0 * math.pi / length)


@functools.cache
def tables():
    centred = np.arange(KY)
    centred = np.where(centred < KY // 2, centred, centred - KY)
    second = angles(NY, centred)
    third = angles(NZ, np.arange(KZ))
    first = angles(NX, centred)
    ty = np.concatenate([np.cos(second).T, -np.sin(second).T], axis=0)
    ty_high, ty_low = halves(ty)
    ty_stack = np.concatenate(
        [np.concatenate([ty_high, ty_high], axis=1), np.concatenate([ty_low, np.zeros_like(ty_low)], axis=1)], axis=0
    )
    ty_inverse = np.concatenate([ty_high.T, ty_high.T, ty_low.T], axis=1)
    depth = {}
    for name, weights in (("plain", np.ones(KZ)), ("weighted", np.where(np.arange(KZ) == 0, 1.0, 2.0))):
        cosine = (np.cos(third) * weights[None, :]).T
        sine = (np.sin(third) * weights[None, :]).T
        real_row = np.concatenate([cosine, sine], axis=1)
        imag_row = np.concatenate([-sine, cosine], axis=1)
        analysis = np.zeros((2 * ROWS, 2 * NZ))
        analysis[:KZ] = real_row
        analysis[ROWS : ROWS + KZ] = imag_row
        synthesis = np.zeros((2, 15 * ROWS, 2 * NZ))
        synthesis[0, 7 * ROWS : 7 * ROWS + KZ] = real_row
        synthesis[1, 7 * ROWS : 7 * ROWS + KZ] = imag_row
        depth[name] = (np.concatenate(halves(analysis), axis=0),) + halves(synthesis)
    place = first.reshape(SLAB, XP, KX)
    cosine = np.cos(place).transpose(1, 0, 2) * NORM
    sine = np.sin(place).transpose(1, 0, 2) * NORM
    rows = np.zeros((2, XP, 4, SLAB, 2, 4, KX))
    for group in range(4):
        rows[0, :, group, :, 0, group] = cosine
        rows[1, :, group, :, 0, group] = sine
        rows[0, :, group, :, 1, group] = -sine
        rows[1, :, group, :, 1, group] = cosine
    rows = rows.reshape(2 * XP * 4 * SLAB, 2 * 4 * KX)
    ty_inverse = np.concatenate([ty_inverse, np.zeros_like(ty_inverse[:, :64])], axis=1)
    flat = {}
    for name, (analysis, high, low) in depth.items():
        flat[name] = (analysis, high.reshape(-1, 2 * NZ), low.reshape(-1, 2 * NZ))
    columns = rows.T.reshape(256, 4, 256).transpose(1, 0, 2).reshape(1024, 256)
    first_part = (ty_stack, flat["plain"][0]) + halves(rows) + halves(columns) + (ty_inverse,) + flat["weighted"]
    return np.concatenate(first_part, axis=0), np.concatenate((ty_inverse,) + flat["plain"][1:], axis=0)


TY = 0
TZP = 128
XH = 192
XL = XH + 1024
IH = XL + 1024
IL = IH + 1024
TYI = IL + 1024
TZW = TYI + 128
ZWH = TZW + 64
ZWL = ZWH + 480
TABLE = ZWL + 480
LAST_TABLE = 128 + 960


def each_channel(step, carry):
    for c in range(CH):
        carry = step(c, carry)
    return carry


def split(value):
    high = value.astype(BF16)
    low = (value - high.astype(F32)).astype(BF16)
    return high, low


def dot(left, right):
    return jnp.dot(left, right, preferred_element_type=F32)


def dot_t(left, right):
    return lax.dot_general(left, right, (((1,), (1,)), ((), ())), preferred_element_type=F32)


def cat(pieces, axis):
    return jnp.concatenate(pieces, axis=axis)


def analyse_y(pair, ty_stack, store, group):
    high, low = split(pair)
    out = dot(ty_stack[...], cat([high, low], 0))
    out = out[:64] + out[64:]
    store[pl.ds(pl.multiple_of(group * PITCH, 8), 64), :] = out[:, :NZ]
    store[pl.ds(pl.multiple_of((group + 1) * PITCH, 8), 64), :] = out[:, NZ:]


def analyse_z(store, tz_stack, sbuf, phase, first_group, send, send_own):
    lanes = lax.broadcasted_iota(jnp.int32, (ROWS, 128), 1) < 64

    def analyse(group):
        pieces = []
        for each in range(4):
            j = group * 4 + each
            pieces.append(cat([store[pl.ds(j, 64, stride=PITCH), :], store[pl.ds(KY + j, 64, stride=PITCH), :]], 1))
        high, low = split(cat(pieces, 0))
        out = dot_t(tz_stack[...], high)
        out = out[:32] + out[32:] + dot_t(tz_stack[:32, :], low)
        for each in range(2):
            tile = out[:, 128 * each : 128 * each + 128]
            real, imag = tile[:ROWS], tile[ROWS:]
            first = jnp.where(lanes, real, pltpu.roll(imag, 64, axis=1))
            second = jnp.where(lanes, pltpu.roll(real, 64, axis=1), imag)
            sbuf[phase, group * 4 + 2 * each] = first[:KZ]
            sbuf[phase, group * 4 + 2 * each + 1] = second[:KZ]

    def step(turn, carry):
        group = lax.rem(first_group + turn, KY // 4)
        analyse(group)
        for each in range(4):
            send(group * 4 + each)
        return carry

    lax.fori_loop(0, 4, step, 0, unroll=4)
    analyse(lax.rem(first_group + 4, KY // 4))
    send_own()
    lax.fori_loop(5, KY // 4, step, 0, unroll=3)


def analyse_x(rbuf, phase, rows_high, rows_low):
    parts = []
    for t in range(3):
        block = cat([rbuf[phase, :, 4 * t + k, :] for k in range(4)], 0).T
        parts.append(cat([block[16 * q : 16 * q + 16] for q in range(8)], 1))
    high, low = split(cat(parts, 0))
    out = dot(cat([high, low], 0), rows_high[...])
    return out[:48] + out[48:] + dot(high, rows_low[...])


def synthesise_x(modes, columns_high, columns_low, put):
    high, low = split(modes)
    both = cat([high, low], 0)
    tiles = []
    for n in range(4):
        out = dot(both, columns_high[pl.ds(256 * n, 256), :])
        tiles.append(out[:48] + out[48:] + dot(high, columns_low[pl.ds(256 * n, 256), :]))
    out = cat(tiles, 1)
    for t in range(3):
        part = out[16 * t : 16 * t + 16]
        block = cat([part[:, 128 * q : 128 * q + 128] for q in range(8)], 0).T
        for k in range(4):
            put(4 * t + k, block[SLAB * k : SLAB * k + SLAB])


def synthesise_z(rbuf, zi_high, zi_low, held, store):
    spare = jnp.zeros((ROWS - KZ, 128), F32)
    for g in range(4):
        pieces = []
        for each in range(8):
            pieces += [rbuf[8 * g + each], spare]
        block = cat(pieces, 0).T
        high, low = split(cat([block[:64], block[64:]], 1))
        held[pl.ds(64 * g, 64), :] = high
        held[pl.ds(256 + 64 * g, 64), :] = low

    def step(jj, carry):
        at = pl.multiple_of(7 * ROWS - ROWS * jj, ROWS)
        table_high = cat([zi_high[pl.ds(at, 128), :], zi_high[pl.ds(at + 240, 128), :]], 0)
        table_low = cat([zi_low[pl.ds(at, 128), :], zi_low[pl.ds(at + 240, 128), :]], 0)
        out = dot(held[...], table_high)
        out = out[:256] + out[256:] + dot(held[:256, :], table_low)
        for g in range(4):
            store[pl.ds(8 * g + jj, 64, stride=PITCH), :] = out[64 * g : 64 * g + 64, :NZ]
            store[pl.ds(KY + 8 * g + jj, 64, stride=PITCH), :] = out[64 * g : 64 * g + 64, NZ:]
        return carry

    lax.fori_loop(0, 8, step, 0, unroll=8)


def synthesise_y(store, ty_inverse, group):
    pair = cat(
        [
            store[pl.ds(pl.multiple_of(group * PITCH, 8), 64), :],
            store[pl.ds(pl.multiple_of((group + 1) * PITCH, 8), 64), :],
        ],
        1,
    )
    high, low = split(pair)
    return dot(ty_inverse[:, :192], cat([high, low, high], 0))


def rows_of(source, x, y0):
    left = cat([source[c, x, pl.ds(y0, 8), :] for c in range(CH)], 0)
    right = cat([source[c, x, pl.ds(y0 + 8, 8), :] for c in range(CH)], 0)
    return cat([left, right], 1)


def mix_channels(kron, halves_stack, target, x, y0):
    out = dot(kron[...], halves_stack)
    out = out[:128] + out[128:]
    for c in range(CH):
        target[c, x, pl.ds(y0, 8), :] = out[8 * c : 8 * c + 8, :NZ]
        target[c, x, pl.ds(y0 + 8, 8), :] = out[8 * c : 8 * c + 8, NZ:]


def kernel(
    x_hbm, cot_hbm, w_hbm, pw_hbm, table_hbm,
    rows_hbm, mixed_hbm, gs_hbm, q_hbm,
    xv, cv, bv, wv, wco, woc, pw, table, store, store2, held, sbuf, rbuf, vv, gv, kron1, kron2, pacc,
    vsend, vrecv, grecv, psend, precv, qsend, gs_ref,
    xsem, csem, wsem, pwsem, tsem, osem, ssem, rsem, vssem, vrsem, gssem, grsem, hssem, hrsem, pssem, prsem, qssem, qrsem, ownsem, qownsem, gsem,
):
    me = lax.axis_index("slab")
    mine = lax.axis_index("dp")

    def x_copy(c):
        return pltpu.make_async_copy(x_hbm.at[pl.ds(2 * c, 2)], xv.at[pl.ds(2 * c, 2)], xsem.at[c])

    def table_copy(index, start, size):
        return pltpu.make_async_copy(
            table_hbm.at[pl.ds(start, size)], table.at[pl.ds(start, size)], tsem.at[index]
        )

    first_table = table_copy(0, 0, XH)
    first_table.start()
    for c in range(CH // 2):
        x_copy(c).start()
    pw_copy = pltpu.make_async_copy(pw_hbm, pw, pwsem)
    pw_copy.start()
    second_table = table_copy(1, XH, TABLE - XH)
    second_table.start()
    w_copy = pltpu.make_async_copy(w_hbm, wv, wsem)
    w_copy.start()
    c_copy = pltpu.make_async_copy(cot_hbm, cv, csem)
    c_copy.start()

    barrier = pltpu.get_barrier_semaphore()

    def greet_slab(d, carry):
        pl.semaphore_signal(barrier, inc=1, device_id={"slab": lax.rem(me + d, SLAB)}, device_id_type=MESH)
        return carry

    def greet_dp(d, carry):
        pl.semaphore_signal(barrier, inc=1, device_id={"dp": lax.rem(mine + d, DP)}, device_id_type=MESH)
        return carry

    lax.fori_loop(1, SLAB, greet_slab, 0)
    lax.fori_loop(1, DP, greet_dp, 0)

    ty_stack = table.at[pl.ds(TY, 128)]
    tz_plain = table.at[pl.ds(TZP, 64)]
    rows_high = table.at[pl.ds(XH, 1024)]
    rows_low = table.at[pl.ds(XL, 1024)]
    columns_high = table.at[pl.ds(IH, 1024)]
    columns_low = table.at[pl.ds(IL, 1024)]
    ty_inverse = table.at[pl.ds(TYI, 128)]
    tz_weighted = table.at[pl.ds(TZW, 64)]
    zw_high = table.at[pl.ds(ZWH, 480)]
    zw_low = table.at[pl.ds(ZWL, 480)]

    def slab_copy(phase, p):
        return pltpu.make_async_remote_copy(
            src_ref=sbuf.at[phase, p],
            dst_ref=rows_hbm.at[me] if phase == 3 else rbuf.at[phase, me],
            send_sem=ssem.at[phase],
            recv_sem=rsem.at[phase],
            device_id={"slab": p},
            device_id_type=MESH,
        )

    def slab_all(phase):
        every = pl.ds(0, SLAB - 1)
        return pltpu.make_async_remote_copy(
            src_ref=sbuf.at[phase, every],
            dst_ref=rows_hbm.at[every] if phase == 3 else rbuf.at[phase, every],
            send_sem=ssem.at[phase],
            recv_sem=rsem.at[phase],
            device_id={"slab": lax.rem(me + 1, SLAB)},
            device_id_type=MESH,
        )

    own_copy = pltpu.make_async_copy(sbuf.at[3, me], rows_hbm.at[me], ownsem)

    def keep_own(phase):
        if phase == 3:
            own_copy.start()
        else:
            rbuf[phase, me] = sbuf[phase, me]

    def send_one(phase):
        def send(p):
            slab_copy(phase, p).start()

        return send

    def send_group(phase):
        def send():
            for d in range(1, 4):
                slab_copy(phase, me // 4 * 4 + lax.rem(me + d, 4)).start()
            keep_own(phase)

        return send

    def send_all(phase):
        def step(turn, carry):
            for each in range(4):
                slab_copy(phase, lax.rem(me + 16 + 4 * turn + each, SLAB)).start()
            return carry

        lax.fori_loop(0, 4, step, 0)

        def near_step(turn, carry):
            for each in range(3):
                slab_copy(phase, lax.rem(me + 1 + 3 * turn + each, SLAB)).start()
            return carry

        lax.fori_loop(0, 5, near_step, 0)
        keep_own(phase)

    first_group = me // 4 + 4
    core = lax.rem(mine, 2)
    place = core * 4 + mine // 2

    spread = (
        lax.broadcasted_iota(jnp.int32, (128, CH), 0) // 8 == lax.broadcasted_iota(jnp.int32, (128, CH), 1)
    ).astype(F32)
    same_row = (
        lax.broadcasted_iota(jnp.int32, (128, 128), 0) % 8 == lax.broadcasted_iota(jnp.int32, (128, 128), 1) % 8
    )

    first_table.wait()

    def forward_step(c, carry):
        x_copy(c).wait()
        for x in range(XP):
            analyse_y(cat([xv[2 * c, x], xv[2 * c + 1, x]], 1), ty_stack, store, x * CH + 2 * c)
        return carry

    lax.fori_loop(0, CH // 2, forward_step, 0)
    pl.semaphore_wait(barrier, SLAB - 1 + DP - 1)
    analyse_z(store, tz_plain, sbuf, 0, first_group, send_one(0), send_group(0))

    pw_copy.wait()
    wide = jnp.dot(spread, pw[...], precision=lax.Precision.HIGHEST, preferred_element_type=F32)
    wide = lax.dot_general(
        wide, spread, (((1,), (1,)), ((), ())), precision=lax.Precision.HIGHEST, preferred_element_type=F32
    )
    wide = jnp.where(same_row, wide, 0.0)
    for kron, value in ((kron1, wide.T), (kron2, wide)):
        high, low = split(value)
        kron[...] = cat([cat([high, high], 1), cat([low, jnp.zeros_like(low)], 1)], 0)

    w_copy.wait()

    def regroup_step(c, carry):
        base = pl.multiple_of(c * 96, 16)
        for ri in range(2):
            for t in range(3):
                wco[pl.ds(base + 48 * ri + 16 * t, 16), :] = wv[c, :, ri, 128 * t : 128 * t + 128]
        return carry

    lax.fori_loop(0, CH, regroup_step, 0)
    second_table.wait()
    slab_all(0).wait_recv()
    modes = analyse_x(rbuf, 0, rows_high, rows_low)
    vv[:48, :] = modes[:, :128]
    vv[48:, :] = modes[:, 128:]

    def spread_row(modes, c):
        return cat([jnp.broadcast_to(modes[pl.ds(16 * t + c, 1), :], (16, 128)) for t in range(3)], 0), cat(
            [jnp.broadcast_to(modes[pl.ds(48 + 16 * t + c, 1), :], (16, 128)) for t in range(3)], 0
        )

    def mode_step(c, carry):
        base = c * 96
        wr, wi = wco[pl.ds(base, 48), :], wco[pl.ds(base + 48, 48), :]
        vr, vi = spread_row(vv, c)
        return carry[0] + (wr * vr - wi * vi), carry[1] + (wr * vi + wi * vr)

    no_modes = (jnp.zeros((48, 128), F32), jnp.zeros((48, 128), F32))
    mixed = cat(each_channel(mode_step, no_modes), 1)

    def put_mixed(k, value):
        sbuf[1, :, k, :] = value

    synthesise_x(mixed, columns_high, columns_low, put_mixed)
    send_all(1)

    def v_copy(d):
        return pltpu.make_async_remote_copy(
            src_ref=vsend.at[pl.ds(pl.multiple_of(16 * d, 16), 16)],
            dst_ref=vrecv.at[pl.ds(pl.multiple_of(16 * place, 16), 16)],
            send_sem=vssem,
            recv_sem=vrsem,
            device_id={"dp": d},
            device_id_type=MESH,
        )

    vsend[...] = jnp.zeros_like(vsend)
    for d in range(DP):
        for c in range(2):
            for t in range(3):
                row = 16 * t + 2 * d + c
                at = 16 * d + 6 * c + t
                vsend[at : at + 1, :] = vv[row : row + 1, :]
                vsend[at + 3 : at + 4, :] = vv[row + 48 : row + 49, :]

    def v_send(d, carry):
        v_copy(lax.rem(mine + d, DP)).start()
        return carry

    lax.fori_loop(1, DP, v_send, 0)
    vrecv[pl.ds(pl.multiple_of(16 * place, 16), 16), :] = vsend[pl.ds(pl.multiple_of(16 * mine, 16), 16), :]

    def turn_step(o, carry):
        base = pl.multiple_of(o * 96, 16)
        for part in range(6):
            woc[pl.ds(base + 16 * part, 16), :] = wco[pl.ds(16 * part + o, 16, stride=96), :]
        return carry

    lax.fori_loop(0, CH, turn_step, 0)

    def mix_step(yg, carry):
        y0 = pl.multiple_of(yg * 16, 16)
        for x in range(XP):
            high, low = split(rows_of(xv, x, y0))
            mix_channels(kron1, cat([high, low], 0), bv, x, y0)
        return carry

    lax.fori_loop(0, NY // 16, mix_step, 0)
    c_copy.wait()
    slab_all(1).wait_recv()

    synthesise_z(rbuf.at[1], zw_high, zw_low, held, store)

    def middle_step(o, carry):
        for x in range(XP):
            carried = synthesise_y(store, ty_inverse, x * CH + 2 * o)
            grads = []
            for each in range(2):
                before = carried[:, NZ * each : NZ * each + NZ] + bv[2 * o + each, x]
                slope = 0.5 * (1.0 + lax.erf(before * (1.0 / math.sqrt(2.0)))) + before * jnp.exp(
                    -0.5 * before * before
                ) * (1.0 / math.sqrt(2.0 * math.pi))
                grad = cv[2 * o + each, x] * slope
                cv[2 * o + each, x] = grad
                grads.append(grad)
            analyse_y(cat(grads, 1), ty_stack, store2, x * CH + 2 * o)
        return carry

    lax.fori_loop(0, CH // 2, middle_step, 0, unroll=4)
    analyse_z(store2, tz_weighted, sbuf, 2, first_group, send_one(2), send_group(2))

    pacc[...] = jnp.zeros_like(pacc)

    def pointwise_step(yg, carry):
        y0 = pl.multiple_of(yg * 16, 16)
        for x in range(XP):
            high, low = split(rows_of(cv, x, y0))
            xhigh, xlow = split(rows_of(xv, x, y0))
            pacc[...] += dot_t(cat([xhigh, xlow], 0), cat([high, low], 0))
        return carry

    lax.fori_loop(0, NY // 16, pointwise_step, 0)
    part = pacc[:128, :128] + pacc[:128, 128:] + pacc[128:, :128] + pacc[128:, 128:]
    part = jnp.where(same_row, part, 0.0)
    part = jnp.dot(part, spread, precision=lax.Precision.HIGHEST, preferred_element_type=F32)
    part = lax.dot_general(
        spread, part, (((0,), (0,)), ((), ())), precision=lax.Precision.HIGHEST, preferred_element_type=F32
    )
    flat = [cat([part[8 * r + i : 8 * r + i + 1, :] for i in range(8)], 1) for r in range(2)]
    part = cat(flat + [jnp.zeros((6, 128), F32)], 0)

    def p_copy(p):
        return pltpu.make_async_remote_copy(
            src_ref=psend,
            dst_ref=precv.at[pl.ds(pl.multiple_of(8 * me, 8), 8)],
            send_sem=pssem,
            recv_sem=prsem,
            device_id={"slab": p},
            device_id_type=MESH,
        )

    psend[...] = part

    def p_send(d, carry):
        p_copy(lax.rem(me + d, SLAB)).start()
        return carry

    lax.fori_loop(1, SLAB, p_send, 0)
    precv[pl.ds(pl.multiple_of(8 * me, 8), 8), :] = part

    slab_all(2).wait_recv()
    modes = analyse_x(rbuf, 2, rows_high, rows_low)
    gv[:48, :] = modes[:, :128]
    gv[48:, :] = modes[:, 128:]

    def g_copy(d):
        return pltpu.make_async_remote_copy(
            src_ref=gv,
            dst_ref=grecv.at[pl.ds(pl.multiple_of(96 * place, 16), 96)],
            send_sem=gssem,
            recv_sem=grsem,
            device_id={"dp": lax.rem(mine + 2 * d, DP)},
            device_id_type=MESH,
        )

    for d in range(1, 4):
        g_copy(d).start()
    grecv[pl.ds(pl.multiple_of(96 * place, 16), 96), :] = gv[...]

    def back_mode_step(o, carry):
        base = o * 96
        wr, wi = woc[pl.ds(base, 48), :], woc[pl.ds(base + 48, 48), :]
        gr, gi = spread_row(gv, o)
        return carry[0] + (wr * gr + wi * gi), carry[1] + (wr * gi - wi * gr)

    back = cat(each_channel(back_mode_step, no_modes), 1)

    def put_back(k, value):
        sbuf[3, :, k, :] = value

    def dp_all(source, target, size, send_sem, recv_sem):
        return pltpu.make_async_remote_copy(
            src_ref=source.at[pl.ds(0, size)],
            dst_ref=target.at[pl.ds(0, size)],
            send_sem=send_sem,
            recv_sem=recv_sem,
            device_id={"dp": lax.rem(mine + 1, DP)},
            device_id_type=MESH,
        )

    v_all = dp_all(vrecv, vrecv, 16 * (DP - 1), vssem, vrsem)
    g_all = dp_all(grecv, grecv, 96 * 3, gssem, grsem)
    synthesise_x(back, columns_high, columns_low, put_back)
    send_all(3)

    p_all = pltpu.make_async_remote_copy(
        src_ref=precv.at[pl.ds(0, 8 * (SLAB - 1))],
        dst_ref=precv.at[pl.ds(0, 8 * (SLAB - 1))],
        send_sem=pssem,
        recv_sem=prsem,
        device_id={"slab": lax.rem(me + 1, SLAB)},
        device_id_type=MESH,
    )
    p_all.wait_recv()
    total = precv[0:8, :]
    for p in range(1, SLAB):
        total = total + precv[8 * p : 8 * p + 8, :]
    qsend[...] = total

    def q_copy(d):
        return pltpu.make_async_remote_copy(
            src_ref=qsend,
            dst_ref=q_hbm.at[pl.ds(pl.multiple_of(8 * mine, 8), 8)],
            send_sem=qssem,
            recv_sem=qrsem,
            device_id={"dp": d},
            device_id_type=MESH,
        )

    def q_send(d, carry):
        q_copy(lax.rem(mine + d, DP)).start()
        return carry

    lax.fori_loop(1, DP, q_send, 0)
    q_own = pltpu.make_async_copy(qsend, q_hbm.at[pl.ds(pl.multiple_of(8 * mine, 8), 8)], qownsem)
    q_own.start()
    q_all = dp_all(q_hbm, q_hbm, 8 * (DP - 1), qssem, qrsem)
    v_all.wait_recv()
    g_all.wait_recv()
    half = pl.ds(pl.multiple_of(core * 384, 16), 384)
    h_copy = pltpu.make_async_remote_copy(
        src_ref=grecv.at[half],
        dst_ref=grecv.at[half],
        send_sem=hssem,
        recv_sem=hrsem,
        device_id={"dp": mine + 1 - 2 * core},
        device_id_type=MESH,
    )
    h_copy.start()

    def back_step(yg, carry):
        y0 = pl.multiple_of(yg * 16, 16)
        for x in range(XP):
            high, low = split(rows_of(cv, x, y0))
            mix_channels(kron2, cat([high, low], 0), bv, x, y0)
        return carry

    lax.fori_loop(0, NY // 16, back_step, 0)
    o_copy = pltpu.make_async_copy(bv, mixed_hbm, osem)
    o_copy.start()
    h_copy.wait()

    for c in range(2):
        def sample_step(d, carry):
            out = []
            base = pl.multiple_of(96 * d, 16)
            for t in range(3):
                vr = vrecv[pl.ds(16 * d + 6 * c + t, 1), :]
                vi = vrecv[pl.ds(16 * d + 6 * c + 3 + t, 1), :]
                gr = grecv[pl.ds(base + 16 * t, 16), :]
                gi = grecv[pl.ds(base + 48 + 16 * t, 16), :]
                out.append(carry[2 * t] + (gr * vr + gi * vi))
                out.append(carry[2 * t + 1] + (gi * vr - gr * vi))
            return tuple(out)

        total = lax.fori_loop(0, DP, sample_step, tuple(jnp.zeros((CH, 128), F32) for _ in range(6)))
        for t in range(3):
            gs_ref[c, :, 0, 128 * t : 128 * t + 128] = total[2 * t]
            gs_ref[c, :, 1, 128 * t : 128 * t + 128] = total[2 * t + 1]

    gs_copy = pltpu.make_async_copy(gs_ref, gs_hbm, gsem)
    gs_copy.start()
    for phase in range(4):
        slab_all(phase).wait_send()
    p_all.wait_send()
    q_all.wait_send()
    v_all.wait_send()
    g_all.wait_send()
    o_copy.wait()
    own_copy.wait()
    q_own.wait()
    gs_copy.wait()
    slab_all(3).wait_recv()
    q_all.wait_recv()


def last_kernel(
    rows_hbm, mixed_hbm, gs_in, q_hbm, table_hbm, gi_hbm, gs_hbm, gp_hbm,
    rows_ref, gs_ref, q_ref, bv, table, held, store, gp, insem, tsem, osem, gssem, gpsem, rsem, qsem,
):
    rows_copy = pltpu.make_async_copy(rows_hbm, rows_ref, rsem)
    rows_copy.start()
    table_copy = pltpu.make_async_copy(table_hbm, table, tsem)
    table_copy.start()

    def in_copy(c):
        return pltpu.make_async_copy(mixed_hbm.at[pl.ds(2 * c, 2)], bv.at[pl.ds(2 * c, 2)], insem.at[c])

    def out_copy(c):
        return pltpu.make_async_copy(bv.at[pl.ds(2 * c, 2)], gi_hbm.at[pl.ds(2 * c, 2)], osem.at[c])

    for c in range(CH // 2):
        in_copy(c).start()
    gs_load = pltpu.make_async_copy(gs_in, gs_ref, gssem)
    gs_load.start()
    q_copy = pltpu.make_async_copy(q_hbm, q_ref, qsem)
    q_copy.start()
    rows_copy.wait()
    table_copy.wait()
    ty_inverse = table.at[pl.ds(0, 128)]
    synthesise_z(rows_ref, table.at[pl.ds(128, 480)], table.at[pl.ds(608, 480)], held, store)

    def last_step(c, carry):
        in_copy(c).wait()
        for x in range(XP):
            out = synthesise_y(store, ty_inverse, x * CH + 2 * c)
            bv[2 * c, x] = bv[2 * c, x] + out[:, :NZ]
            bv[2 * c + 1, x] = bv[2 * c + 1, x] + out[:, NZ:]
        out_copy(c).start()
        return carry

    q_copy.wait()
    total = q_ref[0:8, :]
    for d in range(1, DP):
        total = total + q_ref[8 * d : 8 * d + 8, :]
    total = total * (1.0 / math.sqrt(DP * NX * NY * NZ))
    for r in range(2):
        for i in range(8):
            gp[8 * r + i : 8 * r + i + 1, :] = total[r : r + 1, CH * i : CH * i + CH]
    gp_copy = pltpu.make_async_copy(gp, gp_hbm, gpsem)
    gp_copy.start()
    gs_load.wait()
    gs_copy = pltpu.make_async_copy(gs_ref, gs_hbm, gssem)
    gs_copy.start()
    lax.fori_loop(0, CH // 2, last_step, 0)
    gs_copy.wait()
    gp_copy.wait()
    for c in range(CH // 2):
        out_copy(c).wait()


def body(inputs, cotangent, spectral_weights, pointwise_weights):
    main_table, last_table = (jnp.asarray(table) for table in tables())
    hbm = pl.BlockSpec(memory_space=pltpu.HBM)
    block = (CH, XP, NY, NZ)
    dma = pltpu.SemaphoreType.DMA
    block_shape = jax.ShapeDtypeStruct(block, F32)
    weight_shape = jax.ShapeDtypeStruct((2, CH, 2, KX * KZ), F32)
    store_shape = pltpu.VMEM((CH * XP * PITCH, NZ), F32)
    rows, mixed, weight_part, point_part = pl.pallas_call(
        kernel,
        out_shape=[
            jax.ShapeDtypeStruct((SLAB, KZ, 128), F32),
            block_shape,
            weight_shape,
            jax.ShapeDtypeStruct((8 * DP, 128), F32),
        ],
        in_specs=[hbm] * 5,
        out_specs=[hbm] * 4,
        scratch_shapes=[
            pltpu.VMEM(block, F32),
            pltpu.VMEM(block, F32),
            pltpu.VMEM(block, F32),
            pltpu.VMEM((CH, CH, 2, KX * KZ), F32),
            pltpu.VMEM((CH * 96, 128), F32),
            pltpu.VMEM((CH * 96, 128), F32),
            pltpu.VMEM((CH, CH), F32),
            pltpu.VMEM((TABLE, 256), BF16),
            store_shape,
            store_shape,
            pltpu.VMEM((512, 256), BF16),
            pltpu.VMEM((4, SLAB, KZ, 128), F32),
            pltpu.VMEM((3, SLAB, KZ, 128), F32),
            pltpu.VMEM((96, 128), F32),
            pltpu.VMEM((96, 128), F32),
            pltpu.VMEM((256, 256), BF16),
            pltpu.VMEM((256, 256), BF16),
            pltpu.VMEM((256, 256), F32),
            pltpu.VMEM((16 * DP, 128), F32),
            pltpu.VMEM((16 * DP, 128), F32),
            pltpu.VMEM((96 * DP, 128), F32),
            pltpu.VMEM((8, 128), F32),
            pltpu.VMEM((8 * SLAB, 128), F32),
            pltpu.VMEM((8, 128), F32),
            pltpu.VMEM((2, CH, 2, KX * KZ), F32),
            dma((CH // 2,)),
            dma,
            dma,
            dma,
            dma((2,)),
            dma,
            dma((4,)),
            dma((4,)),
            dma,
            dma,
            dma,
            dma,
            dma,
            dma,
            dma,
            dma,
            dma,
            dma,
            dma,
            dma,
            dma,
        ],
        compiler_params=pltpu.CompilerParams(
            collective_id=0, has_side_effects=True, vmem_limit_bytes=60 * 1024 * 1024
        ),
        name="layer_backward",
    )(inputs.reshape(block), cotangent.reshape(block), spectral_weights, pointwise_weights, main_table)
    grad_inputs, grad_spectral, grad_pointwise = pl.pallas_call(
        last_kernel,
        out_shape=[block_shape, weight_shape, jax.ShapeDtypeStruct((CH, CH), F32)],
        in_specs=[hbm] * 5,
        out_specs=[hbm, hbm, hbm],
        scratch_shapes=[
            pltpu.VMEM((SLAB, KZ, 128), F32),
            pltpu.VMEM((2, CH, 2, KX * KZ), F32),
            pltpu.VMEM((8 * DP, 128), F32),
            pltpu.VMEM(block, F32),
            pltpu.VMEM((LAST_TABLE, 256), BF16),
            pltpu.VMEM((512, 256), BF16),
            store_shape,
            pltpu.VMEM((CH, CH), F32),
            dma((CH // 2,)),
            dma,
            dma((CH // 2,)),
            dma,
            dma,
            dma,
            dma,
        ],
        compiler_params=pltpu.CompilerParams(vmem_limit_bytes=60 * 1024 * 1024),
        name="input_gradient",
    )(rows, mixed, weight_part, point_part, last_table)
    return (grad_inputs[None], grad_spectral, grad_pointwise)


def solution(mesh):
    placed = (
        P("dp", None, "slab", None, None),
        P("dp", None, "slab", None, None),
        P(None, None, None, "slab"),
        P(),
    )
    return jax.shard_map(
        body,
        mesh=mesh,
        in_specs=placed,
        out_specs=(P("dp", None, "slab", None, None), P("dp", None, None, "slab"), P()),
        check_vma=False,
    )
```

```python
import functools
import math

import jax
import jax.numpy as jnp
import ml_dtypes
import numpy as np
from jax import lax
from jax.experimental import pallas as pl
from jax.experimental.pallas import tpu as pltpu
from jax.sharding import PartitionSpec as P

CH = 16
XP = 4
NX = 128
NY = 128
NZ = 128
KX = 32
KY = 32
KZ = 12
SLAB = 32
DP = 8
ROWS = 16
PITCH = 72
F32 = jnp.float32
BF16 = jnp.bfloat16
MESH = pl.DeviceIdType.MESH
NORM = 1.0 / math.sqrt(NX * NY * NZ)


def halves(table):
    table = np.asarray(table, np.float64)
    high = table.astype(ml_dtypes.bfloat16)
    low = (table - high.astype(np.float64)).astype(ml_dtypes.bfloat16)
    return high, low


def angles(length, orders):
    places = np.arange(length)[:, None]
    return ((places * orders[None, :]) % length) * (2.0 * math.pi / length)


@functools.cache
def tables():
    centred = np.arange(KY)
    centred = np.where(centred < KY // 2, centred, centred - KY)
    second = angles(NY, centred)
    third = angles(NZ, np.arange(KZ))
    first = angles(NX, centred)
    ty = np.concatenate([np.cos(second).T, -np.sin(second).T], axis=0)
    ty_high, ty_low = halves(ty)
    ty_stack = np.concatenate(
        [np.concatenate([ty_high, ty_high], axis=1), np.concatenate([ty_low, np.zeros_like(ty_low)], axis=1)], axis=0
    )
    ty_inverse = np.concatenate([ty_high.T, ty_high.T, ty_low.T], axis=1)
    depth = {}
    for name, weights in (("plain", np.ones(KZ)), ("weighted", np.where(np.arange(KZ) == 0, 1.0, 2.0))):
        cosine = (np.cos(third) * weights[None, :]).T
        sine = (np.sin(third) * weights[None, :]).T
        real_row = np.concatenate([cosine, sine], axis=1)
        imag_row = np.concatenate([-sine, cosine], axis=1)
        analysis = np.zeros((2 * ROWS, 2 * NZ))
        analysis[:KZ] = real_row
        analysis[ROWS : ROWS + KZ] = imag_row
        synthesis = np.zeros((2, 15 * ROWS, 2 * NZ))
        synthesis[0, 7 * ROWS : 7 * ROWS + KZ] = real_row
        synthesis[1, 7 * ROWS : 7 * ROWS + KZ] = imag_row
        depth[name] = (np.concatenate(halves(analysis), axis=0),) + halves(synthesis)
    place = first.reshape(SLAB, XP, KX)
    cosine = np.cos(place).transpose(1, 0, 2) * NORM
    sine = np.sin(place).transpose(1, 0, 2) * NORM
    rows = np.zeros((2, XP, 4, SLAB, 2, 4, KX))
    for group in range(4):
        rows[0, :, group, :, 0, group] = cosine
        rows[1, :, group, :, 0, group] = sine
        rows[0, :, group, :, 1, group] = -sine
        rows[1, :, group, :, 1, group] = cosine
    rows = rows.reshape(2 * XP * 4 * SLAB, 2 * 4 * KX)
    ty_inverse = np.concatenate([ty_inverse, np.zeros_like(ty_inverse[:, :64])], axis=1)
    flat = {}
    for name, (analysis, high, low) in depth.items():
        flat[name] = (analysis, high.reshape(-1, 2 * NZ), low.reshape(-1, 2 * NZ))
    columns = rows.T.reshape(256, 4, 256).transpose(1, 0, 2).reshape(1024, 256)
    first_part = (ty_stack, flat["plain"][0]) + halves(rows) + halves(columns) + (ty_inverse,) + flat["weighted"]
    return np.concatenate(first_part, axis=0), np.concatenate((ty_inverse,) + flat["plain"][1:], axis=0)


TY = 0
TZP = 128
XH = 192
XL = XH + 1024
IH = XL + 1024
IL = IH + 1024
TYI = IL + 1024
TZW = TYI + 128
ZWH = TZW + 64
ZWL = ZWH + 480
TABLE = ZWL + 480
LAST_TABLE = 128 + 960


def each_channel(step, carry):
    for c in range(CH):
        carry = step(c, carry)
    return carry


def split(value):
    high = value.astype(BF16)
    low = (value - high.astype(F32)).astype(BF16)
    return high, low


def dot(left, right):
    return jnp.dot(left, right, preferred_element_type=F32)


def dot_t(left, right):
    return lax.dot_general(left, right, (((1,), (1,)), ((), ())), preferred_element_type=F32)


def cat(pieces, axis):
    return jnp.concatenate(pieces, axis=axis)


def analyse_y(pair, ty_stack, store, group):
    high, low = split(pair)
    out = dot(ty_stack[...], cat([high, low], 0))
    out = out[:64] + out[64:]
    store[pl.ds(pl.multiple_of(group * PITCH, 8), 64), :] = out[:, :NZ]
    store[pl.ds(pl.multiple_of((group + 1) * PITCH, 8), 64), :] = out[:, NZ:]


def analyse_z(store, tz_stack, sbuf, phase, first_group, send, send_own):
    lanes = lax.broadcasted_iota(jnp.int32, (ROWS, 128), 1) < 64

    def analyse(group):
        pieces = []
        for each in range(4):
            j = group * 4 + each
            pieces.append(cat([store[pl.ds(j, 64, stride=PITCH), :], store[pl.ds(KY + j, 64, stride=PITCH), :]], 1))
        high, low = split(cat(pieces, 0))
        out = dot_t(tz_stack[...], high)
        out = out[:32] + out[32:] + dot_t(tz_stack[:32, :], low)
        for each in range(2):
            tile = out[:, 128 * each : 128 * each + 128]
            real, imag = tile[:ROWS], tile[ROWS:]
            first = jnp.where(lanes, real, pltpu.roll(imag, 64, axis=1))
            second = jnp.where(lanes, pltpu.roll(real, 64, axis=1), imag)
            sbuf[phase, group * 4 + 2 * each] = first[:KZ]
            sbuf[phase, group * 4 + 2 * each + 1] = second[:KZ]

    def step(turn, carry):
        group = lax.rem(first_group + turn, KY // 4)
        analyse(group)
        for each in range(4):
            send(group * 4 + each)
        return carry

    lax.fori_loop(0, 4, step, 0, unroll=4)
    analyse(lax.rem(first_group + 4, KY // 4))
    send_own()
    lax.fori_loop(5, KY // 4, step, 0, unroll=3)


def analyse_x(rbuf, phase, rows_high, rows_low):
    parts = []
    for t in range(3):
        block = cat([rbuf[phase, :, 4 * t + k, :] for k in range(4)], 0).T
        parts.append(cat([block[16 * q : 16 * q + 16] for q in range(8)], 1))
    high, low = split(cat(parts, 0))
    out = dot(cat([high, low], 0), rows_high[...])
    return out[:48] + out[48:] + dot(high, rows_low[...])


def synthesise_x(modes, columns_high, columns_low, put):
    high, low = split(modes)
    both = cat([high, low], 0)
    tiles = []
    for n in range(4):
        out = dot(both, columns_high[pl.ds(256 * n, 256), :])
        tiles.append(out[:48] + out[48:] + dot(high, columns_low[pl.ds(256 * n, 256), :]))
    out = cat(tiles, 1)
    for t in range(3):
        part = out[16 * t : 16 * t + 16]
        block = cat([part[:, 128 * q : 128 * q + 128] for q in range(8)], 0).T
        for k in range(4):
            put(4 * t + k, block[SLAB * k : SLAB * k + SLAB])


def synthesise_z(rbuf, zi_high, zi_low, held, store):
    spare = jnp.zeros((ROWS - KZ, 128), F32)
    for g in range(4):
        pieces = []
        for each in range(8):
            pieces += [rbuf[8 * g + each], spare]
        block = cat(pieces, 0).T
        high, low = split(cat([block[:64], block[64:]], 1))
        held[pl.ds(64 * g, 64), :] = high
        held[pl.ds(256 + 64 * g, 64), :] = low

    def step(jj, carry):
        at = pl.multiple_of(7 * ROWS - ROWS * jj, ROWS)
        table_high = cat([zi_high[pl.ds(at, 128), :], zi_high[pl.ds(at + 240, 128), :]], 0)
        table_low = cat([zi_low[pl.ds(at, 128), :], zi_low[pl.ds(at + 240, 128), :]], 0)
        out = dot(held[...], table_high)
        out = out[:256] + out[256:] + dot(held[:256, :], table_low)
        for g in range(4):
            store[pl.ds(8 * g + jj, 64, stride=PITCH), :] = out[64 * g : 64 * g + 64, :NZ]
            store[pl.ds(KY + 8 * g + jj, 64, stride=PITCH), :] = out[64 * g : 64 * g + 64, NZ:]
        return carry

    lax.fori_loop(0, 8, step, 0, unroll=8)


def synthesise_y(store, ty_inverse, group):
    pair = cat(
        [
            store[pl.ds(pl.multiple_of(group * PITCH, 8), 64), :],
            store[pl.ds(pl.multiple_of((group + 1) * PITCH, 8), 64), :],
        ],
        1,
    )
    high, low = split(pair)
    return dot(ty_inverse[:, :192], cat([high, low, high], 0))


def rows_of(source, x, y0):
    left = cat([source[c, x, pl.ds(y0, 8), :] for c in range(CH)], 0)
    right = cat([source[c, x, pl.ds(y0 + 8, 8), :] for c in range(CH)], 0)
    return cat([left, right], 1)


def mix_channels(kron, halves_stack, target, x, y0):
    out = dot(kron[...], halves_stack)
    out = out[:128] + out[128:]
    for c in range(CH):
        target[c, x, pl.ds(y0, 8), :] = out[8 * c : 8 * c + 8, :NZ]
        target[c, x, pl.ds(y0 + 8, 8), :] = out[8 * c : 8 * c + 8, NZ:]


def kernel(
    x_hbm, cot_hbm, w_hbm, pw_hbm, table_hbm,
    rows_hbm, mixed_hbm, gs_hbm, q_hbm,
    xv, cv, bv, wv, wco, woc, pw, table, store, store2, held, sbuf, rbuf, vv, gv, kron1, kron2, pacc,
    vsend, vrecv, grecv, psend, precv, qsend, gs_ref,
    xsem, csem, wsem, pwsem, tsem, osem, ssem, rsem, vssem, vrsem, gssem, grsem, hssem, hrsem, pssem, prsem, qssem, qrsem, ownsem, qownsem, gsem,
):
    me = lax.axis_index("slab")
    mine = lax.axis_index("dp")

    def x_copy(c):
        return pltpu.make_async_copy(x_hbm.at[pl.ds(2 * c, 2)], xv.at[pl.ds(2 * c, 2)], xsem.at[c])

    def table_copy(index, start, size):
        return pltpu.make_async_copy(
            table_hbm.at[pl.ds(start, size)], table.at[pl.ds(start, size)], tsem.at[index]
        )

    first_table = table_copy(0, 0, XH)
    first_table.start()
    for c in range(CH // 2):
        x_copy(c).start()
    pw_copy = pltpu.make_async_copy(pw_hbm, pw, pwsem)
    pw_copy.start()
    second_table = table_copy(1, XH, TABLE - XH)
    second_table.start()
    w_copy = pltpu.make_async_copy(w_hbm, wv, wsem)
    w_copy.start()
    c_copy = pltpu.make_async_copy(cot_hbm, cv, csem)
    c_copy.start()

    barrier = pltpu.get_barrier_semaphore()

    def greet_slab(d, carry):
        pl.semaphore_signal(barrier, inc=1, device_id={"slab": lax.rem(me + d, SLAB)}, device_id_type=MESH)
        return carry

    def greet_dp(d, carry):
        pl.semaphore_signal(barrier, inc=1, device_id={"dp": lax.rem(mine + d, DP)}, device_id_type=MESH)
        return carry

    lax.fori_loop(1, SLAB, greet_slab, 0)
    lax.fori_loop(1, DP, greet_dp, 0)

    ty_stack = table.at[pl.ds(TY, 128)]
    tz_plain = table.at[pl.ds(TZP, 64)]
    rows_high = table.at[pl.ds(XH, 1024)]
    rows_low = table.at[pl.ds(XL, 1024)]
    columns_high = table.at[pl.ds(IH, 1024)]
    columns_low = table.at[pl.ds(IL, 1024)]
    ty_inverse = table.at[pl.ds(TYI, 128)]
    tz_weighted = table.at[pl.ds(TZW, 64)]
    zw_high = table.at[pl.ds(ZWH, 480)]
    zw_low = table.at[pl.ds(ZWL, 480)]

    def slab_copy(phase, p):
        return pltpu.make_async_remote_copy(
            src_ref=sbuf.at[phase, p],
            dst_ref=rows_hbm.at[me] if phase == 3 else rbuf.at[phase, me],
            send_sem=ssem.at[phase],
            recv_sem=rsem.at[phase],
            device_id={"slab": p},
            device_id_type=MESH,
        )

    def slab_all(phase):
        every = pl.ds(0, SLAB - 1)
        return pltpu.make_async_remote_copy(
            src_ref=sbuf.at[phase, every],
            dst_ref=rows_hbm.at[every] if phase == 3 else rbuf.at[phase, every],
            send_sem=ssem.at[phase],
            recv_sem=rsem.at[phase],
            device_id={"slab": lax.rem(me + 1, SLAB)},
            device_id_type=MESH,
        )

    own_copy = pltpu.make_async_copy(sbuf.at[3, me], rows_hbm.at[me], ownsem)

    def keep_own(phase):
        if phase == 3:
            own_copy.start()
        else:
            rbuf[phase, me] = sbuf[phase, me]

    def send_one(phase):
        def send(p):
            slab_copy(phase, p).start()

        return send

    def send_group(phase):
        def send():
            for d in range(1, 4):
                slab_copy(phase, me // 4 * 4 + lax.rem(me + d, 4)).start()
            keep_own(phase)

        return send

    def send_all(phase):
        def step(turn, carry):
            for each in range(4):
                slab_copy(phase, lax.rem(me + 16 + 4 * turn + each, SLAB)).start()
            return carry

        lax.fori_loop(0, 4, step, 0)

        def near_step(turn, carry):
            for each in range(3):
                slab_copy(phase, lax.rem(me + 1 + 3 * turn + each, SLAB)).start()
            return carry

        lax.fori_loop(0, 5, near_step, 0)
        keep_own(phase)

    first_group = me // 4 + 4
    core = lax.rem(mine, 2)
    place = core * 4 + mine // 2

    spread = (
        lax.broadcasted_iota(jnp.int32, (128, CH), 0) // 8 == lax.broadcasted_iota(jnp.int32, (128, CH), 1)
    ).astype(F32)
    same_row = (
        lax.broadcasted_iota(jnp.int32, (128, 128), 0) % 8 == lax.broadcasted_iota(jnp.int32, (128, 128), 1) % 8
    )

    first_table.wait()

    def forward_step(c, carry):
        x_copy(c).wait()
        for x in range(XP):
            analyse_y(cat([xv[2 * c, x], xv[2 * c + 1, x]], 1), ty_stack, store, x * CH + 2 * c)
        return carry

    lax.fori_loop(0, CH // 2, forward_step, 0)
    pl.semaphore_wait(barrier, SLAB - 1 + DP - 1)
    analyse_z(store, tz_plain, sbuf, 0, first_group, send_one(0), send_group(0))

    pw_copy.wait()
    wide = jnp.dot(spread, pw[...], precision=lax.Precision.HIGHEST, preferred_element_type=F32)
    wide = lax.dot_general(
        wide, spread, (((1,), (1,)), ((), ())), precision=lax.Precision.HIGHEST, preferred_element_type=F32
    )
    wide = jnp.where(same_row, wide, 0.0)
    for kron, value in ((kron1, wide.T), (kron2, wide)):
        high, low = split(value)
        kron[...] = cat([cat([high, high], 1), cat([low, jnp.zeros_like(low)], 1)], 0)

    w_copy.wait()

    def regroup_step(c, carry):
        base = pl.multiple_of(c * 96, 16)
        for ri in range(2):
            for t in range(3):
                wco[pl.ds(base + 48 * ri + 16 * t, 16), :] = wv[c, :, ri, 128 * t : 128 * t + 128]
        return carry

    lax.fori_loop(0, CH, regroup_step, 0)
    second_table.wait()
    slab_all(0).wait_recv()
    modes = analyse_x(rbuf, 0, rows_high, rows_low)
    vv[:48, :] = modes[:, :128]
    vv[48:, :] = modes[:, 128:]

    def spread_row(modes, c):
        return cat([jnp.broadcast_to(modes[pl.ds(16 * t + c, 1), :], (16, 128)) for t in range(3)], 0), cat(
            [jnp.broadcast_to(modes[pl.ds(48 + 16 * t + c, 1), :], (16, 128)) for t in range(3)], 0
        )

    def mode_step(c, carry):
        base = c * 96
        wr, wi = wco[pl.ds(base, 48), :], wco[pl.ds(base + 48, 48), :]
        vr, vi = spread_row(vv, c)
        return carry[0] + (wr * vr - wi * vi), carry[1] + (wr * vi + wi * vr)

    no_modes = (jnp.zeros((48, 128), F32), jnp.zeros((48, 128), F32))
    mixed = cat(each_channel(mode_step, no_modes), 1)

    def put_mixed(k, value):
        sbuf[1, :, k, :] = value

    synthesise_x(mixed, columns_high, columns_low, put_mixed)
    send_all(1)

    def v_copy(d):
        return pltpu.make_async_remote_copy(
            src_ref=vsend.at[pl.ds(pl.multiple_of(16 * d, 16), 16)],
            dst_ref=vrecv.at[pl.ds(pl.multiple_of(16 * place, 16), 16)],
            send_sem=vssem,
            recv_sem=vrsem,
            device_id={"dp": d},
            device_id_type=MESH,
        )

    vsend[...] = jnp.zeros_like(vsend)
    for d in range(DP):
        for c in range(2):
            for t in range(3):
                row = 16 * t + 2 * d + c
                at = 16 * d + 6 * c + t
                vsend[at : at + 1, :] = vv[row : row + 1, :]
                vsend[at + 3 : at + 4, :] = vv[row + 48 : row + 49, :]

    def v_send(d, carry):
        v_copy(lax.rem(mine + d, DP)).start()
        return carry

    lax.fori_loop(1, DP, v_send, 0)
    vrecv[pl.ds(pl.multiple_of(16 * place, 16), 16), :] = vsend[pl.ds(pl.multiple_of(16 * mine, 16), 16), :]

    def turn_step(o, carry):
        base = pl.multiple_of(o * 96, 16)
        for part in range(6):
            woc[pl.ds(base + 16 * part, 16), :] = wco[pl.ds(16 * part + o, 16, stride=96), :]
        return carry

    lax.fori_loop(0, CH, turn_step, 0)

    def mix_step(yg, carry):
        y0 = pl.multiple_of(yg * 16, 16)
        for x in range(XP):
            high, low = split(rows_of(xv, x, y0))
            mix_channels(kron1, cat([high, low], 0), bv, x, y0)
        return carry

    lax.fori_loop(0, NY // 16, mix_step, 0)
    c_copy.wait()
    slab_all(1).wait_recv()

    synthesise_z(rbuf.at[1], zw_high, zw_low, held, store)

    def middle_step(o, carry):
        for x in range(XP):
            carried = synthesise_y(store, ty_inverse, x * CH + 2 * o)
            grads = []
            for each in range(2):
                before = carried[:, NZ * each : NZ * each + NZ] + bv[2 * o + each, x]
                slope = 0.5 * (1.0 + lax.erf(before * (1.0 / math.sqrt(2.0)))) + before * jnp.exp(
                    -0.5 * before * before
                ) * (1.0 / math.sqrt(2.0 * math.pi))
                grad = cv[2 * o + each, x] * slope
                cv[2 * o + each, x] = grad
                grads.append(grad)
            analyse_y(cat(grads, 1), ty_stack, store2, x * CH + 2 * o)
        return carry

    lax.fori_loop(0, CH // 2, middle_step, 0, unroll=4)
    analyse_z(store2, tz_weighted, sbuf, 2, first_group, send_one(2), send_group(2))

    pacc[...] = jnp.zeros_like(pacc)

    def pointwise_step(yg, carry):
        y0 = pl.multiple_of(yg * 16, 16)
        for x in range(XP):
            high, low = split(rows_of(cv, x, y0))
            xhigh, xlow = split(rows_of(xv, x, y0))
            pacc[...] += dot_t(cat([xhigh, xlow], 0), cat([high, low], 0))
        return carry

    lax.fori_loop(0, NY // 16, pointwise_step, 0)
    part = pacc[:128, :128] + pacc[:128, 128:] + pacc[128:, :128] + pacc[128:, 128:]
    part = jnp.where(same_row, part, 0.0)
    part = jnp.dot(part, spread, precision=lax.Precision.HIGHEST, preferred_element_type=F32)
    part = lax.dot_general(
        spread, part, (((0,), (0,)), ((), ())), precision=lax.Precision.HIGHEST, preferred_element_type=F32
    )
    flat = [cat([part[8 * r + i : 8 * r + i + 1, :] for i in range(8)], 1) for r in range(2)]
    part = cat(flat + [jnp.zeros((6, 128), F32)], 0)

    def p_copy(p):
        return pltpu.make_async_remote_copy(
            src_ref=psend,
            dst_ref=precv.at[pl.ds(pl.multiple_of(8 * me, 8), 8)],
            send_sem=pssem,
            recv_sem=prsem,
            device_id={"slab": p},
            device_id_type=MESH,
        )

    psend[...] = part

    def p_send(d, carry):
        p_copy(lax.rem(me + d, SLAB)).start()
        return carry

    lax.fori_loop(1, SLAB, p_send, 0)
    precv[pl.ds(pl.multiple_of(8 * me, 8), 8), :] = part

    slab_all(2).wait_recv()
    modes = analyse_x(rbuf, 2, rows_high, rows_low)
    gv[:48, :] = modes[:, :128]
    gv[48:, :] = modes[:, 128:]

    def g_copy(d):
        return pltpu.make_async_remote_copy(
            src_ref=gv,
            dst_ref=grecv.at[pl.ds(pl.multiple_of(96 * place, 16), 96)],
            send_sem=gssem,
            recv_sem=grsem,
            device_id={"dp": lax.rem(mine + 2 * d, DP)},
            device_id_type=MESH,
        )

    for d in range(1, 4):
        g_copy(d).start()
    grecv[pl.ds(pl.multiple_of(96 * place, 16), 96), :] = gv[...]

    def back_mode_step(o, carry):
        base = o * 96
        wr, wi = woc[pl.ds(base, 48), :], woc[pl.ds(base + 48, 48), :]
        gr, gi = spread_row(gv, o)
        return carry[0] + (wr * gr + wi * gi), carry[1] + (wr * gi - wi * gr)

    back = cat(each_channel(back_mode_step, no_modes), 1)

    def put_back(k, value):
        sbuf[3, :, k, :] = value

    def dp_all(source, target, size, send_sem, recv_sem):
        return pltpu.make_async_remote_copy(
            src_ref=source.at[pl.ds(0, size)],
            dst_ref=target.at[pl.ds(0, size)],
            send_sem=send_sem,
            recv_sem=recv_sem,
            device_id={"dp": lax.rem(mine + 1, DP)},
            device_id_type=MESH,
        )

    v_all = dp_all(vrecv, vrecv, 16 * (DP - 1), vssem, vrsem)
    g_all = dp_all(grecv, grecv, 96 * 3, gssem, grsem)
    synthesise_x(back, columns_high, columns_low, put_back)
    p_all = pltpu.make_async_remote_copy(
        src_ref=precv.at[pl.ds(0, 8 * (SLAB - 1))],
        dst_ref=precv.at[pl.ds(0, 8 * (SLAB - 1))],
        send_sem=pssem,
        recv_sem=prsem,
        device_id={"slab": lax.rem(me + 1, SLAB)},
        device_id_type=MESH,
    )
    p_all.wait_recv()
    total = precv[0:8, :]
    for p in range(1, SLAB):
        total = total + precv[8 * p : 8 * p + 8, :]
    qsend[...] = total

    def q_copy(d):
        return pltpu.make_async_remote_copy(
            src_ref=qsend,
            dst_ref=q_hbm.at[pl.ds(pl.multiple_of(8 * mine, 8), 8)],
            send_sem=qssem,
            recv_sem=qrsem,
            device_id={"dp": d},
            device_id_type=MESH,
        )

    def q_send(d, carry):
        q_copy(lax.rem(mine + d, DP)).start()
        return carry

    lax.fori_loop(1, DP, q_send, 0)
    q_own = pltpu.make_async_copy(qsend, q_hbm.at[pl.ds(pl.multiple_of(8 * mine, 8), 8)], qownsem)
    q_own.start()
    q_all = dp_all(q_hbm, q_hbm, 8 * (DP - 1), qssem, qrsem)
    send_all(3)

    v_all.wait_recv()
    g_all.wait_recv()
    half = pl.ds(pl.multiple_of(core * 384, 16), 384)
    h_copy = pltpu.make_async_remote_copy(
        src_ref=grecv.at[half],
        dst_ref=grecv.at[half],
        send_sem=hssem,
        recv_sem=hrsem,
        device_id={"dp": mine + 1 - 2 * core},
        device_id_type=MESH,
    )
    h_copy.start()

    def back_step(yg, carry):
        y0 = pl.multiple_of(yg * 16, 16)
        for x in range(XP):
            high, low = split(rows_of(cv, x, y0))
            mix_channels(kron2, cat([high, low], 0), bv, x, y0)
        return carry

    lax.fori_loop(0, NY // 16, back_step, 0)
    o_copy = pltpu.make_async_copy(bv, mixed_hbm, osem)
    o_copy.start()
    h_copy.wait()

    for c in range(2):
        def sample_step(d, carry):
            out = []
            base = pl.multiple_of(96 * d, 16)
            for t in range(3):
                vr = vrecv[pl.ds(16 * d + 6 * c + t, 1), :]
                vi = vrecv[pl.ds(16 * d + 6 * c + 3 + t, 1), :]
                gr = grecv[pl.ds(base + 16 * t, 16), :]
                gi = grecv[pl.ds(base + 48 + 16 * t, 16), :]
                out.append(carry[2 * t] + (gr * vr + gi * vi))
                out.append(carry[2 * t + 1] + (gi * vr - gr * vi))
            return tuple(out)

        total = lax.fori_loop(0, DP, sample_step, tuple(jnp.zeros((CH, 128), F32) for _ in range(6)))
        for t in range(3):
            gs_ref[c, :, 0, 128 * t : 128 * t + 128] = total[2 * t]
            gs_ref[c, :, 1, 128 * t : 128 * t + 128] = total[2 * t + 1]

    gs_copy = pltpu.make_async_copy(gs_ref, gs_hbm, gsem)
    gs_copy.start()
    for phase in range(4):
        slab_all(phase).wait_send()
    p_all.wait_send()
    q_all.wait_send()
    v_all.wait_send()
    g_all.wait_send()
    o_copy.wait()
    own_copy.wait()
    q_own.wait()
    gs_copy.wait()
    slab_all(3).wait_recv()
    q_all.wait_recv()


def last_kernel(
    rows_hbm, mixed_hbm, gs_in, q_hbm, table_hbm, gi_hbm, gs_hbm, gp_hbm,
    rows_ref, gs_ref, q_ref, bv, table, held, store, gp, insem, tsem, osem, gssem, gpsem, rsem, qsem,
):
    rows_copy = pltpu.make_async_copy(rows_hbm, rows_ref, rsem)
    rows_copy.start()
    table_copy = pltpu.make_async_copy(table_hbm, table, tsem)
    table_copy.start()

    def in_copy(c):
        return pltpu.make_async_copy(mixed_hbm.at[pl.ds(2 * c, 2)], bv.at[pl.ds(2 * c, 2)], insem.at[c])

    def out_copy(c):
        return pltpu.make_async_copy(bv.at[pl.ds(2 * c, 2)], gi_hbm.at[pl.ds(2 * c, 2)], osem.at[c])

    for c in range(CH // 2):
        in_copy(c).start()
    gs_load = pltpu.make_async_copy(gs_in, gs_ref, gssem)
    gs_load.start()
    q_copy = pltpu.make_async_copy(q_hbm, q_ref, qsem)
    q_copy.start()
    rows_copy.wait()
    table_copy.wait()
    ty_inverse = table.at[pl.ds(0, 128)]
    synthesise_z(rows_ref, table.at[pl.ds(128, 480)], table.at[pl.ds(608, 480)], held, store)

    def last_step(c, carry):
        in_copy(c).wait()
        for x in range(XP):
            out = synthesise_y(store, ty_inverse, x * CH + 2 * c)
            bv[2 * c, x] = bv[2 * c, x] + out[:, :NZ]
            bv[2 * c + 1, x] = bv[2 * c + 1, x] + out[:, NZ:]
        out_copy(c).start()
        return carry

    q_copy.wait()
    total = q_ref[0:8, :]
    for d in range(1, DP):
        total = total + q_ref[8 * d : 8 * d + 8, :]
    total = total * (1.0 / math.sqrt(DP * NX * NY * NZ))
    for r in range(2):
        for i in range(8):
            gp[8 * r + i : 8 * r + i + 1, :] = total[r : r + 1, CH * i : CH * i + CH]
    gp_copy = pltpu.make_async_copy(gp, gp_hbm, gpsem)
    gp_copy.start()
    gs_load.wait()
    gs_copy = pltpu.make_async_copy(gs_ref, gs_hbm, gssem)
    gs_copy.start()
    lax.fori_loop(0, CH // 2, last_step, 0)
    gs_copy.wait()
    gp_copy.wait()
    for c in range(CH // 2):
        out_copy(c).wait()


def body(inputs, cotangent, spectral_weights, pointwise_weights):
    main_table, last_table = (jnp.asarray(table) for table in tables())
    hbm = pl.BlockSpec(memory_space=pltpu.HBM)
    block = (CH, XP, NY, NZ)
    dma = pltpu.SemaphoreType.DMA
    block_shape = jax.ShapeDtypeStruct(block, F32)
    weight_shape = jax.ShapeDtypeStruct((2, CH, 2, KX * KZ), F32)
    store_shape = pltpu.VMEM((CH * XP * PITCH, NZ), F32)
    rows, mixed, weight_part, point_part = pl.pallas_call(
        kernel,
        out_shape=[
            jax.ShapeDtypeStruct((SLAB, KZ, 128), F32),
            block_shape,
            weight_shape,
            jax.ShapeDtypeStruct((8 * DP, 128), F32),
        ],
        in_specs=[hbm] * 5,
        out_specs=[hbm] * 4,
        scratch_shapes=[
            pltpu.VMEM(block, F32),
            pltpu.VMEM(block, F32),
            pltpu.VMEM(block, F32),
            pltpu.VMEM((CH, CH, 2, KX * KZ), F32),
            pltpu.VMEM((CH * 96, 128), F32),
            pltpu.VMEM((CH * 96, 128), F32),
            pltpu.VMEM((CH, CH), F32),
            pltpu.VMEM((TABLE, 256), BF16),
            store_shape,
            store_shape,
            pltpu.VMEM((512, 256), BF16),
            pltpu.VMEM((4, SLAB, KZ, 128), F32),
            pltpu.VMEM((3, SLAB, KZ, 128), F32),
            pltpu.VMEM((96, 128), F32),
            pltpu.VMEM((96, 128), F32),
            pltpu.VMEM((256, 256), BF16),
            pltpu.VMEM((256, 256), BF16),
            pltpu.VMEM((256, 256), F32),
            pltpu.VMEM((16 * DP, 128), F32),
            pltpu.VMEM((16 * DP, 128), F32),
            pltpu.VMEM((96 * DP, 128), F32),
            pltpu.VMEM((8, 128), F32),
            pltpu.VMEM((8 * SLAB, 128), F32),
            pltpu.VMEM((8, 128), F32),
            pltpu.VMEM((2, CH, 2, KX * KZ), F32),
            dma((CH // 2,)),
            dma,
            dma,
            dma,
            dma((2,)),
            dma,
            dma((4,)),
            dma((4,)),
            dma,
            dma,
            dma,
            dma,
            dma,
            dma,
            dma,
            dma,
            dma,
            dma,
            dma,
            dma,
            dma,
        ],
        compiler_params=pltpu.CompilerParams(
            collective_id=0, has_side_effects=True, vmem_limit_bytes=60 * 1024 * 1024
        ),
        name="layer_backward",
    )(inputs.reshape(block), cotangent.reshape(block), spectral_weights, pointwise_weights, main_table)
    grad_inputs, grad_spectral, grad_pointwise = pl.pallas_call(
        last_kernel,
        out_shape=[block_shape, weight_shape, jax.ShapeDtypeStruct((CH, CH), F32)],
        in_specs=[hbm] * 5,
        out_specs=[hbm, hbm, hbm],
        scratch_shapes=[
            pltpu.VMEM((SLAB, KZ, 128), F32),
            pltpu.VMEM((2, CH, 2, KX * KZ), F32),
            pltpu.VMEM((8 * DP, 128), F32),
            pltpu.VMEM(block, F32),
            pltpu.VMEM((LAST_TABLE, 256), BF16),
            pltpu.VMEM((512, 256), BF16),
            store_shape,
            pltpu.VMEM((CH, CH), F32),
            dma((CH // 2,)),
            dma,
            dma((CH // 2,)),
            dma,
            dma,
            dma,
            dma,
        ],
        compiler_params=pltpu.CompilerParams(vmem_limit_bytes=60 * 1024 * 1024),
        name="input_gradient",
    )(rows, mixed, weight_part, point_part, last_table)
    return (grad_inputs[None], grad_spectral, grad_pointwise)


def solution(mesh):
    placed = (
        P("dp", None, "slab", None, None),
        P("dp", None, "slab", None, None),
        P(None, None, None, "slab"),
        P(),
    )
    return jax.shard_map(
        body,
        mesh=mesh,
        in_specs=placed,
        out_specs=(P("dp", None, "slab", None, None), P("dp", None, None, "slab"), P()),
        check_vma=False,
    )
```
